512 devices in a mesh: gx: 64 (over x, y, core), gy: 4 (over z_hi), gz: 2 (over z_lo).
Axes of the slice: x: 4, y: 8, z: 8 (z_hi: 4, z_lo: 2; z = z_hi * 2 + z_lo), core: 2. Of those that a mesh axis runs over, the one named last changes fastest.
Arguments:
- right_side: float32 [2560, 160, 256], P('gx', 'gy', 'gz'), may hold values from -6 to 6
- guess_field: float32 [2560, 160, 256], P('gx', 'gy', 'gz'), may hold values from -0.6 to 0.6
- conduct_field: float32 [2560, 160, 256], P('gx', 'gy', 'gz'), may hold values from 1 to 10
Outputs:
- solution_field: float32 [2560, 160, 256], P('gx', 'gy', 'gz')
- residual: float32 [2560, 160, 256], P('gx', 'gy', 'gz')
The draws below stay inside these ranges and needn't reach their ends.
All inputs are finite; a program needn't handle non-finite values.
Results may differ from the reference program's by a relative error of at most 0.0055.
Values sent between devices are 32-bit elements; how exact they have to be, the bound alone decides.
No kernel may reach another device: no remote copies, remote signals or barrier semaphores. Data moves between devices by JAX's collectives and lax.ppermute only.
A program may use at most 64 MiB of HBM per device.

```python
import jax
import jax.numpy as jnp
from jax import lax

C = 40
CZ = 128
OVER = 8
ITERS = 1
NX = 2560
NY = 160
NZ = 256
N_GX = 64
N_GY = 4
N_GZ = 2


def draw_right_side(key, part):
    key = jax.random.fold_in(key, 11)
    return jnp.clip(jax.random.normal(key, (NX, NY, NZ), jnp.float32), -6.0, 6.0)


def draw_conduct_field(key, part):
    key = jax.random.fold_in(key, 23)
    return jnp.exp(jax.random.uniform(key, (NX, NY, NZ), jnp.float32, 0.0, jnp.log(10.0)))


def shard_levels(key, shape, cuts, least, high):
    def one(axis_at, blocks):
        draws = jax.random.uniform(jax.random.fold_in(jax.random.fold_in(key, 6), axis_at), (blocks,), jnp.float32, least / len(cuts), high / len(cuts))
        return jnp.repeat(jnp.exp(draws), shape[axis_at] // blocks).reshape((-1,) + (1,) * (len(shape) - axis_at - 1))

    level = one(*cuts[0])
    for cut in cuts[1:]:
        level = level * one(*cut)
    return level


def noise(rng, shape, scale, bound, cuts=(), kind=jnp.bfloat16):
    level = shard_levels(rng, shape, cuts, -0.22, 0.18) if cuts else 1.0
    array = jax.random.normal(rng, shape, jnp.float32) * scale * level
    return jnp.minimum(jnp.maximum(array, -bound), bound).astype(kind)


def setup_inputs(seed: int = 0) -> dict:
    arg_keys = jax.random.split(jax.random.key(seed), 4)
    return {
        "right_side": draw_right_side(jax.random.fold_in(arg_keys[3], 71), 0),
        "guess_field": noise(arg_keys[1], (NX, NY, NZ), 0.1, 0.6, ((0, 64), (1, 4), (2, 2)), jnp.float32),
        "conduct_field": draw_conduct_field(jax.random.fold_in(arg_keys[3], 71), 0),
    }


stiff_scale = 3.0
mass_term = 0.001

def sine_table(count):
    steps_range = jnp.arange(1, count + 1).astype(jnp.float32)
    angles = jnp.pi * steps_range[:, None] * steps_range[None, :] / (count + 1)
    basis = jnp.sqrt(2.0 / (count + 1)) * jnp.sin(angles)
    eigen = 2.0 - 2.0 * jnp.cos(jnp.pi * steps_range / (count + 1))
    return (basis, eigen)

def transform(values, basis_a, basis_b, basis_c):
    values = jnp.einsum('abc,cz->abz', values, basis_c, precision=lax.Precision.HIGHEST)
    values = jnp.einsum('abz,by->ayz', values, basis_b, precision=lax.Precision.HIGHEST)
    return jnp.einsum('ayz,ax->xyz', values, basis_a, precision=lax.Precision.HIGHEST)

def solve_box(extended):
    basis_a, eigen_a = sine_table(extended.shape[0])
    basis_b, eigen_b = sine_table(extended.shape[1])
    basis_c, eigen_c = sine_table(extended.shape[2])
    spectral = transform(extended, basis_a, basis_b, basis_c)
    denom = stiff_scale * (eigen_a[:, None, None] + eigen_b[None, :, None] + eigen_c[None, None, :]) + mass_term
    return transform(spectral / denom, basis_a, basis_b, basis_c)

def face_terms(padded_h):
    face_x = 0.5 * (padded_h[1:, 1:-1, 1:-1] + padded_h[:-1, 1:-1, 1:-1])
    face_y = 0.5 * (padded_h[1:-1, 1:, 1:-1] + padded_h[1:-1, :-1, 1:-1])
    face_z = 0.5 * (padded_h[1:-1, 1:-1, 1:] + padded_h[1:-1, 1:-1, :-1])
    return (face_x, face_y, face_z)

def apply_padded(padded, faces):
    face_x, face_y, face_z = faces
    field = padded[1:-1, 1:-1, 1:-1]
    flux_x = face_x * (padded[1:, 1:-1, 1:-1] - padded[:-1, 1:-1, 1:-1])
    flux_y = face_y * (padded[1:-1, 1:, 1:-1] - padded[1:-1, :-1, 1:-1])
    flux_z = face_z * (padded[1:-1, 1:-1, 1:] - padded[1:-1, 1:-1, :-1])
    return mass_term * field - (flux_x[1:] - flux_x[:-1]) - (flux_y[:, 1:] - flux_y[:, :-1]) - (flux_z[:, :, 1:] - flux_z[:, :, :-1])

def precondition(resid):
    padded = jnp.pad(resid, OVER)
    total = jnp.zeros_like(padded)
    extent = (C + 2 * OVER, C + 2 * OVER, CZ + 2 * OVER)

    def visit(number, total):
        number = jnp.asarray(number).astype(jnp.int32)
        first = number // (N_GY * N_GZ)
        second = number // N_GZ % N_GY
        third = number % N_GZ
        start = ((first * C).astype(jnp.int32), (second * C).astype(jnp.int32), (third * CZ).astype(jnp.int32))
        extended = lax.dynamic_slice(padded, start, extent)
        local_sol = solve_box(extended)
        current = lax.dynamic_slice(total, start, extent)
        return lax.dynamic_update_slice(total, current + local_sol, start)
    total = lax.fori_loop(0, N_GX * N_GY * N_GZ, visit, total)
    return total[OVER:-OVER, OVER:-OVER, OVER:-OVER]

def reference(right_side, guess_field, conduct_field):
    faces = face_terms(jnp.pad(conduct_field, 1))
    resid = right_side - apply_padded(jnp.pad(guess_field, 1), faces)
    solution = guess_field
    precond = precondition(resid)
    product_now = jnp.sum(resid * precond)
    direction = precond
    for iteration in range(ITERS):
        applied = apply_padded(jnp.pad(direction, 1), faces)
        step_size = product_now / jnp.sum(direction * applied)
        solution = solution + step_size * direction
        resid = resid - step_size * applied
        if iteration + 1 < ITERS:
            precond = precondition(resid)
            product_next = jnp.sum(resid * precond)
            direction = precond + product_next / product_now * direction
            product_now = product_next
    return (solution, resid)
```

```python
import functools

import jax
import jax.numpy as jnp
import ml_dtypes
import numpy as np
from jax import lax
from jax.experimental import pallas as pl
from jax.experimental.pallas import tpu as pltpu
from jax.sharding import Mesh
from jax.sharding import PartitionSpec as P

OVER = 8
C = 40
CZ = 128
EXT = C + 2 * OVER
EXTZ = CZ + 2 * OVER
TILES = EXT // 8
GROUPS = EXT * TILES
stiff_scale = 3.0
mass_term = 0.001

F32 = jnp.float32
BF16 = jnp.bfloat16
VMEM = pl.BlockSpec(memory_space=pltpu.VMEM)
SMEM = pl.BlockSpec(memory_space=pltpu.SMEM)

YROWS = 440
XROWS = 568
PER_Z = 12
ZROWS = 8 * -(-GROUPS // PER_Z)
PER = 14
XROWS2 = 9 * EXT + 40
YROWS2 = 416
ZGROUPS2 = 42 * 5 + 12
ZROWS2 = 8 * -(-ZGROUPS2 // PER)


def sine_table(count):
    k = np.arange(1, count + 1)
    basis = np.sqrt(2.0 / (count + 1)) * np.sin(np.pi * k[:, None] * k[None, :] / (count + 1))
    eigen = 2.0 - 2.0 * np.cos(np.pi * k / (count + 1))
    return basis, eigen


def two_parts(table):
    high = table.astype(ml_dtypes.bfloat16)
    low = (table - high.astype(np.float64)).astype(ml_dtypes.bfloat16)
    return high, low


@functools.cache
def tables():
    basis, eigen = sine_table(EXT)
    basis_z, eigen_z = sine_table(EXTZ)
    high, low = two_parts(basis)
    plane = np.zeros((EXT, 192), ml_dtypes.bfloat16)
    plane[:, 0:EXT] = high
    plane[:, 64 : 64 + EXT] = low
    plane[:, 128 : 128 + EXT] = high
    forward = np.zeros((2, 256, 256))
    inverse = np.zeros((2, 256, 256))
    for gz in range(2):
        own = basis_z[8 : 8 + CZ]
        strip = basis_z[136:144] if gz == 0 else basis_z[0:8]
        face_own, face_far = (135, 136) if gz == 0 else (8, 7)
        forward[gz, :CZ, :EXTZ] = own
        forward[gz, CZ, :EXTZ] = basis_z[face_own] - basis_z[face_far]
        forward[gz, CZ + 2 : CZ + 10, :EXTZ] = strip
        inverse[gz, :EXTZ, :CZ] = own.T
        inverse[gz, :EXTZ, CZ : CZ + 9] = (basis_z[135:144] if gz == 0 else basis_z[0:9]).T
    forward = np.stack(two_parts(forward), 1)
    inverse = np.stack(two_parts(inverse), 1)
    denom = np.full((EXT, 256), 1.0)
    denom[:, :EXTZ] = stiff_scale * (eigen[:, None] + eigen_z[None, :]) + mass_term
    return (
        plane,
        forward,
        inverse,
        denom.astype(np.float32),
        (stiff_scale * eigen).astype(np.float32),
    )


def roll(value, shift, axis):
    if isinstance(shift, int):
        shift = shift % value.shape[axis]
        return value if shift == 0 else pltpu.roll(value, shift, axis)
    return pltpu.roll(value, lax.rem(shift + 2 * value.shape[axis], value.shape[axis]), axis)


def lanes(rows):
    return lax.broadcasted_iota(jnp.int32, (rows, CZ), 1)


def rows_at(start, size):
    return pl.ds(pl.multiple_of(start, 8), size)


def tile_at(index):
    return rows_at(index * 8, 8)


def call(body, out_rows, *args, scratch=(), limit=16, name=None, smem=(), flops=0):
    return pl.pallas_call(
        body,
        out_shape=[jax.ShapeDtypeStruct((rows, CZ), F32) for rows in out_rows],
        in_specs=[SMEM if i in smem else VMEM for i in range(len(args))],
        out_specs=[VMEM] * len(out_rows),
        scratch_shapes=list(scratch),
        compiler_params=pltpu.CompilerParams(vmem_limit_bytes=limit * 2**20),
        name=name,
    )(*args)


def strip_base():
    return jnp.where(lax.axis_index("gz") == 0, 118, 126)


def face_lane():
    return jnp.where(lax.axis_index("gz") == 0, 127, 0)


def residual_kernel(v, h, b, part, vh, up, down, edge):
    gz = lax.axis_index("gz")
    base, face = strip_base(), face_lane()
    lane = lanes(C)
    row = lax.broadcasted_iota(jnp.int32, (C, CZ), 0)
    y_half = jnp.where(row > 0, 0.5, 0.0)
    z_half = jnp.where(lane < CZ - 1, 0.5, 0.0)
    outer = jnp.where(lane == jnp.where(gz == 0, 0, 127), 0.5, 0.0)
    v_lane, h_lane = lane == base, lane == base + 1

    def visit(x, carry):
        flux_x, pack_up, pack_down = carry
        own = rows_at(x * C, C)
        following = rows_at(jnp.minimum(x + 1, C - 1) * C, C)
        vi, hi = v[own, :], h[own, :]
        next_x = 0.5 * (hi + h[following, :]) * (v[following, :] - vi)
        flux_y = y_half * (hi + roll(hi, 1, 0)) * (vi - roll(vi, 1, 0))
        flux_z = z_half * (hi + roll(hi, -1, 1)) * (roll(vi, -1, 1) - vi)
        applied = (
            mass_term * vi
            - (next_x - flux_x)
            - (roll(flux_y, -1, 0) - flux_y)
            - (flux_z - roll(flux_z, 1, 1))
            + outer * hi * vi
        )
        resid = b[own, :] - applied
        part[own, :] = resid
        down[tile_at(x), :] = resid[0:8]
        up[tile_at(x), :] = resid[32:40]
        pair = jnp.where(v_lane, roll(vi, base - face, 1), 0.0) + jnp.where(
            h_lane, roll(hi, base + 1 - face, 1), 0.0
        )
        vh[own, :] = pair
        shift = 2 * x - base
        return (
            next_x,
            pack_up + roll(pair[32:40], shift, 1),
            pack_down + roll(pair[0:8], shift, 1),
        )

    zero = jnp.zeros((C, CZ), F32)
    zero8 = jnp.zeros((8, CZ), F32)
    _, pack_up, pack_down = lax.fori_loop(0, C, visit, (zero, zero8, zero8), unroll=4)
    up[432:440, :] = pack_up
    down[432:440, :] = pack_down
    last = (C - 1) * C
    for message, first in ((up, 32), (down, 0)):
        face_row = C - 1 if first else 0
        message[320:360, :] = v[pl.ds(face_row, C, stride=C), :]
        message[360:400, :] = h[pl.ds(face_row, C, stride=C), :]
        message[400:408, :] = v[first : first + 8, :]
        message[408:416, :] = h[first : first + 8, :]
        message[416:424, :] = v[last + first : last + first + 8, :]
        message[424:432, :] = h[last + first : last + first + 8, :]
    edge[0:40, :] = v[0:40, :]
    edge[40:80, :] = h[0:40, :]
    edge[80:120, :] = v[last : last + 40, :]
    edge[120:160, :] = h[last : last + 40, :]


def pack_pairs(vh, first):
    base = strip_base()

    def visit(i, acc):
        for t in range(TILES):
            j = i * TILES + t
            acc = acc + roll(vh[tile_at(first + j), :], 2 * j - base, 1)
        return acc

    return lax.fori_loop(0, OVER, visit, jnp.zeros((8, CZ), F32), unroll=2)


def extend_y_kernel(flags, part, vh, up, down, edge, low, high, out, vh_out, right, left):
    base = strip_base()
    lane = lanes(8)
    pair_lanes = (lane == base) | (lane == base + 1)

    def visit(x, _):
        out[rows_at(x * EXT, 8), :] = low[tile_at(x), :]
        out[rows_at(x * EXT + 8, C), :] = part[rows_at(x * C, C), :]
        out[rows_at(x * EXT + 48, 8), :] = high[tile_at(x), :]
        vh_out[rows_at(x * EXT, 8), :] = jnp.where(
            pair_lanes, roll(low[432:440, :], base - 2 * x, 1), 0.0
        )
        vh_out[rows_at(x * EXT + 8, C), :] = vh[rows_at(x * C, C), :]
        vh_out[rows_at(x * EXT + 48, 8), :] = jnp.where(
            pair_lanes, roll(high[432:440, :], base - 2 * x, 1), 0.0
        )
        return 0

    lax.fori_loop(0, C, visit, 0, unroll=4)
    flux = 0.5 * (low[360:400, :] + down[360:400, :]) * (down[320:360, :] - low[320:360, :])
    out[pl.ds(8, C, stride=EXT), :] = out[pl.ds(8, C, stride=EXT), :] - flux
    out[pl.ds(7, C, stride=EXT), :] = out[pl.ds(7, C, stride=EXT), :] + flux * flags[2]
    flux = 0.5 * (up[360:400, :] + high[360:400, :]) * (high[320:360, :] - up[320:360, :])
    out[pl.ds(47, C, stride=EXT), :] = out[pl.ds(47, C, stride=EXT), :] + flux
    out[pl.ds(48, C, stride=EXT), :] = out[pl.ds(48, C, stride=EXT), :] - flux * flags[3]
    for message, first, strip, own in ((left, 0, 400, 0), (right, 32, 416, 80)):
        message[0:448, :] = out[first * EXT : first * EXT + 448, :]
        for k in range(2):
            at = 448 + k * EXT
            message[at : at + 8, :] = low[strip + 8 * k : strip + 8 * k + 8, :]
            message[at + 8 : at + 48, :] = edge[own + 40 * k : own + 40 * k + 40, :]
            message[at + 48 : at + 56, :] = high[strip + 8 * k : strip + 8 * k + 8, :]
        message[560:568, :] = pack_pairs(vh_out, first * TILES)


def extend_x_kernel(flags, part, vh, right, left, before, after, out, message, vh_all):
    base = strip_base()
    gz = lax.axis_index("gz")
    lane = lanes(8)
    pair_lanes = (lane == base) | (lane == base + 1)
    strip_lanes = jnp.where(gz == 0, lane - 120, 7 - lane) >= 0
    side = OVER * EXT
    out[0:side, :] = before[0:side, :]
    out[side : side + C * EXT, :] = part[...]
    out[side + C * EXT : EXT * EXT, :] = after[0:side, :]
    vh_all[side : side + C * EXT, :] = vh[...]

    def visit(j, _):
        vh_all[tile_at(j), :] = jnp.where(
            pair_lanes, roll(before[560:568, :], base - 2 * j, 1), 0.0
        )
        vh_all[tile_at(j + (OVER + C) * TILES), :] = jnp.where(
            pair_lanes, roll(after[560:568, :], base - 2 * j, 1), 0.0
        )
        return 0

    lax.fori_loop(0, OVER * TILES, visit, 0, unroll=8)
    flux = 0.5 * (before[504:560, :] + left[504:560, :]) * (left[448:504, :] - before[448:504, :])
    at = OVER * EXT
    out[at : at + EXT, :] = out[at : at + EXT, :] - flux
    out[at - EXT : at, :] = out[at - EXT : at, :] + flux * flags[0]
    flux = 0.5 * (right[504:560, :] + after[504:560, :]) * (after[448:504, :] - right[448:504, :])
    at = (OVER + C) * EXT
    out[at - EXT : at, :] = out[at - EXT : at, :] + flux
    out[at : at + EXT, :] = out[at : at + EXT, :] - flux * flags[1]

    def pack(q, count):
        acc = jnp.zeros((8, CZ), F32)
        for j in range(count):
            at = tile_at(q * PER_Z + j)
            both = jnp.where(strip_lanes, out[at, :], vh_all[at, :])
            acc = acc + roll(both, 10 * j - base, 1)
        message[tile_at(q), :] = acc

    def visit_pack(q, _):
        pack(q, PER_Z)
        return 0

    whole = GROUPS // PER_Z
    lax.fori_loop(0, whole, visit_pack, 0, unroll=2)
    pack(whole, GROUPS - whole * PER_Z)


def halves(value):
    high = value.astype(BF16)
    return high, (value - high.astype(F32)).astype(BF16)


def dot(a, b):
    return jnp.dot(a, b, preferred_element_type=F32)


def along_lanes(value, table_high, table_low):
    high, low = halves(value)
    return dot(high, table_high) + (dot(low, table_high) + dot(high, table_low))


def along_rows(table, value):
    padded = jnp.concatenate([value, jnp.zeros((8, value.shape[1]), F32)], axis=0)
    high, low = halves(padded)
    return dot(table, jnp.concatenate([high, high, low], axis=0))


PLANES = 8


def solve_kernel(
    eigen,
    ext,
    own_z,
    far_z,
    plane,
    forward,
    inverse,
    denom,
    resid,
    coef,
    sol,
    strip,
    right,
    left,
    halo_pack,
    coef_pack,
    halo,
    first_a,
    first_b,
    second_a,
    second_b,
):
    gz = lax.axis_index("gz")
    face = face_lane()
    lane = lanes(ZROWS)
    at_face = lax.rem(lane, 10) == 0
    both = own_z[...] + far_z[...]
    half = 0.5 * roll(both, -1, 1)
    halo_pack[...] = jnp.where(at_face, half * (far_z[...] - own_z[...]), far_z[...])
    coef_pack[...] = half
    lane8 = lanes(8)
    face_only = lane8 == face

    def unpack(q, count):
        packed = halo_pack[tile_at(q), :]
        for j in range(count):
            halo[tile_at(q * PER_Z + j), :] = roll(packed, -10 * j, 1)

    def visit_unpack(q, _):
        unpack(q, PER_Z)
        return 0

    whole = GROUPS // PER_Z
    lax.fori_loop(0, whole, visit_unpack, 0, unroll=2)
    unpack(whole, GROUPS - whole * PER_Z)

    def visit_own(x, _):
        for t in range(5):
            g = (x + OVER) * TILES + 1 + t
            q = g // PER_Z
            to = rows_at(x * C + 8 * t, 8)
            flux = roll(halo[tile_at(g), :], face, 1)
            resid[to, :] = ext[tile_at(g), :] + jnp.where(face_only, flux, 0.0)
            shift = face - 10 * (g - q * PER_Z)
            coef[to, :] = jnp.where(face_only, roll(coef_pack[tile_at(q), :], shift, 1), 0.0)
        return 0

    lax.fori_loop(0, C, visit_own, 0, unroll=2)

    table = plane[...]
    forward_high, forward_low = forward[gz, 0], forward[gz, 1]
    inverse_high, inverse_low = inverse[gz, 0], inverse[gz, 1]

    def visit_forward(c, _):
        at = rows_at(c * PLANES * EXT, PLANES * EXT)
        value = jnp.concatenate([ext[at, :], halo[at, :]], axis=1)
        value = along_lanes(value, forward_high, forward_low)
        for i in range(PLANES):
            part = along_rows(table, value[i * EXT : (i + 1) * EXT])
            to = rows_at((c * PLANES + i) * EXT, EXT)
            first_a[to, :] = part[:, :CZ]
            first_b[to, :] = part[:, CZ:]
        return 0

    lax.fori_loop(0, EXT // PLANES, visit_forward, 0)

    def visit_middle(c, _):
        for i in range(4):
            y = c * 4 + i
            at = pl.ds(y, EXT, stride=EXT)
            value = jnp.concatenate([first_a[at, :], first_b[at, :]], axis=1)
            value = along_rows(table, value) / (denom[...] + eigen[y])
            value = along_rows(table, value)
            second_a[at, :] = value[:, :CZ]
            second_b[at, :] = value[:, CZ:]
        return 0

    lax.fori_loop(0, EXT // 4, visit_middle, 0)

    def visit_inverse(c, _):
        parts = []
        for i in range(PLANES):
            at = rows_at((c * PLANES + i) * EXT, EXT)
            value = jnp.concatenate([second_a[at, :], second_b[at, :]], axis=1)
            parts.append(along_rows(table, value))
        value = along_lanes(jnp.concatenate(parts, axis=0), inverse_high, inverse_low)
        to = rows_at(c * PLANES * EXT, PLANES * EXT)
        sol[to, :] = value[:, :CZ]
        strip[to, :] = value[:, CZ:]
        return 0

    lax.fori_loop(0, EXT // PLANES, visit_inverse, 0)

    for message, start in ((left, 0), (right, 47)):
        message[0 : 9 * EXT, :] = sol[start * EXT : (start + 9) * EXT, :]
        pack_tiles(message, 9 * EXT, [strip[pl.ds((start * TILES + j) * 8, 8), :] for j in range(63)])


def pack_tiles(message, at, values):
    for q in range(-(-len(values) // PER)):
        acc = values[q * PER]
        for j, value in enumerate(values[q * PER + 1 : (q + 1) * PER], 1):
            acc = acc + roll(value, 9 * j, 1)
        message[at + 8 * q : at + 8 * q + 8, :] = acc


def unpack_tile(message, at, index):
    q = index // PER
    return roll(message[rows_at(at + 8 * q, 8), :], -9 * (index - q * PER), 1)


def fold_x_kernel(flags, sol, strip, before, after, out, out_strip, up, down, line):
    first = 7 * EXT
    size = 42 * EXT
    narrow = lanes(8) < 9
    out[...] = sol[first : first + size, :]
    out_strip[...] = strip[first : first + size, :]
    out[0 : 9 * EXT, :] = out[0 : 9 * EXT, :] + before[0 : 9 * EXT, :]
    tail = 33 * EXT
    out[tail:size, :] = out[tail:size, :] + after[0 : 9 * EXT, :]

    for j in range(63):
        for message, at in ((before, 8 * j), (after, tail + 8 * j)):
            value = jnp.where(narrow, unpack_tile(message, 9 * EXT, j), 0.0)
            out_strip[at : at + 8, :] = out_strip[at : at + 8, :] + value

    for array in (out, out_strip):
        array[0:EXT, :] = array[0:EXT, :] * flags[0]
        array[41 * EXT : size, :] = array[41 * EXT : size, :] * flags[1]

    for message, tile, single in ((up, 6, 47), (down, 0, 8)):
        for p in range(42):
            message[8 * p : 8 * p + 8, :] = out[p * EXT + 8 * tile : p * EXT + 8 * tile + 8, :]
        message[376:384, :] = jnp.zeros((8, CZ), F32)
        message[336:378, :] = out[pl.ds(single, 42, stride=EXT), :]
        line[40:48, :] = jnp.zeros((8, CZ), F32)
        line[0:42, :] = out_strip[pl.ds(single, 42, stride=EXT), :]
        values = [out_strip[p * EXT + 8 * tile : p * EXT + 8 * tile + 8, :] for p in range(42)]
        values += [line[8 * j : 8 * j + 8, :] for j in range(6)]
        pack_tiles(message, 384, values)


def fold_y_kernel(flags, sol, strip, low, high, out, message, work, line):
    narrow = lanes(8) < 9
    out[...] = sol[...]
    work[...] = strip[...]
    for source, tile, single, flag in ((low, 1, 7, 2), (high, 5, 48, 3)):
        for p in range(42):
            at = p * EXT + 8 * tile
            out[at : at + 8, :] = out[at : at + 8, :] + source[8 * p : 8 * p + 8, :]
            value = jnp.where(narrow, unpack_tile(source, 384, p), 0.0)
            work[at : at + 8, :] = work[at : at + 8, :] + value
        at = pl.ds(single, 42, stride=EXT)
        out[at, :] = (out[at, :] + source[336:378, :]) * flags[flag]
        for j in range(6):
            line[8 * j : 8 * j + 8, :] = jnp.where(narrow, unpack_tile(source, 384, 42 + j), 0.0)
        work[at, :] = (work[at, :] + line[0:42, :]) * flags[flag]
    values = []
    for p in range(42):
        for t in range(1, 6):
            at = p * EXT + 8 * t
            values.append(work[at : at + 8, :])
    for k, single in enumerate((7, 48)):
        line[48 * k + 40 : 48 * k + 48, :] = jnp.zeros((8, CZ), F32)
        line[48 * k : 48 * k + 42, :] = work[pl.ds(single, 42, stride=EXT), :]
        values += [line[48 * k + 8 * j : 48 * k + 8 * j + 8, :] for j in range(6)]
    pack_tiles(message, 0, values)


def conduct_kernel(h, low, high, before, after, out):
    out[0:EXT, :] = before[504:560, :]
    out[41 * EXT : 42 * EXT, :] = after[504:560, :]

    def visit(x, _):
        out[rows_at((x + 1) * EXT + 8, C), :] = h[rows_at(x * C, C), :]
        return 0

    lax.fori_loop(0, C, visit, 0, unroll=4)
    out[pl.ds(EXT + 7, C, stride=EXT), :] = low[360:400, :]
    out[pl.ds(EXT + 48, C, stride=EXT), :] = high[360:400, :]


def apply_kernel(sol, own_z, far_z, resid, cond, coef, out, applied, sums, field, pack, line):
    gz = lax.axis_index("gz")
    lane = lanes(ZROWS2)
    at_face = lax.rem(lane, 9) == jnp.where(gz == 0, 8, 0)
    shift = jnp.where(gz == 0, 7, 121)
    pack[...] = far_z[...] + jnp.where(at_face, roll(own_z[...], shift, 1), 0.0)
    lane8 = lanes(8)
    folded = jnp.where(gz == 0, lane8 - 120, 7 - lane8) >= 0
    base = jnp.where(gz == 0, 120, 127)
    toward = jnp.where(gz == 0, 119, 128)

    def tile(index, to):
        q = index // PER
        return roll(pack[rows_at(8 * q, 8), :], to - 9 * (index - q * PER), 1)

    def visit_fold(p, _):
        for t in range(5):
            at = rows_at(p * EXT + 8 * t + 8, 8)
            field[at, :] = sol[at, :] + jnp.where(folded, tile(p * 5 + t, base), 0.0)
        return 0

    lax.fori_loop(0, 42, visit_fold, 0, unroll=2)
    for k, single in enumerate((7, 48)):
        for j in range(6):
            line[8 * j : 8 * j + 8, :] = jnp.where(folded, tile(210 + 6 * k + j, base), 0.0)
        at = pl.ds(single, 42, stride=EXT)
        field[at, :] = sol[at, :] + line[0:42, :]

    lane40 = lanes(C)
    z_half = jnp.where(lane40 < CZ - 1, 0.5, 0.0)
    outer = jnp.where(lane40 == jnp.where(gz == 0, 0, 127), 0.5, 0.0)

    def visit(x, carry):
        flux_x, sum_a, sum_b = carry
        at = (x + 1) * EXT
        own = rows_at(at + 8, C)
        z, h = field[own, :], cond[own, :]
        ahead = rows_at(at + EXT + 8, C)
        next_x = 0.5 * (h + cond[ahead, :]) * (field[ahead, :] - z)
        z_plane, h_plane = field[rows_at(at, EXT), :], cond[rows_at(at, EXT), :]
        z_up, h_up = roll(z_plane, -1, 0)[8:48], roll(h_plane, -1, 0)[8:48]
        z_down, h_down = roll(z_plane, 1, 0)[8:48], roll(h_plane, 1, 0)[8:48]
        net = (next_x - flux_x) + 0.5 * ((h + h_up) * (z_up - z) - (h + h_down) * (z - z_down))
        flux_z = z_half * (h + roll(h, -1, 1)) * (roll(z, -1, 1) - z)
        far = jnp.concatenate([tile((x + 1) * 5 + t, toward) for t in range(5)], axis=0)
        to = rows_at(x * C, C)
        net = net + (flux_z - roll(flux_z, 1, 1)) + coef[to, :] * (far - z) - outer * h * z
        image = mass_term * z - net
        out[to, :] = z
        applied[to, :] = image
        a, b = resid[to, :] * z, z * image
        for t in range(5):
            sum_a = sum_a + a[8 * t : 8 * t + 8]
            sum_b = sum_b + b[8 * t : 8 * t + 8]
        return next_x, sum_a, sum_b

    own = pl.ds(EXT + 8, C)
    behind = pl.ds(8, C)
    flux = 0.5 * (cond[own, :] + cond[behind, :]) * (field[own, :] - field[behind, :])
    zero8 = jnp.zeros((8, CZ), F32)
    _, sum_a, sum_b = lax.fori_loop(0, C, visit, (flux, zero8, zero8), unroll=2)
    total_a = jnp.sum(sum_a, axis=0, keepdims=True)
    total_b = jnp.sum(sum_b, axis=0, keepdims=True)
    row = lax.broadcasted_iota(jnp.int32, (8, CZ), 0)
    sums[...] = jnp.where(row == 0, total_a, jnp.where(row == 1, total_b, 0.0))


def update_kernel(sums, guess, resid, field, applied, solution_out, resid_out):
    total = jnp.sum(sums[...], axis=1, keepdims=True)
    step = total[0:1, :] / total[1:2, :]
    solution_out[...] = guess[...] + step * field[...]
    resid_out[...] = resid[...] - step * applied[...]


def on_device(gx, splits, right_side, guess_field, conduct_field):
    shape = right_side.shape
    b, v, h = (a.reshape(C * C, CZ) for a in (right_side, guess_field, conduct_field))
    n_gx, n_gy = lax.axis_size(gx), lax.axis_size("gy")
    at_x, at_y = lax.axis_index(gx), lax.axis_index("gy")
    flags = jnp.stack([at_x > 0, at_x < n_gx - 1, at_y > 0, at_y < n_gy - 1]).astype(F32)

    def exchange(axis, up, down):
        n = lax.axis_size(axis)
        forward = [(i, i + 1) for i in range(n - 1)]
        backward = [(i + 1, i) for i in range(n - 1)]
        return lax.ppermute(up, axis, forward), lax.ppermute(down, axis, backward)

    def swap(value):
        return lax.ppermute(value, "gz", [(0, 1), (1, 0)])

    plane, forward, inverse, denom, eigen = tables()

    part, vh, up, down, edge = call(
        residual_kernel, (1600, 1600, YROWS, YROWS, 160), v, h, b, name="residual"
    )
    low, high = exchange("gy", up, down)
    part, vh, right, left = call(
        extend_y_kernel,
        (C * EXT, C * EXT, XROWS, XROWS),
        flags, part, vh, up, down, edge, low, high,
        smem=(0,),
        name="extend_y",
    )
    before, after = exchange(gx, right, left)
    ext, own_z = call(
        extend_x_kernel,
        (EXT * EXT, ZROWS),
        flags, part, vh, right, left, before, after,
        scratch=[pltpu.VMEM((EXT * EXT, CZ), F32)],
        smem=(0,),
        name="extend_x",
    )
    far_z = swap(own_z)
    (cond,) = call(conduct_kernel, (42 * EXT,), h, low, high, before, after, name="conduct")
    big = pltpu.VMEM((EXT * EXT, CZ), F32)
    small = pltpu.VMEM((ZROWS, CZ), F32)
    resid, coef, sol, strip, right, left = call(
        solve_kernel,
        (1600, 1600, EXT * EXT, EXT * EXT, XROWS2, XROWS2),
        eigen, ext, own_z, far_z, plane, forward, inverse, denom,
        scratch=[small, small, big, big, big, big, big],
        smem=(0,),
        limit=32,
        name="solve",
    )
    before, after = exchange(gx, right, left)
    sol, strip, up, down = call(
        fold_x_kernel,
        (42 * EXT, 42 * EXT, YROWS2, YROWS2),
        flags, sol, strip, before, after,
        scratch=[pltpu.VMEM((48, CZ), F32)],
        smem=(0,),
        name="fold_x",
    )
    low, high = exchange("gy", up, down)
    sol, own_z = call(
        fold_y_kernel,
        (42 * EXT, ZROWS2),
        flags, sol, strip, low, high,
        scratch=[pltpu.VMEM((42 * EXT, CZ), F32), pltpu.VMEM((96, CZ), F32)],
        smem=(0,),
        name="fold_y",
    )
    far_z = swap(own_z)
    field, applied, sums = call(
        apply_kernel,
        (1600, 1600, 8),
        sol, own_z, far_z, resid, cond, coef,
        scratch=[
            pltpu.VMEM((42 * EXT, CZ), F32),
            pltpu.VMEM((ZROWS2, CZ), F32),
            pltpu.VMEM((48, CZ), F32),
        ],
        name="apply",
    )
    for axes in splits:
        sums = lax.psum(sums, axes)
    out, resid = call(
        update_kernel, (1600, 1600), sums, v, resid, field, applied, name="update"
    )
    return out.reshape(shape), resid.reshape(shape)


def solution(mesh):
    n_gx, n_gy, n_gz = mesh.devices.shape
    if n_gx == 64:
        mesh = Mesh(mesh.devices.reshape(4, 8, 2, n_gy, n_gz), ("gx_x", "gx_y", "gx_c", "gy", "gz"))
        gx = ("gx_x", "gx_y", "gx_c")
        splits = (("gx_c",), ("gx_x",), ("gx_y",), ("gy", "gz"))
    else:
        gx = "gx"
        splits = (("gx", "gy", "gz"),)
    placed = P(gx, "gy", "gz")
    return jax.shard_map(
        functools.partial(on_device, gx, splits),
        mesh=mesh,
        in_specs=(placed,) * 3,
        out_specs=(placed,) * 2,
        check_vma=False,
    )
```

```python
import functools

import jax
import jax.numpy as jnp
import ml_dtypes
import numpy as np
from jax import lax
from jax.experimental import pallas as pl
from jax.experimental.pallas import tpu as pltpu
from jax.sharding import Mesh
from jax.sharding import PartitionSpec as P

OVER = 8
C = 40
CZ = 128
EXT = C + 2 * OVER
EXTZ = CZ + 2 * OVER
TILES = EXT // 8
stiff_scale = 3.0
mass_term = 0.001

F32 = jnp.float32
BF16 = jnp.bfloat16
VMEM = pl.BlockSpec(memory_space=pltpu.VMEM)
SMEM = pl.BlockSpec(memory_space=pltpu.SMEM)
HBM = pl.BlockSpec(memory_space=pltpu.HBM)

YROWS = 440
XROWS = 568
PER_Z = 12
BLOCKS_Z = -(-EXT // PER_Z)
ZROWS = BLOCKS_Z * EXT
PER = 14
XROWS2 = 9 * EXT + 40
YROWS2 = 416
ZGROUPS2 = 42 * 5 + 12
ZROWS2 = 8 * -(-ZGROUPS2 // PER)


def sine_table(count):
    k = np.arange(1, count + 1)
    basis = np.sqrt(2.0 / (count + 1)) * np.sin(np.pi * k[:, None] * k[None, :] / (count + 1))
    eigen = 2.0 - 2.0 * np.cos(np.pi * k / (count + 1))
    return basis, eigen


def two_parts(table):
    high = table.astype(ml_dtypes.bfloat16)
    low = (table - high.astype(np.float64)).astype(ml_dtypes.bfloat16)
    return high, low


@functools.cache
def tables():
    basis, eigen = sine_table(EXT)
    basis_z, eigen_z = sine_table(EXTZ)
    high, low = two_parts(basis)
    plane = np.zeros((EXT, 192), ml_dtypes.bfloat16)
    plane[:, 0:EXT] = high
    plane[:, 64 : 64 + EXT] = low
    plane[:, 128 : 128 + EXT] = high
    forward = np.zeros((2, 256, 256))
    inverse = np.zeros((2, 256, 256))
    for gz in range(2):
        own = basis_z[8 : 8 + CZ]
        strip = basis_z[136:144] if gz == 0 else basis_z[0:8]
        face_own, face_far = (135, 136) if gz == 0 else (8, 7)
        forward[gz, :CZ, :EXTZ] = own
        forward[gz, CZ, :EXTZ] = basis_z[face_own] - basis_z[face_far]
        forward[gz, CZ + 2 : CZ + 10, :EXTZ] = strip
        inverse[gz, :EXTZ, :CZ] = own.T
        inverse[gz, :EXTZ, CZ : CZ + 9] = (basis_z[135:144] if gz == 0 else basis_z[0:9]).T

    def stacked(table):
        high, low = two_parts(table)
        return np.concatenate([high, high, low], axis=1)

    denom = np.full((EXT, 256), 1.0)
    denom[:, :EXTZ] = stiff_scale * (eigen[:, None] + eigen_z[None, :]) + mass_term
    return (
        plane,
        stacked(forward),
        stacked(inverse),
        denom.astype(np.float32),
        (stiff_scale * eigen).astype(np.float32),
    )


def roll(value, shift, axis):
    if isinstance(shift, int):
        shift = shift % value.shape[axis]
        return value if shift == 0 else pltpu.roll(value, shift, axis)
    return pltpu.roll(value, lax.rem(shift + 2 * value.shape[axis], value.shape[axis]), axis)


def lanes(rows):
    return lax.broadcasted_iota(jnp.int32, (rows, CZ), 1)


def rows_at(start, size):
    return pl.ds(pl.multiple_of(start, 8), size)


def tile_at(index):
    return rows_at(index * 8, 8)


def call(body, out_rows, *args, scratch=(), limit=16, name=None, smem=(), hbm=(), work=0):
    place = {**{i: SMEM for i in smem}, **{i: HBM for i in hbm}}
    return pl.pallas_call(
        body,
        out_shape=[jax.ShapeDtypeStruct((rows, CZ), F32) for rows in out_rows],
        in_specs=[place.get(i, VMEM) for i in range(len(args))],
        out_specs=[VMEM] * len(out_rows),
        scratch_shapes=list(scratch),
        compiler_params=pltpu.CompilerParams(vmem_limit_bytes=limit * 2**20),
        cost_estimate=pl.CostEstimate(
            flops=int(work * 1e9), bytes_accessed=int(work * 2e6), transcendentals=0
        )
        if work
        else None,
        name=name,
    )(*args)


def strip_base():
    return jnp.where(lax.axis_index("gz") == 0, 118, 126)


def face_lane():
    return jnp.where(lax.axis_index("gz") == 0, 127, 0)


def outer_lane():
    return jnp.where(lax.axis_index("gz") == 0, 0, 127)


CHUNKS = 5


def pair_of(v, h, lane, base, face):
    return jnp.where(lane == base, roll(v, base - face, 1), 0.0) + jnp.where(
        lane == base + 1, roll(h, base + 1 - face, 1), 0.0
    )


def residual_kernel(v_in, h_in, b_in, part, up, down, edge, v, h, b, sems):
    base, face = strip_base(), face_lane()
    size = C * C // CHUNKS
    copies = []
    for c in range(CHUNKS):
        at = pl.ds(c * size, size)
        for k, (source, target) in enumerate(((v_in, v), (h_in, h), (b_in, b))):
            copies.append(pltpu.make_async_copy(source.at[at, :], target.at[at, :], sems.at[k, c]))
            copies[-1].start()
    lane, lane8 = lanes(C), lanes(8)
    row = lax.broadcasted_iota(jnp.int32, (C, CZ), 0)
    y_half = jnp.where(row > 0, 0.5, 0.0)
    z_half = jnp.where(lane < CZ - 1, 0.5, 0.0)
    outer = jnp.where(lane == outer_lane(), 0.5, 0.0)
    flux_x = jnp.zeros((C, CZ), F32)
    pack_up = jnp.zeros((8, CZ), F32)
    pack_down = jnp.zeros((8, CZ), F32)
    waited = 0
    for x in range(C):
        need = min((x + 1) // 8 + 1, CHUNKS)
        while waited < need:
            for k in range(3):
                copies[3 * waited + k].wait()
            waited += 1
        vi, hi = v[x * C : x * C + C, :], h[x * C : x * C + C, :]
        flux_y = y_half * (hi + roll(hi, 1, 0)) * (vi - roll(vi, 1, 0))
        flux_z = z_half * (hi + roll(hi, -1, 1)) * (roll(vi, -1, 1) - vi)
        applied = (
            mass_term * vi
            - (roll(flux_y, -1, 0) - flux_y)
            - (flux_z - roll(flux_z, 1, 1))
            + outer * hi * vi
        )
        if x < C - 1:
            to = pl.ds((x + 1) * C, C)
            next_x = 0.5 * (hi + h[to, :]) * (v[to, :] - vi)
            applied = applied - (next_x - flux_x)
            flux_x = next_x
        else:
            applied = applied + flux_x
        resid = b[x * C : x * C + C, :] - applied
        part[x * C : x * C + C, :] = resid
        down[8 * x : 8 * x + 8, :] = resid[0:8]
        up[8 * x : 8 * x + 8, :] = resid[32:40]
        pack_up = pack_up + roll(pair_of(vi[32:40], hi[32:40], lane8, base, face), 2 * x, 1)
        pack_down = pack_down + roll(pair_of(vi[0:8], hi[0:8], lane8, base, face), 2 * x, 1)
    up[432:440, :] = roll(pack_up, -base, 1)
    down[432:440, :] = roll(pack_down, -base, 1)
    last = (C - 1) * C
    for message, first in ((up, 32), (down, 0)):
        face_row = C - 1 if first else 0
        message[320:360, :] = v[pl.ds(face_row, C, stride=C), :]
        message[360:400, :] = h[pl.ds(face_row, C, stride=C), :]
        message[400:408, :] = v[first : first + 8, :]
        message[408:416, :] = h[first : first + 8, :]
        message[416:424, :] = v[last + first : last + first + 8, :]
        message[424:432, :] = h[last + first : last + first + 8, :]
    edge[0:40, :] = v[0:40, :]
    edge[40:80, :] = h[0:40, :]
    edge[80:120, :] = v[last : last + 40, :]
    edge[120:160, :] = h[last : last + 40, :]


def pairs_kernel(v, h, out):
    base, face = strip_base(), face_lane()
    lane = lanes(C)

    def visit(x, _):
        at = rows_at(x * C, C)
        out[at, :] = pair_of(v[at, :], h[at, :], lane, base, face)
        return 0

    lax.fori_loop(0, C, visit, 0, unroll=8)


def scale_kernel(eigen, denom, out_a, out_b):
    def visit(y, _):
        value = 1.0 / (denom[...] + eigen[y])
        at = rows_at(y * EXT, EXT)
        out_a[at, :] = value[:, :CZ]
        out_b[at, :] = value[:, CZ:]
        return 0

    lax.fori_loop(0, EXT, visit, 0, unroll=4)


def pick(pack, index, to):
    pair = lax.div(lanes(8), 2) == index
    return roll(jnp.where(pair, pack, 0.0), to - 2 * index, 1)


def extend_y_kernel(flags, part, vh, up, down, edge, low, high, out, right, left):
    base = strip_base()
    for x in range(C):
        out[x * EXT : x * EXT + 8, :] = low[8 * x : 8 * x + 8, :]
        out[x * EXT + 8 : x * EXT + 48, :] = part[x * C : x * C + C, :]
        out[x * EXT + 48 : x * EXT + 56, :] = high[8 * x : 8 * x + 8, :]
    flux = 0.5 * (low[360:400, :] + down[360:400, :]) * (down[320:360, :] - low[320:360, :])
    out[pl.ds(8, C, stride=EXT), :] = out[pl.ds(8, C, stride=EXT), :] - flux
    out[pl.ds(7, C, stride=EXT), :] = out[pl.ds(7, C, stride=EXT), :] + flux * flags[2]
    flux = 0.5 * (up[360:400, :] + high[360:400, :]) * (high[320:360, :] - up[320:360, :])
    out[pl.ds(47, C, stride=EXT), :] = out[pl.ds(47, C, stride=EXT), :] + flux
    out[pl.ds(48, C, stride=EXT), :] = out[pl.ds(48, C, stride=EXT), :] - flux * flags[3]
    for message, first, strip, own in ((left, 0, 400, 0), (right, 32, 416, 80)):
        message[0:448, :] = out[first * EXT : first * EXT + 448, :]
        for k in range(2):
            at = 448 + k * EXT
            message[at : at + 8, :] = low[strip + 8 * k : strip + 8 * k + 8, :]
            message[at + 8 : at + 48, :] = edge[own + 40 * k : own + 40 * k + 40, :]
            message[at + 48 : at + 56, :] = high[strip + 8 * k : strip + 8 * k + 8, :]
        near = jnp.zeros((8, CZ), F32)
        taken = jnp.zeros((8, CZ), F32)
        for i in range(OVER):
            x = first + i
            for t in range(5):
                at = x * C + 8 * t
                near = near + roll(vh[at : at + 8, :], 2 * (i * TILES + 1 + t), 1)
            taken = taken + pick(low[432:440, :], x, 2 * i * TILES)
            taken = taken + pick(high[432:440, :], x, 2 * (i * TILES + 6))
        message[560:568, :] = roll(near, -base, 1) + taken


def extend_x_kernel(flags, part, vh, low, high, right, left, before, after, out, message):
    base = strip_base()
    gz = lax.axis_index("gz")
    lane = lanes(8)
    strip_lanes = jnp.where(gz == 0, lane - 120, 7 - lane) >= 0
    side = OVER * EXT
    out[0:side, :] = before[0:side, :]
    out[side : side + C * EXT, :] = part[...]
    out[side + C * EXT : EXT * EXT, :] = after[0:side, :]
    flux = 0.5 * (before[504:560, :] + left[504:560, :]) * (left[448:504, :] - before[448:504, :])
    at = OVER * EXT
    out[at : at + EXT, :] = out[at : at + EXT, :] - flux
    out[at - EXT : at, :] = out[at - EXT : at, :] + flux * flags[0]
    flux = 0.5 * (right[504:560, :] + after[504:560, :]) * (after[448:504, :] - right[448:504, :])
    at = (OVER + C) * EXT
    out[at - EXT : at, :] = out[at - EXT : at, :] + flux
    out[at : at + EXT, :] = out[at : at + EXT, :] - flux * flags[1]
    for q in range(BLOCKS_Z):
        for t in range(TILES):
            near = jnp.zeros((8, CZ), F32)
            taken = jnp.zeros((8, CZ), F32)
            for j in range(min(PER_Z, EXT - q * PER_Z)):
                x = q * PER_Z + j
                own = x - OVER
                at = x * EXT + 8 * t
                value = jnp.where(strip_lanes, out[at : at + 8, :], 0.0)
                if own < 0:
                    taken = taken + pick(before[560:568, :], x * TILES + t, 10 * j)
                elif own >= C:
                    taken = taken + pick(after[560:568, :], (own - C) * TILES + t, 10 * j)
                elif t == 0:
                    taken = taken + pick(low[432:440, :], own, 10 * j)
                elif t == 6:
                    taken = taken + pick(high[432:440, :], own, 10 * j)
                else:
                    start = own * C + 8 * (t - 1)
                    value = value + vh[start : start + 8, :]
                near = near + roll(value, 10 * j, 1)
            at = q * EXT + 8 * t
            message[at : at + 8, :] = roll(near, -base, 1) + taken


def halves(value):
    high = value.astype(BF16)
    return high, (value - high.astype(F32)).astype(BF16)


def dot(a, b):
    return jnp.dot(a, b, preferred_element_type=F32)


def along_lanes(value, table):
    high, low = halves(value)
    return dot(jnp.concatenate([high, low, high], axis=1), table)


def along_rows(table, value):
    padded = jnp.concatenate([value, jnp.zeros((8, value.shape[1]), F32)], axis=0)
    high, low = halves(padded)
    return dot(table, jnp.concatenate([high, high, low], axis=0))


def beside(a, b):
    return jnp.concatenate([a, b], axis=1)


def forward_kernel(plane, ext, out, first):
    table = plane[...]

    def visit_y(c, _):
        for i in range(14):
            x = 2 * (c * 14 + i)
            at, then = rows_at(x * EXT, EXT), rows_at((x + 1) * EXT, EXT)
            value = along_rows(table, beside(ext[at, :], ext[then, :]))
            first[at, :] = value[:, :CZ]
            first[then, :] = value[:, CZ:]
        return 0

    lax.fori_loop(0, 2, visit_y, 0)

    def visit_x(c, _):
        for i in range(14):
            y = 2 * (c * 14 + i)
            value = beside(first[pl.ds(y, EXT, stride=EXT), :], first[pl.ds(y + 1, EXT, stride=EXT), :])
            value = along_rows(table, value)
            out[rows_at(y * EXT, EXT), :] = value[:, :CZ]
            out[rows_at((y + 1) * EXT, EXT), :] = value[:, CZ:]
        return 0

    lax.fori_loop(0, 2, visit_x, 0)


def face_terms(own_z, far_z):
    both = own_z[...] + far_z[...]
    half = 0.5 * roll(both, -1, 1)
    return half, half * (far_z[...] - own_z[...])


STEP = 8


def solve_kernel(
    own_z, far_z, main, plane, forward, inverse, scale_a, scale_b,
    second_a, second_b, sol, strip, right, left, halo,
):
    gz = lax.axis_index("gz")
    table = plane[...]
    _, flux = face_terms(own_z, far_z)
    pack = jnp.where(lax.rem(lanes(ZROWS), 10) == 0, flux, far_z[...])
    blocks = [pack[q * EXT : (q + 1) * EXT] for q in range(BLOCKS_Z)]
    done = []
    for q in range(0, BLOCKS_Z - 1, 2):
        value = along_rows(table, beside(blocks[q], blocks[q + 1]))
        done += [value[:, :CZ], value[:, CZ:]]
    done.append(along_rows(table, blocks[-1]))
    for x in range(EXT):
        q, j = x // PER_Z, x % PER_Z
        halo[x * EXT : (x + 1) * EXT, :] = roll(done[q], -10 * j, 1)

    forward_table = forward[gz]
    inverse_table = inverse[gz]

    def visit(c, _):
        parts = []
        for i in range(0, STEP, 2):
            y = c * STEP + i
            value = beside(halo[pl.ds(y, EXT, stride=EXT), :], halo[pl.ds(y + 1, EXT, stride=EXT), :])
            value = along_rows(table, value)
            parts.append(beside(main[rows_at(y * EXT, EXT), :], value[:, :CZ]))
            parts.append(beside(main[rows_at((y + 1) * EXT, EXT), :], value[:, CZ:]))
        value = along_lanes(jnp.concatenate(parts, axis=0), forward_table)
        at = rows_at(c * STEP * EXT, STEP * EXT)
        value = value * beside(scale_a[at, :], scale_b[at, :])
        for i in range(STEP):
            part = along_rows(table, value[i * EXT : (i + 1) * EXT])
            to = pl.ds(c * STEP + i, EXT, stride=EXT)
            second_a[to, :] = part[:, :CZ]
            second_b[to, :] = part[:, CZ:]
        return 0

    lax.fori_loop(0, EXT // STEP, visit, 0)

    for k, (message, start) in enumerate(((left, 0), (right, 47))):
        inverse_planes(table, inverse_table, second_a, second_b, sol, strip, range(start, start + 9), 9 * k)
        message[0 : 9 * EXT, :] = sol[9 * k * EXT : 9 * (k + 1) * EXT, :]
        tiles = [strip[pl.ds((9 * k * TILES + j) * 8, 8), :] for j in range(63)]
        pack_tiles(message, 9 * EXT, tiles)


def inverse_planes(table, inverse_table, second_a, second_b, sol, strip, planes, to):
    parts = []
    for x in planes:
        at = pl.ds(x * EXT, EXT)
        parts.append(along_rows(table, beside(second_a[at, :], second_b[at, :])))
    value = along_lanes(jnp.concatenate(parts, axis=0), inverse_table)
    at = pl.ds(to * EXT, len(planes) * EXT)
    sol[at, :] = value[:, :CZ]
    strip[at, :] = value[:, CZ:]


def rest_kernel(plane, inverse, second_a, second_b, sol, strip):
    table, inverse_table = plane[...], inverse[lax.axis_index("gz")]
    for first, last in ((9, 19), (19, 29), (29, 38), (38, 47)):
        inverse_planes(
            table, inverse_table, second_a, second_b, sol, strip, range(first, last), first - 9
        )


def own_kernel(h, low, high, before, after, ext, own_z, far_z, resid, c_x, c_down, c_up, c_z, c_face, cond):
    face, outer = face_lane(), outer_lane()
    half, flux = face_terms(own_z, far_z)
    half, flux = roll(half, face, 1), roll(flux, face, 1)
    lane8 = lanes(8)
    for x in range(C):
        q, j = (x + OVER) // PER_Z, (x + OVER) % PER_Z
        for t in range(5):
            at = q * EXT + 8 * (t + 1)
            to = x * C + 8 * t
            source = (x + OVER) * EXT + 8 * (t + 1)
            moved = jnp.where(lane8 == face, roll(flux[at : at + 8], -10 * j, 1), 0.0)
            resid[to : to + 8, :] = ext[source : source + 8, :] + moved
            c_face[to : to + 8, :] = jnp.where(
                lane8 == face, roll(half[at : at + 8], -10 * j, 1), 0.0
            )
    cond[0:C, :] = before[512:552, :]
    cond[C : C + C * C, :] = h[...]
    cond[C + C * C :, :] = after[512:552, :]
    z_half = jnp.where(lanes(C) < CZ - 1, 0.5, 0.0)
    row = lax.broadcasted_iota(jnp.int32, (C, CZ), 0)
    for x in range(C):
        at = x * C
        hi = h[at : at + C, :]
        c_x[at : at + C, :] = 0.5 * (cond[at : at + C, :] + hi)
        below = jnp.where(row == 0, low[360 + x : 361 + x, :], roll(hi, 1, 0))
        above = jnp.where(row == C - 1, high[360 + x : 361 + x, :], roll(hi, -1, 0))
        c_down[at : at + C, :] = 0.5 * (hi + below)
        c_up[at : at + C, :] = 0.5 * (hi + above)
        c_z[at : at + C, :] = z_half * (hi + roll(hi, -1, 1))
    c_x[C * C :, :] = 0.5 * (cond[C * C : C * C + C, :] + cond[C * C + C :, :])


def pack_tiles(message, at, values):
    for q in range(-(-len(values) // PER)):
        acc = values[q * PER]
        for j, value in enumerate(values[q * PER + 1 : (q + 1) * PER], 1):
            acc = acc + roll(value, 9 * j, 1)
        message[at + 8 * q : at + 8 * q + 8, :] = acc


def unpack_tile(message, at, index):
    q = index // PER
    return roll(message[rows_at(at + 8 * q, 8), :], -9 * (index - q * PER), 1)


def fold_x_kernel(flags, sides, side_strip, sol, strip, before, after, out, out_strip, up, down, line):
    size = 42 * EXT
    narrow = lanes(8) < 9
    for target, outside, inside in ((out, sides, sol), (out_strip, side_strip, strip)):
        target[0 : 2 * EXT, :] = outside[7 * EXT : 9 * EXT, :]
        target[2 * EXT : 40 * EXT, :] = inside[...]
        target[40 * EXT : size, :] = outside[9 * EXT : 11 * EXT, :]
    out[0 : 9 * EXT, :] = out[0 : 9 * EXT, :] + before[0 : 9 * EXT, :]
    tail = 33 * EXT
    out[tail:size, :] = out[tail:size, :] + after[0 : 9 * EXT, :]

    for j in range(63):
        for message, at in ((before, 8 * j), (after, tail + 8 * j)):
            value = jnp.where(narrow, unpack_tile(message, 9 * EXT, j), 0.0)
            out_strip[at : at + 8, :] = out_strip[at : at + 8, :] + value

    for array in (out, out_strip):
        array[0:EXT, :] = array[0:EXT, :] * flags[0]
        array[41 * EXT : size, :] = array[41 * EXT : size, :] * flags[1]

    for message, tile, single in ((up, 6, 47), (down, 0, 8)):
        for p in range(42):
            message[8 * p : 8 * p + 8, :] = out[p * EXT + 8 * tile : p * EXT + 8 * tile + 8, :]
        message[376:384, :] = jnp.zeros((8, CZ), F32)
        message[336:378, :] = out[pl.ds(single, 42, stride=EXT), :]
        line[40:48, :] = jnp.zeros((8, CZ), F32)
        line[0:42, :] = out_strip[pl.ds(single, 42, stride=EXT), :]
        values = [out_strip[p * EXT + 8 * tile : p * EXT + 8 * tile + 8, :] for p in range(42)]
        values += [line[8 * j : 8 * j + 8, :] for j in range(6)]
        pack_tiles(message, 384, values)


def fold_y_kernel(flags, sol, strip, low, high, out, message, work, line):
    narrow = lanes(8) < 9
    out[...] = sol[...]
    work[...] = strip[...]
    for source, tile, single, flag in ((low, 1, 7, 2), (high, 5, 48, 3)):
        for p in range(42):
            at = p * EXT + 8 * tile
            out[at : at + 8, :] = out[at : at + 8, :] + source[8 * p : 8 * p + 8, :]
            value = jnp.where(narrow, unpack_tile(source, 384, p), 0.0)
            work[at : at + 8, :] = work[at : at + 8, :] + value
        at = pl.ds(single, 42, stride=EXT)
        out[at, :] = (out[at, :] + source[336:378, :]) * flags[flag]
        for j in range(6):
            line[8 * j : 8 * j + 8, :] = jnp.where(narrow, unpack_tile(source, 384, 42 + j), 0.0)
        work[at, :] = (work[at, :] + line[0:42, :]) * flags[flag]
    values = []
    for p in range(42):
        for t in range(1, 6):
            at = p * EXT + 8 * t
            values.append(work[at : at + 8, :])
    for k, single in enumerate((7, 48)):
        line[48 * k + 40 : 48 * k + 48, :] = jnp.zeros((8, CZ), F32)
        line[48 * k : 48 * k + 42, :] = work[pl.ds(single, 42, stride=EXT), :]
        values += [line[48 * k + 8 * j : 48 * k + 8 * j + 8, :] for j in range(6)]
    pack_tiles(message, 0, values)


def apply_kernel(
    sol, own_z, far_z, resid, c_x, c_down, c_up, c_z, c_face, h,
    out, applied, sums, field, pack, line,
):
    gz = lax.axis_index("gz")
    lane = lanes(ZROWS2)
    at_face = lax.rem(lane, 9) == jnp.where(gz == 0, 8, 0)
    shift = jnp.where(gz == 0, 7, 121)
    packed = far_z[...] + jnp.where(at_face, roll(own_z[...], shift, 1), 0.0)
    pack[...] = roll(packed, jnp.where(gz == 0, 120, 127), 1)
    toward = jnp.where(gz == 0, 127, 1)
    lane8 = lanes(8)
    folded = jnp.where(gz == 0, lane8 - 120, 7 - lane8) >= 0

    def tile(index):
        q, j = divmod(index, PER)
        return roll(pack[8 * q : 8 * q + 8, :], -9 * j, 1)

    for p in range(42):
        for t in range(5):
            at = p * EXT + 8 * t + 8
            field[at : at + 8, :] = sol[at : at + 8, :] + jnp.where(folded, tile(p * 5 + t), 0.0)
    for k, single in enumerate((7, 48)):
        for j in range(6):
            line[8 * j : 8 * j + 8, :] = jnp.where(folded, tile(210 + 6 * k + j), 0.0)
        at = pl.ds(single, 42, stride=EXT)
        field[at, :] = sol[at, :] + line[0:42, :]
    pack[...] = roll(pack[...], toward, 1)

    outer = jnp.where(lanes(C) == outer_lane(), 0.5, 0.0)
    flux_x = c_x[0:C, :] * (field[EXT + 8 : EXT + 48, :] - field[8:48, :])
    sum_a = jnp.zeros((8, CZ), F32)
    sum_b = jnp.zeros((8, CZ), F32)
    for x in range(C):
        at = (x + 1) * EXT
        to = pl.ds(x * C, C)
        z = field[at + 8 : at + 48, :]
        next_x = c_x[x * C + C : x * C + 2 * C, :] * (field[at + EXT + 8 : at + EXT + 48, :] - z)
        net = next_x - flux_x
        flux_x = next_x
        net = net + c_up[to, :] * (field[at + 9 : at + 49, :] - z)
        net = net - c_down[to, :] * (z - field[at + 7 : at + 47, :])
        flux_z = c_z[to, :] * (roll(z, -1, 1) - z)
        far = jnp.concatenate([tile((x + 1) * 5 + t) for t in range(5)], axis=0)
        net = net + (flux_z - roll(flux_z, 1, 1)) + c_face[to, :] * (far - z)
        image = mass_term * z - net + outer * h[to, :] * z
        out[to, :] = z
        applied[to, :] = image
        a, b = resid[to, :] * z, z * image
        for t in range(5):
            sum_a = sum_a + a[8 * t : 8 * t + 8]
            sum_b = sum_b + b[8 * t : 8 * t + 8]
    total_a = jnp.sum(sum_a, axis=0, keepdims=True)
    total_b = jnp.sum(sum_b, axis=0, keepdims=True)
    total_a = total_a + roll(total_a, CZ // 2, 1)
    total_b = total_b + roll(total_b, CZ // 2, 1)
    total = jnp.where(lanes(1) < CZ // 2, total_a, total_b)
    sums[...] = jnp.broadcast_to(total, sums.shape)


def gather_kernel(sums, out):
    out[...] = jnp.broadcast_to(jnp.sum(sums[...], axis=0, keepdims=True), out.shape)


def update_kernel(sums, guess, resid, field, applied, solution_out, resid_out):
    total = jnp.sum(sums[...], axis=0, keepdims=True)
    first = lanes(1) < CZ // 2
    above = jnp.sum(jnp.where(first, total, 0.0), axis=1, keepdims=True)
    below = jnp.sum(jnp.where(first, 0.0, total), axis=1, keepdims=True)
    step = above / below
    solution_out[...] = guess[...] + step * field[...]
    resid_out[...] = resid[...] - step * applied[...]


def on_device(gx, splits, right_side, guess_field, conduct_field):
    shape = right_side.shape
    b, v, h = (a.reshape(C * C, CZ) for a in (right_side, guess_field, conduct_field))
    n_gx, n_gy = lax.axis_size(gx), lax.axis_size("gy")
    at_x, at_y = lax.axis_index(gx), lax.axis_index("gy")
    flags = jnp.stack([at_x > 0, at_x < n_gx - 1, at_y > 0, at_y < n_gy - 1]).astype(F32)

    def exchange(axis, up, down):
        n = lax.axis_size(axis)
        forward = [(i, i + 1) for i in range(n - 1)]
        backward = [(i + 1, i) for i in range(n - 1)]
        return lax.ppermute(up, axis, forward), lax.ppermute(down, axis, backward)

    def swap(value):
        return lax.ppermute(value, "gz", [(0, 1), (1, 0)])

    plane, forward, inverse, denom, eigen = tables()
    own = C * C
    box = EXT * EXT

    def buffer(rows):
        return pltpu.VMEM((rows, CZ), F32)

    part, up, down, edge = call(
        residual_kernel, (own, YROWS, YROWS, 160), v, h, b,
        scratch=[buffer(own)] * 3 + [pltpu.SemaphoreType.DMA((3, CHUNKS))],
        hbm=(0, 1, 2), name="residual", work=2,
    )
    low, high = exchange("gy", up, down)
    (pairs,) = call(pairs_kernel, (own,), v, h, name="pairs", work=1)
    scale_a, scale_b = call(
        scale_kernel, (box, box), eigen, denom, smem=(0,), name="scale", work=2
    )
    part, right, left = call(
        extend_y_kernel, (C * EXT, XROWS, XROWS),
        flags, part, pairs, up, down, edge, low, high,
        smem=(0,), name="extend_y", work=1,
    )
    before, after = exchange(gx, right, left)
    ext, own_z = call(
        extend_x_kernel, (box, ZROWS),
        flags, part, pairs, low, high, right, left, before, after,
        smem=(0,), name="extend_x", work=1,
    )
    far_z = swap(own_z)
    (main,) = call(forward_kernel, (box,), plane, ext, scratch=[buffer(box)], name="forward", work=2)
    second_a, second_b, sides, side_strip, right, left = call(
        solve_kernel, (box, box, 18 * EXT, 18 * EXT, XROWS2, XROWS2),
        own_z, far_z, main, plane, forward, inverse, scale_a, scale_b,
        scratch=[buffer(box)], name="solve", work=6,
    )
    resid, c_x, c_down, c_up, c_z, c_face = call(
        own_kernel, (own, own + C, own, own, own, own),
        h, low, high, before, after, ext, own_z, far_z,
        scratch=[buffer(own + 2 * C)], name="own", work=2,
    )
    before, after = exchange(gx, right, left)
    sol, strip = call(
        rest_kernel, (38 * EXT, 38 * EXT), plane, inverse, second_a, second_b, name="rest", work=2
    )
    sol, strip, up, down = call(
        fold_x_kernel, (42 * EXT, 42 * EXT, YROWS2, YROWS2),
        flags, sides, side_strip, sol, strip, before, after,
        scratch=[buffer(48)], smem=(0,), name="fold_x", work=1,
    )
    low, high = exchange("gy", up, down)
    sol, own_z = call(
        fold_y_kernel, (42 * EXT, ZROWS2),
        flags, sol, strip, low, high,
        scratch=[buffer(42 * EXT), buffer(96)], smem=(0,), name="fold_y", work=1,
    )
    far_z = swap(own_z)
    first, last = splits
    field, applied, sums = call(
        apply_kernel, (own, own, lax.axis_size(first)),
        sol, own_z, far_z, resid, c_x, c_down, c_up, c_z, c_face, h,
        scratch=[buffer(42 * EXT), buffer(ZROWS2), buffer(48)], name="apply", work=3,
    )
    sums = lax.all_to_all(sums, first, 0, 0, tiled=True)
    (sums,) = call(gather_kernel, (lax.axis_size(last),), sums, name="gather")
    sums = lax.all_to_all(sums, last, 0, 0, tiled=True)
    out, resid = call(update_kernel, (own, own), sums, v, resid, field, applied, name="update", work=2)
    return out.reshape(shape), resid.reshape(shape)


def solution(mesh):
    n_gx, n_gy, n_gz = mesh.devices.shape
    if n_gx == 64:
        mesh = Mesh(mesh.devices.reshape(4, 8, 2, n_gy, n_gz), ("gx_x", "gx_y", "gx_c", "gy", "gz"))
        gx = ("gx_x", "gx_y", "gx_c")
        splits = (("gx_x", "gx_y"), ("gx_c", "gy", "gz"))
    else:
        gx = "gx"
        splits = (("gx",), ("gy", "gz"))
    placed = P(gx, "gy", "gz")
    return jax.shard_map(
        functools.partial(on_device, gx, splits),
        mesh=mesh,
        in_specs=(placed,) * 3,
        out_specs=(placed,) * 2,
        check_vma=False,
    )
```

```python
import functools

import jax
import jax.numpy as jnp
import ml_dtypes
import numpy as np
from jax import lax
from jax.experimental import pallas as pl
from jax.experimental.pallas import tpu as pltpu
from jax.sharding import Mesh
from jax.sharding import PartitionSpec as P

OVER = 8
C = 40
CZ = 128
EXT = C + 2 * OVER
EXTZ = CZ + 2 * OVER
TILES = EXT // 8
stiff_scale = 3.0
mass_term = 0.001

F32 = jnp.float32
BF16 = jnp.bfloat16
VMEM = pl.BlockSpec(memory_space=pltpu.VMEM)
SMEM = pl.BlockSpec(memory_space=pltpu.SMEM)
HBM = pl.BlockSpec(memory_space=pltpu.HBM)

YROWS = 440
XROWS = 616
PER_Z = 12
BLOCKS_Z = -(-EXT // PER_Z)
ZROWS = BLOCKS_Z * EXT
PER = 14
XROWS2 = 9 * EXT + 40
YROWS2 = 416
ZGROUPS2 = 42 * 5 + 12
ZROWS2 = 8 * -(-ZGROUPS2 // PER)


def sine_table(count):
    k = np.arange(1, count + 1)
    basis = np.sqrt(2.0 / (count + 1)) * np.sin(np.pi * k[:, None] * k[None, :] / (count + 1))
    eigen = 2.0 - 2.0 * np.cos(np.pi * k / (count + 1))
    return basis, eigen


def two_parts(table):
    high = table.astype(ml_dtypes.bfloat16)
    low = (table - high.astype(np.float64)).astype(ml_dtypes.bfloat16)
    return high, low


@functools.cache
def tables():
    basis, eigen = sine_table(EXT)
    basis_z, eigen_z = sine_table(EXTZ)
    high, low = two_parts(basis)
    plane = np.zeros((EXT, 192), ml_dtypes.bfloat16)
    plane[:, 0:EXT] = high
    plane[:, 64 : 64 + EXT] = low
    plane[:, 128 : 128 + EXT] = high
    forward = np.zeros((2, 256, 256))
    inverse = np.zeros((2, 256, 256))
    for gz in range(2):
        own = basis_z[8 : 8 + CZ]
        strip = basis_z[136:144] if gz == 0 else basis_z[0:8]
        face_own, face_far = (135, 136) if gz == 0 else (8, 7)
        forward[gz, :CZ, :EXTZ] = own
        forward[gz, CZ, :EXTZ] = basis_z[face_own] - basis_z[face_far]
        forward[gz, CZ + 2 : CZ + 10, :EXTZ] = strip
        inverse[gz, :EXTZ, :CZ] = own.T
        inverse[gz, :EXTZ, CZ : CZ + 9] = (basis_z[135:144] if gz == 0 else basis_z[0:9]).T

    def stacked(table):
        high, low = two_parts(table)
        return np.concatenate([high, high, low], axis=1)

    denom = np.full((EXT, 256), 1.0)
    denom[:, :EXTZ] = stiff_scale * (eigen[:, None] + eigen_z[None, :]) + mass_term
    return (
        plane,
        stacked(forward),
        stacked(inverse),
        denom.astype(np.float32),
        (stiff_scale * eigen).astype(np.float32),
    )


def roll(value, shift, axis):
    if isinstance(shift, int):
        shift = shift % value.shape[axis]
        return value if shift == 0 else pltpu.roll(value, shift, axis)
    return pltpu.roll(value, lax.rem(shift + 2 * value.shape[axis], value.shape[axis]), axis)


def lanes(rows):
    return lax.broadcasted_iota(jnp.int32, (rows, CZ), 1)


def rows_at(start, size):
    return pl.ds(pl.multiple_of(start, 8), size)


def tile_at(index):
    return rows_at(index * 8, 8)


def call(body, out_rows, *args, scratch=(), limit=16, name=None, smem=(), hbm=(), hbm_out=(), alias=(), work=0):
    place = {**{i: SMEM for i in smem}, **{i: HBM for i in hbm}}
    return pl.pallas_call(
        body,
        out_shape=[jax.ShapeDtypeStruct((rows, CZ), F32) for rows in out_rows],
        in_specs=[place.get(i, VMEM) for i in range(len(args))],
        out_specs=[HBM if i in hbm_out else VMEM for i in range(len(out_rows))],
        input_output_aliases=dict(alias),
        scratch_shapes=list(scratch),
        compiler_params=pltpu.CompilerParams(vmem_limit_bytes=limit * 2**20),
        cost_estimate=pl.CostEstimate(
            flops=int(work * 1e9), bytes_accessed=int(work * 2e6), transcendentals=0
        )
        if work
        else None,
        name=name,
    )(*args)


def strip_base():
    return jnp.where(lax.axis_index("gz") == 0, 118, 126)


def face_lane():
    return jnp.where(lax.axis_index("gz") == 0, 127, 0)


def outer_lane():
    return jnp.where(lax.axis_index("gz") == 0, 0, 127)


CHUNKS = 5


def pair_of(v, h, lane, base, face):
    return jnp.where(lane == base, roll(v, base - face, 1), 0.0) + jnp.where(
        lane == base + 1, roll(h, base + 1 - face, 1), 0.0
    )


def residual_kernel(v_in, h_in, b_in, part_out, up, down, edge, part, v, h, b, sems):
    base, face = strip_base(), face_lane()
    planes = C // CHUNKS
    size = planes * C
    copies = []
    for c in range(CHUNKS):
        at = pl.ds(c * size, size)
        for k, (source, target) in enumerate(((v_in, v), (h_in, h), (b_in, b))):
            copies.append(pltpu.make_async_copy(source.at[at, :], target.at[at, :], sems.at[k, c]))
            copies[-1].start()
    lane, lane8 = lanes(C), lanes(8)
    row = lax.broadcasted_iota(jnp.int32, (C, CZ), 0)
    y_half = jnp.where(row > 0, 0.5, 0.0)
    z_half = jnp.where(lane < CZ - 1, 0.5, 0.0)
    outer = jnp.where(lane == outer_lane(), 0.5, 0.0)

    def visit(x, carry):
        flux_x, pack_up, pack_down = carry
        own = rows_at(x * C, C)
        following = rows_at(jnp.minimum(x + 1, C - 1) * C, C)
        vi, hi = v[own, :], h[own, :]
        next_x = 0.5 * (hi + h[following, :]) * (v[following, :] - vi)
        flux_y = y_half * (hi + roll(hi, 1, 0)) * (vi - roll(vi, 1, 0))
        flux_z = z_half * (hi + roll(hi, -1, 1)) * (roll(vi, -1, 1) - vi)
        applied = (
            mass_term * vi
            - (next_x - flux_x)
            - (roll(flux_y, -1, 0) - flux_y)
            - (flux_z - roll(flux_z, 1, 1))
            + outer * hi * vi
        )
        resid = b[own, :] - applied
        part[own, :] = resid
        down[tile_at(x), :] = resid[0:8]
        up[tile_at(x), :] = resid[32:40]
        pair = pair_of(vi[32:40], hi[32:40], lane8, base, face)
        pack_up = pack_up + roll(pair, 2 * x - base, 1)
        pair = pair_of(vi[0:8], hi[0:8], lane8, base, face)
        pack_down = pack_down + roll(pair, 2 * x - base, 1)
        return next_x, pack_up, pack_down

    carry = (jnp.zeros((C, CZ), F32), jnp.zeros((8, CZ), F32), jnp.zeros((8, CZ), F32))
    for k in range(3):
        copies[k].wait()
    for c in range(CHUNKS):
        if c < CHUNKS - 1:
            for k in range(3):
                copies[3 * (c + 1) + k].wait()
        carry = lax.fori_loop(c * planes, (c + 1) * planes, visit, carry, unroll=4)
        at = pl.ds(c * size, size)
        copies.append(pltpu.make_async_copy(part.at[at, :], part_out.at[at, :], sems.at[3, c]))
        copies[-1].start()
    up[432:440, :] = carry[1]
    down[432:440, :] = carry[2]
    last = (C - 1) * C
    for message, first in ((up, 32), (down, 0)):
        face_row = C - 1 if first else 0
        message[320:360, :] = v[pl.ds(face_row, C, stride=C), :]
        message[360:400, :] = h[pl.ds(face_row, C, stride=C), :]
        message[400:408, :] = v[first : first + 8, :]
        message[408:416, :] = h[first : first + 8, :]
        message[416:424, :] = v[last + first : last + first + 8, :]
        message[424:432, :] = h[last + first : last + first + 8, :]
    edge[0:40, :] = v[0:40, :]
    edge[40:80, :] = h[0:40, :]
    edge[80:120, :] = v[last : last + 40, :]
    edge[120:160, :] = h[last : last + 40, :]
    for copy in copies[-CHUNKS:]:
        copy.wait()


def prepare_kernel(eigen, v, h, denom, out, out_a, out_b):
    base, face = strip_base(), face_lane()
    lane = lanes(C)

    def visit_pair(x, _):
        at = rows_at(x * C, C)
        out[at, :] = pair_of(v[at, :], h[at, :], lane, base, face)
        return 0

    lax.fori_loop(0, C, visit_pair, 0, unroll=8)

    def visit(y, _):
        value = 1.0 / (denom[...] + eigen[y])
        at = rows_at(y * EXT, EXT)
        out_a[at, :] = value[:, :CZ]
        out_b[at, :] = value[:, CZ:]
        return 0

    lax.fori_loop(0, EXT, visit, 0, unroll=4)


def choose(flag, a, b):
    return jnp.where(flag > 0.5, a, b)


def by_parity(flags, first, second):
    def before(start, stop):
        return choose(flags[4], second[start:stop, :], first[start:stop, :])

    def after(start, stop):
        return choose(flags[4], first[start:stop, :], second[start:stop, :])

    return before, after


def pick(pack, index, to):
    pair = lax.div(lanes(8), 2) == index
    return roll(jnp.where(pair, pack, 0.0), to - 2 * index, 1)


def strip_mask():
    lane = lanes(8)
    return jnp.where(lax.axis_index("gz") == 0, lane - 120, 7 - lane) >= 0


def extend_y_kernel(flags, part, vh, up, down, edge, low, high, out, first, second, faces, right, left):
    base, strip_lanes = strip_base(), strip_mask()

    def visit(x, _):
        out[rows_at(x * EXT, 8), :] = low[tile_at(x), :]
        out[rows_at(x * EXT + 8, C), :] = part[rows_at(x * C, C), :]
        out[rows_at(x * EXT + 48, 8), :] = high[tile_at(x), :]
        return 0

    lax.fori_loop(0, C, visit, 0, unroll=8)
    flux = 0.5 * (low[360:400, :] + down[360:400, :]) * (down[320:360, :] - low[320:360, :])
    out[pl.ds(8, C, stride=EXT), :] = out[pl.ds(8, C, stride=EXT), :] - flux
    out[pl.ds(7, C, stride=EXT), :] = out[pl.ds(7, C, stride=EXT), :] + flux * flags[2]
    flux = 0.5 * (up[360:400, :] + high[360:400, :]) * (high[320:360, :] - up[320:360, :])
    out[pl.ds(47, C, stride=EXT), :] = out[pl.ds(47, C, stride=EXT), :] + flux
    out[pl.ds(48, C, stride=EXT), :] = out[pl.ds(48, C, stride=EXT), :] - flux * flags[3]
    for message, start, strip, own in ((left, 0, 400, 0), (right, 32, 416, 80)):
        message[0:448, :] = out[start * EXT : start * EXT + 448, :]
        for k in range(2):
            at = 448 + k * EXT
            message[at : at + 8, :] = low[strip + 8 * k : strip + 8 * k + 8, :]
            message[at + 8 : at + 48, :] = edge[own + 40 * k : own + 40 * k + 40, :]
            message[at + 48 : at + 56, :] = high[strip + 8 * k : strip + 8 * k + 8, :]
        for t in range(TILES):
            near = jnp.zeros((8, CZ), F32)
            taken = jnp.zeros((8, CZ), F32)
            for i in range(OVER):
                x = start + i
                value = jnp.where(strip_lanes, out[x * EXT + 8 * t : x * EXT + 8 * t + 8, :], 0.0)
                if t == 0:
                    taken = taken + pick(low[432:440, :], x, 10 * i)
                elif t == 6:
                    taken = taken + pick(high[432:440, :], x, 10 * i)
                else:
                    value = value + vh[x * C + 8 * t - 8 : x * C + 8 * t, :]
                near = near + roll(value, 10 * i, 1)
            message[560 + 8 * t : 568 + 8 * t, :] = roll(near, -base, 1) + taken
    faces[0:112, :] = left[448:560, :]
    faces[112:224, :] = right[448:560, :]
    first[...] = choose(flags[4], right[...], left[...])
    second[...] = choose(flags[4], left[...], right[...])


def pack_z_kernel(part, vh, low, high, message):
    base, strip_lanes = strip_base(), strip_mask()
    for q in range(BLOCKS_Z):
        for t in range(TILES):
            near = jnp.zeros((8, CZ), F32)
            taken = jnp.zeros((8, CZ), F32)
            for j in range(PER_Z):
                x = q * PER_Z + j - OVER
                if not 0 <= x < C:
                    continue
                value = jnp.where(strip_lanes, part[x * EXT + 8 * t : x * EXT + 8 * t + 8, :], 0.0)
                if t == 0:
                    taken = taken + pick(low[432:440, :], x, 10 * j)
                elif t == 6:
                    taken = taken + pick(high[432:440, :], x, 10 * j)
                else:
                    value = value + vh[x * C + 8 * t - 8 : x * C + 8 * t, :]
                near = near + roll(value, 10 * j, 1)
            at = q * EXT + 8 * t
            message[at : at + 8, :] = roll(near, -base, 1) + taken


def extend_x_kernel(flags, packed, faces, first, second, inner, message, fluxes):
    base, strip_lanes = strip_base(), strip_mask()
    before, after = by_parity(flags, first, second)
    flux_a = 0.5 * (before(504, 560) + faces[56:112, :]) * (faces[0:56, :] - before(448, 504))
    flux_b = 0.5 * (faces[168:224, :] + after(504, 560)) * (after(448, 504) - faces[112:168, :])
    fluxes[0:EXT, :] = flux_a
    fluxes[EXT : 2 * EXT, :] = flux_b
    message[...] = packed[...]
    end = (BLOCKS_Z - 1) * EXT
    message[0:EXT, :] = message[0:EXT, :] + before(560, 616)
    message[end : end + EXT, :] = message[end : end + EXT, :] + after(560, 616)

    def add(x, t, value):
        q, j = divmod(x, PER_Z)
        at = q * EXT + 8 * t
        message[at : at + 8, :] = message[at : at + 8, :] + roll(value, 10 * j, 1)

    for t in range(TILES):
        a = roll(jnp.where(strip_lanes, flux_a[8 * t : 8 * t + 8], 0.0), -base, 1)
        b = roll(jnp.where(strip_lanes, flux_b[8 * t : 8 * t + 8], 0.0), -base, 1)
        add(OVER - 1, t, a * flags[0])
        add(OVER, t, -a)
        add(OVER + C - 1, t, b)
        add(OVER + C, t, -b * flags[1])


def halves(value):
    high = value.astype(BF16)
    return high, (value - high.astype(F32)).astype(BF16)


def dot(a, b):
    return jnp.dot(a, b, preferred_element_type=F32)


def along_lanes(value, table):
    high, low = halves(value)
    return dot(jnp.concatenate([high, low, high], axis=1), table)


def along_rows(table, value):
    padded = jnp.concatenate([value, jnp.zeros((8, value.shape[1]), F32)], axis=0)
    high, low = halves(padded)
    return dot(table, jnp.concatenate([high, high, low], axis=0))


def beside(a, b):
    return jnp.concatenate([a, b], axis=1)


def inner_kernel(plane, part, out):
    table = plane[...]
    for x in range(1, C - 1, 2):
        at, then = pl.ds(x * EXT, EXT), pl.ds((x + 1) * EXT, EXT)
        value = along_rows(table, beside(part[at, :], part[then, :]))
        out[(x - 1) * EXT : x * EXT, :] = value[:, :CZ]
        out[x * EXT : (x + 1) * EXT, :] = value[:, CZ:]


def forward_kernel(flags, plane, part, inner, fluxes, one, two, out, first):
    before, after = by_parity(flags, one, two)
    table = plane[...]
    flux_a, flux_b = fluxes[0:EXT, :], fluxes[EXT : 2 * EXT, :]
    planes = {x: before(x * EXT, (x + 1) * EXT) for x in range(OVER)}
    planes[7] = planes[7] + flux_a * flags[0]
    planes[8] = part[0:EXT, :] - flux_a
    planes[47] = part[(C - 1) * EXT : C * EXT, :] + flux_b
    planes.update({48 + x: after(x * EXT, (x + 1) * EXT) for x in range(OVER)})
    planes[48] = planes[48] - flux_b * flags[1]
    first[9 * EXT : 47 * EXT, :] = inner[...]
    order = sorted(planes)
    for x, then in zip(order[0::2], order[1::2]):
        value = along_rows(table, beside(planes[x], planes[then]))
        first[x * EXT : (x + 1) * EXT, :] = value[:, :CZ]
        first[then * EXT : (then + 1) * EXT, :] = value[:, CZ:]

    def visit_x(c, _):
        for i in range(14):
            y = 2 * (c * 14 + i)
            value = beside(first[pl.ds(y, EXT, stride=EXT), :], first[pl.ds(y + 1, EXT, stride=EXT), :])
            value = along_rows(table, value)
            out[rows_at(y * EXT, EXT), :] = value[:, :CZ]
            out[rows_at((y + 1) * EXT, EXT), :] = value[:, CZ:]
        return 0

    lax.fori_loop(0, 2, visit_x, 0)


def face_terms(own_z, far_z):
    both = own_z[...] + far_z[...]
    half = 0.5 * roll(both, -1, 1)
    return half, half * (far_z[...] - own_z[...])


STEP = 28


def solve_kernel(
    flags, own_z, far_z, main, plane, forward, inverse, scale_a, scale_b,
    second_a, second_b, sol, strip, first, second, halo, right, left,
):
    gz = lax.axis_index("gz")
    table = plane[...]
    _, flux = face_terms(own_z, far_z)
    pack = jnp.where(lax.rem(lanes(ZROWS), 10) == 0, flux, far_z[...])
    blocks = [pack[q * EXT : (q + 1) * EXT] for q in range(BLOCKS_Z)]
    done = []
    for q in range(0, BLOCKS_Z - 1, 2):
        value = along_rows(table, beside(blocks[q], blocks[q + 1]))
        done += [value[:, :CZ], value[:, CZ:]]
    done.append(along_rows(table, blocks[-1]))
    for x in range(EXT):
        q, j = x // PER_Z, x % PER_Z
        halo[x * EXT : (x + 1) * EXT, :] = roll(done[q], -10 * j, 1)

    forward_table = forward[gz]
    inverse_table = inverse[gz]

    def visit(c, _):
        parts = []
        for i in range(0, STEP, 2):
            y = c * STEP + i
            value = beside(halo[pl.ds(y, EXT, stride=EXT), :], halo[pl.ds(y + 1, EXT, stride=EXT), :])
            value = along_rows(table, value)
            parts.append(beside(main[rows_at(y * EXT, EXT), :], value[:, :CZ]))
            parts.append(beside(main[rows_at((y + 1) * EXT, EXT), :], value[:, CZ:]))
        value = along_lanes(jnp.concatenate(parts, axis=0), forward_table)
        at = rows_at(c * STEP * EXT, STEP * EXT)
        value = value * beside(scale_a[at, :], scale_b[at, :])
        for i in range(STEP):
            part = along_rows(table, value[i * EXT : (i + 1) * EXT])
            to = pl.ds(c * STEP + i, EXT, stride=EXT)
            second_a[to, :] = part[:, :CZ]
            second_b[to, :] = part[:, CZ:]
        return 0

    lax.fori_loop(0, EXT // STEP, visit, 0)

    for k, (message, start) in enumerate(((left, 0), (right, 47))):
        inverse_planes(table, inverse_table, second_a, second_b, sol, strip, range(start, start + 9), 9 * k)
        message[0 : 9 * EXT, :] = sol[9 * k * EXT : 9 * (k + 1) * EXT, :]
        tiles = [strip[pl.ds((9 * k * TILES + j) * 8, 8), :] for j in range(63)]
        pack_tiles(message, 9 * EXT, tiles)
    first[...] = choose(flags[4], right[...], left[...])
    second[...] = choose(flags[4], left[...], right[...])


def inverse_planes(table, inverse_table, second_a, second_b, sol, strip, planes, to):
    parts = []
    for x in planes:
        at = pl.ds(x * EXT, EXT)
        parts.append(along_rows(table, beside(second_a[at, :], second_b[at, :])))
    value = along_lanes(jnp.concatenate(parts, axis=0), inverse_table)
    at = pl.ds(to * EXT, len(planes) * EXT)
    sol[at, :] = value[:, :CZ]
    strip[at, :] = value[:, CZ:]


def rest_kernel(plane, inverse, second_a, second_b, sides, side_strip, sol, strip):
    table, inverse_table = plane[...], inverse[lax.axis_index("gz")]
    for first, last in ((9, 19), (19, 29), (29, 38), (38, 47)):
        inverse_planes(
            table, inverse_table, second_a, second_b, sol, strip, range(first, last), first - 7
        )
    for target, source in ((sol, sides), (strip, side_strip)):
        target[0 : 2 * EXT, :] = source[7 * EXT : 9 * EXT, :]
        target[40 * EXT : 42 * EXT, :] = source[9 * EXT : 11 * EXT, :]


def own_kernel(flags, h, low, high, one, two, part, fluxes, own_z, far_z, resid, c_x, c_down, c_up, c_z, c_face, cond):
    face, outer = face_lane(), outer_lane()
    half, flux = face_terms(own_z, far_z)
    half, flux = roll(half, face, 1), roll(flux, face, 1)
    lane8 = lanes(8)
    for x in range(C):
        q, j = (x + OVER) // PER_Z, (x + OVER) % PER_Z
        for t in range(5):
            at = q * EXT + 8 * (t + 1)
            to = x * C + 8 * t
            source = x * EXT + 8 * (t + 1)
            moved = jnp.where(lane8 == face, roll(flux[at : at + 8], -10 * j, 1), 0.0)
            if x == 0:
                moved = moved - fluxes[source : source + 8, :]
            elif x == C - 1:
                moved = moved + fluxes[source + EXT - x * EXT : source + EXT - x * EXT + 8, :]
            resid[to : to + 8, :] = part[source : source + 8, :] + moved
            c_face[to : to + 8, :] = jnp.where(
                lane8 == face, roll(half[at : at + 8], -10 * j, 1), 0.0
            )
    before, after = by_parity(flags, one, two)
    cond[0:C, :] = before(512, 552)
    cond[C : C + C * C, :] = h[...]
    cond[C + C * C :, :] = after(512, 552)
    z_half = jnp.where(lanes(C) < CZ - 1, 0.5, 0.0)
    row = lax.broadcasted_iota(jnp.int32, (C, CZ), 0)
    for x in range(C):
        at = x * C
        hi = h[at : at + C, :]
        c_x[at : at + C, :] = 0.5 * (cond[at : at + C, :] + hi)
        below = jnp.where(row == 0, low[360 + x : 361 + x, :], roll(hi, 1, 0))
        above = jnp.where(row == C - 1, high[360 + x : 361 + x, :], roll(hi, -1, 0))
        c_down[at : at + C, :] = 0.5 * (hi + below)
        c_up[at : at + C, :] = 0.5 * (hi + above)
        c_z[at : at + C, :] = z_half * (hi + roll(hi, -1, 1))
    c_x[C * C :, :] = 0.5 * (cond[C * C : C * C + C, :] + cond[C * C + C :, :])


def pack_tiles(message, at, values):
    for q in range(-(-len(values) // PER)):
        acc = values[q * PER]
        for j, value in enumerate(values[q * PER + 1 : (q + 1) * PER], 1):
            acc = acc + roll(value, 9 * j, 1)
        message[at + 8 * q : at + 8 * q + 8, :] = acc


def unpack_tile(message, at, index):
    q = index // PER
    return roll(message[rows_at(at + 8 * q, 8), :], -9 * (index - q * PER), 1)


def fold_x_kernel(flags, sol, strip, one, two, out, out_strip, up, down, line):
    size = 42 * EXT
    narrow = lanes(8) < 9
    before, after = by_parity(flags, one, two)
    out[0 : 9 * EXT, :] = out[0 : 9 * EXT, :] + before(0, 9 * EXT)
    tail = 33 * EXT
    out[tail:size, :] = out[tail:size, :] + after(0, 9 * EXT)
    packs = [side(9 * EXT, XROWS2) for side in (before, after)]

    for j in range(63):
        q, i = divmod(j, PER)
        for pack, at in ((packs[0], 8 * j), (packs[1], tail + 8 * j)):
            value = jnp.where(narrow, roll(pack[8 * q : 8 * q + 8], -9 * i, 1), 0.0)
            out_strip[at : at + 8, :] = out_strip[at : at + 8, :] + value

    for array in (out, out_strip):
        array[0:EXT, :] = array[0:EXT, :] * flags[0]
        array[41 * EXT : size, :] = array[41 * EXT : size, :] * flags[1]

    for message, tile, single in ((up, 6, 47), (down, 0, 8)):
        for p in range(42):
            message[8 * p : 8 * p + 8, :] = out[p * EXT + 8 * tile : p * EXT + 8 * tile + 8, :]
        message[376:384, :] = jnp.zeros((8, CZ), F32)
        message[336:378, :] = out[pl.ds(single, 42, stride=EXT), :]
        line[40:48, :] = jnp.zeros((8, CZ), F32)
        line[0:42, :] = out_strip[pl.ds(single, 42, stride=EXT), :]
        values = [out_strip[p * EXT + 8 * tile : p * EXT + 8 * tile + 8, :] for p in range(42)]
        values += [line[8 * j : 8 * j + 8, :] for j in range(6)]
        pack_tiles(message, 384, values)


def fold_y_kernel(flags, sol, strip, low, high, resid, out, work, message, line):
    narrow = lanes(8) < 9
    for source, tile, single, flag in ((low, 1, 7, 2), (high, 5, 48, 3)):
        for p in range(42):
            at = p * EXT + 8 * tile
            out[at : at + 8, :] = out[at : at + 8, :] + source[8 * p : 8 * p + 8, :]
            value = jnp.where(narrow, unpack_tile(source, 384, p), 0.0)
            work[at : at + 8, :] = work[at : at + 8, :] + value
        at = pl.ds(single, 42, stride=EXT)
        out[at, :] = (out[at, :] + source[336:378, :]) * flags[flag]
        for j in range(6):
            line[8 * j : 8 * j + 8, :] = jnp.where(narrow, unpack_tile(source, 384, 42 + j), 0.0)
        work[at, :] = (work[at, :] + line[0:42, :]) * flags[flag]
    values = []
    for p in range(42):
        for t in range(1, 6):
            at = p * EXT + 8 * t
            values.append(work[at : at + 8, :])
    for k, single in enumerate((7, 48)):
        line[48 * k + 40 : 48 * k + 48, :] = jnp.zeros((8, CZ), F32)
        line[48 * k : 48 * k + 42, :] = work[pl.ds(single, 42, stride=EXT), :]
        values += [line[48 * k + 8 * j : 48 * k + 8 * j + 8, :] for j in range(6)]
    pack_tiles(message, 0, values)


def apply_kernel(
    sol, own_z, far_z, resid, c_x, c_down, c_up, c_z, c_face, h,
    out, applied, sums, field, pack, line,
):
    gz = lax.axis_index("gz")
    lane = lanes(ZROWS2)
    at_face = lax.rem(lane, 9) == jnp.where(gz == 0, 8, 0)
    shift = jnp.where(gz == 0, 7, 121)
    packed = far_z[...] + jnp.where(at_face, roll(own_z[...], shift, 1), 0.0)
    pack[...] = roll(packed, jnp.where(gz == 0, 120, 127), 1)
    toward = jnp.where(gz == 0, 127, 1)
    lane8 = lanes(8)
    folded = jnp.where(gz == 0, lane8 - 120, 7 - lane8) >= 0

    def tile(index):
        q, j = divmod(index, PER)
        return roll(pack[8 * q : 8 * q + 8, :], -9 * j, 1)

    for p in range(42):
        for t in range(5):
            at = p * EXT + 8 * t + 8
            field[at : at + 8, :] = sol[at : at + 8, :] + jnp.where(folded, tile(p * 5 + t), 0.0)
    for k, single in enumerate((7, 48)):
        for j in range(6):
            line[8 * j : 8 * j + 8, :] = jnp.where(folded, tile(210 + 6 * k + j), 0.0)
        at = pl.ds(single, 42, stride=EXT)
        field[at, :] = sol[at, :] + line[0:42, :]
    pack[...] = roll(pack[...], toward, 1)

    outer = jnp.where(lanes(C) == outer_lane(), 0.5, 0.0)
    flux_x = c_x[0:C, :] * (field[EXT + 8 : EXT + 48, :] - field[8:48, :])
    sum_a = jnp.zeros((8, CZ), F32)
    sum_b = jnp.zeros((8, CZ), F32)
    def visit(x, carry):
        flux_x, sum_a, sum_b = carry
        at = (x + 1) * EXT
        to = rows_at(x * C, C)
        z = field[rows_at(at + 8, C), :]
        next_x = c_x[rows_at(x * C + C, C), :] * (field[rows_at(at + EXT + 8, C), :] - z)
        net = next_x - flux_x
        net = net + c_up[to, :] * (field[pl.ds(at + 9, C), :] - z)
        net = net - c_down[to, :] * (z - field[pl.ds(at + 7, C), :])
        flux_z = c_z[to, :] * (roll(z, -1, 1) - z)
        net = net + (flux_z - roll(flux_z, 1, 1)) + c_face[to, :] * (out[to, :] - z)
        image = mass_term * z - net + outer * h[to, :] * z
        out[to, :] = z
        applied[to, :] = image
        a, b = resid[to, :] * z, z * image
        for t in range(5):
            sum_a = sum_a + a[8 * t : 8 * t + 8]
            sum_b = sum_b + b[8 * t : 8 * t + 8]
        return next_x, sum_a, sum_b

    for x in range(C):
        for t in range(5):
            out[x * C + 8 * t : x * C + 8 * t + 8, :] = tile((x + 1) * 5 + t)
    _, sum_a, sum_b = lax.fori_loop(0, C, visit, (flux_x, sum_a, sum_b), unroll=8)
    total_a = jnp.sum(sum_a, axis=0, keepdims=True)
    total_b = jnp.sum(sum_b, axis=0, keepdims=True)
    total_a = total_a + roll(total_a, CZ // 2, 1)
    total_b = total_b + roll(total_b, CZ // 2, 1)
    total = jnp.where(lanes(1) < CZ // 2, total_a, total_b)
    sums[...] = jnp.broadcast_to(total, sums.shape)


def gather_kernel(sums, out):
    out[...] = jnp.broadcast_to(jnp.sum(sums[...], axis=0, keepdims=True), out.shape)


def update_kernel(sums, guess, resid, field, applied, solution_out, resid_out):
    total = jnp.sum(sums[...], axis=0, keepdims=True)
    first = lanes(1) < CZ // 2
    above = jnp.sum(jnp.where(first, total, 0.0), axis=1, keepdims=True)
    below = jnp.sum(jnp.where(first, 0.0, total), axis=1, keepdims=True)
    step = above / below
    solution_out[...] = guess[...] + step * field[...]
    resid_out[...] = resid[...] - step * applied[...]


def on_device(gx, splits, right_side, guess_field, conduct_field):
    shape = right_side.shape
    b, v, h = (a.reshape(C * C, CZ) for a in (right_side, guess_field, conduct_field))
    n_gx, n_gy = lax.axis_size(gx), lax.axis_size("gy")
    at_x, at_y = lax.axis_index(gx), lax.axis_index("gy")
    flags = jnp.stack([at_x > 0, at_x < n_gx - 1, at_y > 0, at_y < n_gy - 1, at_x % 2 == 1]).astype(F32)

    def exchange(axis, up, down):
        n = lax.axis_size(axis)
        forward = [(i, i + 1) for i in range(n - 1)]
        backward = [(i + 1, i) for i in range(n - 1)]
        return lax.ppermute(up, axis, forward), lax.ppermute(down, axis, backward)

    def exchange_x(first, second):
        pairs = [[(i + k, i + 1 - k) for i in range(start, n_gx - 1, 2) for k in (0, 1)] for start in (1, 0)]
        return lax.ppermute(first, gx, pairs[0]), lax.ppermute(second, gx, pairs[1])

    def swap(value):
        return lax.ppermute(value, "gz", [(0, 1), (1, 0)])

    plane, forward, inverse, denom, eigen = tables()
    own = C * C
    box = EXT * EXT

    def buffer(rows):
        return pltpu.VMEM((rows, CZ), F32)

    part, up, down, edge = call(
        residual_kernel, (own, YROWS, YROWS, 160), v, h, b,
        scratch=[buffer(own)] * 4 + [pltpu.SemaphoreType.DMA((4, CHUNKS))],
        hbm=(0, 1, 2), hbm_out=(0,), limit=56, name="residual", work=2,
    )
    low, high = exchange("gy", up, down)
    pairs, scale_a, scale_b = call(
        prepare_kernel, (own, box, box), eigen, v, h, denom, smem=(0,), name="prepare", work=2
    )
    part, right, left, faces = call(
        extend_y_kernel, (C * EXT, XROWS, XROWS, 4 * EXT),
        flags, part, pairs, up, down, edge, low, high,
        scratch=[buffer(XROWS)] * 2, smem=(0,), name="extend_y", work=1,
    )
    one, two = exchange_x(right, left)
    (packed,) = call(pack_z_kernel, (ZROWS,), part, pairs, low, high, name="pack_z", work=2)
    (inner,) = call(inner_kernel, (38 * EXT,), plane, part, name="inner", work=1)
    own_z, fluxes = call(
        extend_x_kernel, (ZROWS, 2 * EXT), flags, packed, faces, one, two, inner,
        smem=(0,), name="extend_x", work=1,
    )
    far_z = swap(own_z)
    (main,) = call(
        forward_kernel, (box,), flags, plane, part, inner, fluxes, one, two,
        scratch=[buffer(box)], smem=(0,), name="forward", work=2,
    )
    second_a, second_b, sides, side_strip, right, left = call(
        solve_kernel, (box, box, 18 * EXT, 18 * EXT, XROWS2, XROWS2),
        flags, own_z, far_z, main, plane, forward, inverse, scale_a, scale_b,
        scratch=[buffer(box), buffer(XROWS2), buffer(XROWS2)], smem=(0,), name="solve", work=6,
    )
    resid, c_x, c_down, c_up, c_z, c_face = call(
        own_kernel, (own, own + C, own, own, own, own),
        flags, h, low, high, one, two, part, fluxes, own_z, far_z,
        scratch=[buffer(own + 2 * C)], smem=(0,), name="own", work=2,
    )
    one, two = exchange_x(right, left)
    sol, strip = call(
        rest_kernel, (42 * EXT, 42 * EXT),
        plane, inverse, second_a, second_b, sides, side_strip, name="rest", work=2,
    )
    sol, strip, up, down = call(
        fold_x_kernel, (42 * EXT, 42 * EXT, YROWS2, YROWS2),
        flags, sol, strip, one, two,
        scratch=[buffer(48)], smem=(0,), alias={1: 0, 2: 1}, name="fold_x", work=1,
    )
    low, high = exchange("gy", up, down)
    sol, _, own_z = call(
        fold_y_kernel, (42 * EXT, 42 * EXT, ZROWS2),
        flags, sol, strip, low, high, resid,
        scratch=[buffer(96)], smem=(0,), alias={1: 0, 2: 1}, name="fold_y", work=1,
    )
    far_z = swap(own_z)
    first, last = splits
    field, applied, sums = call(
        apply_kernel, (own, own, lax.axis_size(first)),
        sol, own_z, far_z, resid, c_x, c_down, c_up, c_z, c_face, h,
        scratch=[buffer(42 * EXT), buffer(ZROWS2), buffer(48)], name="apply", work=3,
    )
    sums = lax.all_to_all(sums, first, 0, 0, tiled=True)
    (sums,) = call(gather_kernel, (lax.axis_size(last),), sums, name="gather")
    sums = lax.all_to_all(sums, last, 0, 0, tiled=True)
    out, resid = call(update_kernel, (own, own), sums, v, resid, field, applied, name="update", work=2)
    return out.reshape(shape), resid.reshape(shape)


def solution(mesh):
    n_gx, n_gy, n_gz = mesh.devices.shape
    if n_gx == 64:
        mesh = Mesh(mesh.devices.reshape(4, 8, 2, n_gy, n_gz), ("gx_x", "gx_y", "gx_c", "gy", "gz"))
        gx = ("gx_x", "gx_y", "gx_c")
        splits = (("gx_x", "gx_y"), ("gx_c", "gy", "gz"))
    else:
        gx = "gx"
        splits = (("gx",), ("gy", "gz"))
    placed = P(gx, "gy", "gz")
    return jax.shard_map(
        functools.partial(on_device, gx, splits),
        mesh=mesh,
        in_specs=(placed,) * 3,
        out_specs=(placed,) * 2,
        check_vma=False,
    )
```

```python
import functools

import jax
import jax.numpy as jnp
import ml_dtypes
import numpy as np
from jax import lax
from jax.experimental import pallas as pl
from jax.experimental.pallas import tpu as pltpu
from jax.sharding import Mesh
from jax.sharding import PartitionSpec as P

OVER = 8
C = 40
CZ = 128
EXT = C + 2 * OVER
EXTZ = CZ + 2 * OVER
TILES = EXT // 8
stiff_scale = 3.0
mass_term = 0.001

F32 = jnp.float32
BF16 = jnp.bfloat16
VMEM = pl.BlockSpec(memory_space=pltpu.VMEM)
SMEM = pl.BlockSpec(memory_space=pltpu.SMEM)
HBM = pl.BlockSpec(memory_space=pltpu.HBM)

YROWS = 440
XROWS = 616
PER_Z = 12
BLOCKS_Z = -(-EXT // PER_Z)
ZROWS = BLOCKS_Z * EXT
PER = 14
XROWS2 = 9 * EXT + 40
YROWS2 = 416
ZGROUPS2 = 42 * 5 + 12
ZROWS2 = 8 * -(-ZGROUPS2 // PER)


def sine_table(count):
    k = np.arange(1, count + 1)
    basis = np.sqrt(2.0 / (count + 1)) * np.sin(np.pi * k[:, None] * k[None, :] / (count + 1))
    eigen = 2.0 - 2.0 * np.cos(np.pi * k / (count + 1))
    return basis, eigen


def two_parts(table):
    high = table.astype(ml_dtypes.bfloat16)
    low = (table - high.astype(np.float64)).astype(ml_dtypes.bfloat16)
    return high, low


@functools.cache
def tables():
    basis, eigen = sine_table(EXT)
    basis_z, eigen_z = sine_table(EXTZ)
    high, low = two_parts(basis)
    plane = np.zeros((EXT, 192), ml_dtypes.bfloat16)
    plane[:, 0:EXT] = high
    plane[:, 64 : 64 + EXT] = low
    plane[:, 128 : 128 + EXT] = high
    forward = np.zeros((2, 256, 256))
    inverse = np.zeros((2, 256, 256))
    for gz in range(2):
        own = basis_z[8 : 8 + CZ]
        strip = basis_z[136:144] if gz == 0 else basis_z[0:8]
        face_own, face_far = (135, 136) if gz == 0 else (8, 7)
        forward[gz, :CZ, :EXTZ] = own
        forward[gz, CZ, :EXTZ] = basis_z[face_own] - basis_z[face_far]
        forward[gz, CZ + 2 : CZ + 10, :EXTZ] = strip
        inverse[gz, :EXTZ, :CZ] = own.T
        inverse[gz, :EXTZ, CZ : CZ + 9] = (basis_z[135:144] if gz == 0 else basis_z[0:9]).T

    def stacked(table):
        high, low = two_parts(table)
        return np.concatenate([high, high, low], axis=1)

    denom = np.full((EXT, 256), 1.0)
    denom[:, :EXTZ] = stiff_scale * (eigen[:, None] + eigen_z[None, :]) + mass_term
    return (
        plane,
        stacked(forward),
        stacked(inverse),
        denom.astype(np.float32),
        (stiff_scale * eigen).astype(np.float32),
    )


def roll(value, shift, axis):
    if isinstance(shift, int):
        shift = shift % value.shape[axis]
        return value if shift == 0 else pltpu.roll(value, shift, axis)
    return pltpu.roll(value, lax.rem(shift + 2 * value.shape[axis], value.shape[axis]), axis)


def lanes(rows):
    return lax.broadcasted_iota(jnp.int32, (rows, CZ), 1)


def rows_at(start, size):
    return pl.ds(pl.multiple_of(start, 8), size)


def tile_at(index):
    return rows_at(index * 8, 8)


def call(body, out_rows, *args, scratch=(), limit=16, name=None, smem=(), hbm=(), hbm_out=(), alias=(), work=0):
    place = {**{i: SMEM for i in smem}, **{i: HBM for i in hbm}}
    return pl.pallas_call(
        body,
        out_shape=[jax.ShapeDtypeStruct((rows, CZ), F32) for rows in out_rows],
        in_specs=[place.get(i, VMEM) for i in range(len(args))],
        out_specs=[HBM if i in hbm_out else VMEM for i in range(len(out_rows))],
        input_output_aliases=dict(alias),
        scratch_shapes=list(scratch),
        compiler_params=pltpu.CompilerParams(vmem_limit_bytes=limit * 2**20),
        cost_estimate=pl.CostEstimate(
            flops=int(work * 1e9), bytes_accessed=int(work * 2e6), transcendentals=0
        )
        if work
        else None,
        name=name,
    )(*args)


def strip_base():
    return jnp.where(lax.axis_index("gz") == 0, 118, 126)


def face_lane():
    return jnp.where(lax.axis_index("gz") == 0, 127, 0)


def outer_lane():
    return jnp.where(lax.axis_index("gz") == 0, 0, 127)


def pair_of(v, h, lane, base, face):
    return jnp.where(lane == base, roll(v, base - face, 1), 0.0) + jnp.where(
        lane == base + 1, roll(h, base + 1 - face, 1), 0.0
    )


def strips_kernel(v_in, h_in, b_in, up, down, v, h, b, sems):
    copies = []
    for k, (source, target, size) in enumerate(((v_in, v, 16), (h_in, h, 16), (b_in, b, 8))):
        for side, first in enumerate((0, C - size)):
            at = pl.ds(first, size)
            copies.append(
                pltpu.make_async_copy(source.at[:, at, :], target.at[:, at, :], sems.at[k, side])
            )
            copies[-1].start()
    base, face = strip_base(), face_lane()
    lane = lanes(8)
    row = lax.broadcasted_iota(jnp.int32, (8, CZ), 0)
    z_half = jnp.where(lane < CZ - 1, 0.5, 0.0)
    outer = jnp.where(lane == outer_lane(), 0.5, 0.0)
    last = C - 1
    for copy in copies:
        copy.wait()

    def tile(x, start, beyond, sign, flux_x):
        following = jnp.minimum(x + 1, last)
        at, to = pl.ds(start, 8), pl.ds(beyond, 8)
        vi, hi = v[x, at, :], h[x, at, :]
        next_x = 0.5 * (hi + h[following, at, :]) * (v[following, at, :] - vi)
        flux_y = 0.5 * (hi + h[x, to, :]) * (v[x, to, :] - vi)
        edge = 0 if sign > 0 else 7
        net_y = flux_y - jnp.where(row == edge, 0.0, roll(flux_y, sign, 0))
        flux_z = z_half * (hi + roll(hi, -1, 1)) * (roll(vi, -1, 1) - vi)
        applied = (
            mass_term * vi
            - (next_x - flux_x)
            - net_y
            - (flux_z - roll(flux_z, 1, 1))
            + outer * hi * vi
        )
        return b[x, at, :] - applied, next_x, vi, hi

    def visit(x, carry):
        flux_up, flux_down, pack_up, pack_down = carry
        resid, flux_down, vi, hi = tile(x, 0, 1, 1, flux_down)
        down[tile_at(x), :] = resid
        down[pl.ds(320 + x, 1), :] = vi[0:1]
        down[pl.ds(360 + x, 1), :] = hi[0:1]
        pack_down = pack_down + roll(pair_of(vi, hi, lane, base, face), 2 * x - base, 1)
        resid, flux_up, vi, hi = tile(x, 32, 31, -1, flux_up)
        up[tile_at(x), :] = resid
        up[pl.ds(320 + x, 1), :] = vi[7:8]
        up[pl.ds(360 + x, 1), :] = hi[7:8]
        pack_up = pack_up + roll(pair_of(vi, hi, lane, base, face), 2 * x - base, 1)
        return flux_up, flux_down, pack_up, pack_down

    zero = jnp.zeros((8, CZ), F32)
    _, _, pack_up, pack_down = lax.fori_loop(0, C, visit, (zero,) * 4, unroll=8)
    up[432:440, :] = pack_up
    down[432:440, :] = pack_down
    for message, first in ((up, 32), (down, 0)):
        at = pl.ds(first, 8)
        message[400:408, :] = v[0, at, :]
        message[408:416, :] = h[0, at, :]
        message[416:424, :] = v[last, at, :]
        message[424:432, :] = h[last, at, :]


def residual_kernel(v, h, b, part, edge):
    lane = lanes(C)
    row = lax.broadcasted_iota(jnp.int32, (C, CZ), 0)
    y_half = jnp.where(row > 0, 0.5, 0.0)
    z_half = jnp.where(lane < CZ - 1, 0.5, 0.0)
    outer = jnp.where(lane == outer_lane(), 0.5, 0.0)

    def visit(x, flux_x):
        own = rows_at(x * C, C)
        following = rows_at(jnp.minimum(x + 1, C - 1) * C, C)
        vi, hi = v[own, :], h[own, :]
        next_x = 0.5 * (hi + h[following, :]) * (v[following, :] - vi)
        flux_y = y_half * (hi + roll(hi, 1, 0)) * (vi - roll(vi, 1, 0))
        flux_z = z_half * (hi + roll(hi, -1, 1)) * (roll(vi, -1, 1) - vi)
        applied = (
            mass_term * vi
            - (next_x - flux_x)
            - (roll(flux_y, -1, 0) - flux_y)
            - (flux_z - roll(flux_z, 1, 1))
            + outer * hi * vi
        )
        part[own, :] = b[own, :] - applied
        return next_x

    lax.fori_loop(0, C, visit, jnp.zeros((C, CZ), F32), unroll=4)
    last = (C - 1) * C
    edge[0:40, :] = v[0:40, :]
    edge[40:80, :] = h[0:40, :]
    edge[80:120, :] = v[last : last + 40, :]
    edge[120:160, :] = h[last : last + 40, :]


def prepare_kernel(eigen, v, h, denom, out, out_a, out_b):
    base, face = strip_base(), face_lane()
    lane = lanes(C)

    def visit_pair(x, _):
        at = rows_at(x * C, C)
        out[at, :] = pair_of(v[at, :], h[at, :], lane, base, face)
        return 0

    lax.fori_loop(0, C, visit_pair, 0, unroll=8)

    def visit(y, _):
        value = 1.0 / (denom[...] + eigen[y])
        at = rows_at(y * EXT, EXT)
        out_a[at, :] = value[:, :CZ]
        out_b[at, :] = value[:, CZ:]
        return 0

    lax.fori_loop(0, EXT, visit, 0, unroll=4)


def choose(flag, a, b):
    return jnp.where(flag > 0.5, a, b)


def by_parity(flags, first, second):
    def before(start, stop):
        return choose(flags[4], second[start:stop, :], first[start:stop, :])

    def after(start, stop):
        return choose(flags[4], first[start:stop, :], second[start:stop, :])

    return before, after


def pick(pack, index, to):
    pair = lax.div(lanes(8), 2) == index
    return roll(jnp.where(pair, pack, 0.0), to - 2 * index, 1)


def strip_mask():
    lane = lanes(8)
    return jnp.where(lax.axis_index("gz") == 0, lane - 120, 7 - lane) >= 0


def y_fluxes(up, down, low, high):
    flux_a = 0.5 * (low[360:400, :] + down[360:400, :]) * (down[320:360, :] - low[320:360, :])
    flux_b = 0.5 * (up[360:400, :] + high[360:400, :]) * (high[320:360, :] - up[320:360, :])
    return flux_a, flux_b


def extend_y(flags, fluxes, part, low, high, out, start, stop):
    for x in range(start, stop):
        at = (x - start) * EXT
        out[at : at + 8, :] = low[8 * x : 8 * x + 8, :]
        out[at + 8 : at + 48, :] = part[x * C : x * C + C, :]
        out[at + 48 : at + 56, :] = high[8 * x : 8 * x + 8, :]
    flux_a, flux_b = (flux[start:stop] for flux in fluxes)
    for row, value in ((8, -flux_a), (7, flux_a * flags[2]), (47, flux_b), (48, -flux_b * flags[3])):
        at = pl.ds(row, stop - start, stride=EXT)
        out[at, :] = out[at, :] + value


def extend_y_kernel(flags, part, vh, up, down, edge, low, high, first, second, faces, right, left):
    base, strip_lanes = strip_base(), strip_mask()
    fluxes = y_fluxes(up, down, low, high)
    for message, start, strip, own in ((left, 0, 400, 0), (right, 32, 416, 80)):
        extend_y(flags, fluxes, part, low, high, message, start, start + OVER)
        for k in range(2):
            at = 448 + k * EXT
            message[at : at + 8, :] = low[strip + 8 * k : strip + 8 * k + 8, :]
            message[at + 8 : at + 48, :] = edge[own + 40 * k : own + 40 * k + 40, :]
            message[at + 48 : at + 56, :] = high[strip + 8 * k : strip + 8 * k + 8, :]
        for t in range(TILES):
            near = jnp.zeros((8, CZ), F32)
            taken = jnp.zeros((8, CZ), F32)
            for i in range(OVER):
                x = start + i
                at = i * EXT + 8 * t
                value = jnp.where(strip_lanes, message[at : at + 8, :], 0.0)
                if t == 0:
                    taken = taken + pick(low[432:440, :], x, 10 * i)
                elif t == 6:
                    taken = taken + pick(high[432:440, :], x, 10 * i)
                else:
                    value = value + vh[x * C + 8 * t - 8 : x * C + 8 * t, :]
                near = near + roll(value, 10 * i, 1)
            message[560 + 8 * t : 568 + 8 * t, :] = roll(near, -base, 1) + taken
    faces[0:112, :] = left[448:560, :]
    faces[112:224, :] = right[448:560, :]
    first[...] = choose(flags[4], right[...], left[...])
    second[...] = choose(flags[4], left[...], right[...])


def pack_z_kernel(part, vh, low, high, message):
    base, strip_lanes = strip_base(), strip_mask()
    for q in range(BLOCKS_Z):
        for t in range(TILES):
            near = jnp.zeros((8, CZ), F32)
            taken = jnp.zeros((8, CZ), F32)
            for j in range(PER_Z):
                x = q * PER_Z + j - OVER
                if not 0 <= x < C:
                    continue
                value = jnp.where(strip_lanes, part[x * EXT + 8 * t : x * EXT + 8 * t + 8, :], 0.0)
                if t == 0:
                    taken = taken + pick(low[432:440, :], x, 10 * j)
                elif t == 6:
                    taken = taken + pick(high[432:440, :], x, 10 * j)
                else:
                    value = value + vh[x * C + 8 * t - 8 : x * C + 8 * t, :]
                near = near + roll(value, 10 * j, 1)
            at = q * EXT + 8 * t
            message[at : at + 8, :] = roll(near, -base, 1) + taken


def extend_x_kernel(flags, packed, faces, first, second, inner, message, fluxes):
    base, strip_lanes = strip_base(), strip_mask()
    before, after = by_parity(flags, first, second)
    flux_a = 0.5 * (before(504, 560) + faces[56:112, :]) * (faces[0:56, :] - before(448, 504))
    flux_b = 0.5 * (faces[168:224, :] + after(504, 560)) * (after(448, 504) - faces[112:168, :])
    fluxes[0:EXT, :] = flux_a
    fluxes[EXT : 2 * EXT, :] = flux_b
    message[...] = packed[...]
    end = (BLOCKS_Z - 1) * EXT
    message[0:EXT, :] = message[0:EXT, :] + before(560, 616)
    message[end : end + EXT, :] = message[end : end + EXT, :] + after(560, 616)

    def add(x, t, value):
        q, j = divmod(x, PER_Z)
        at = q * EXT + 8 * t
        message[at : at + 8, :] = message[at : at + 8, :] + roll(value, 10 * j, 1)

    for t in range(TILES):
        a = roll(jnp.where(strip_lanes, flux_a[8 * t : 8 * t + 8], 0.0), -base, 1)
        b = roll(jnp.where(strip_lanes, flux_b[8 * t : 8 * t + 8], 0.0), -base, 1)
        add(OVER - 1, t, a * flags[0])
        add(OVER, t, -a)
        add(OVER + C - 1, t, b)
        add(OVER + C, t, -b * flags[1])


def halves(value):
    high = value.astype(BF16)
    return high, (value - high.astype(F32)).astype(BF16)


def dot(a, b):
    return jnp.dot(a, b, preferred_element_type=F32)


def along_lanes(value, table):
    high, low = halves(value)
    return dot(jnp.concatenate([high, low, high], axis=1), table)


def along_rows(table, value):
    padded = jnp.concatenate([value, jnp.zeros((8, value.shape[1]), F32)], axis=0)
    high, low = halves(padded)
    return dot(table, jnp.concatenate([high, high, low], axis=0))


def beside(a, b):
    return jnp.concatenate([a, b], axis=1)


def inner_kernel(flags, plane, box, up, down, low, high, out, part):
    table = plane[...]
    extend_y(flags, y_fluxes(up, down, low, high), box, low, high, part, 0, C)
    for x in range(1, C - 1, 2):
        at, then = pl.ds(x * EXT, EXT), pl.ds((x + 1) * EXT, EXT)
        value = along_rows(table, beside(part[at, :], part[then, :]))
        out[(x - 1) * EXT : x * EXT, :] = value[:, :CZ]
        out[x * EXT : (x + 1) * EXT, :] = value[:, CZ:]


def forward_kernel(flags, plane, part, inner, fluxes, one, two, out, first):
    before, after = by_parity(flags, one, two)
    table = plane[...]
    flux_a, flux_b = fluxes[0:EXT, :], fluxes[EXT : 2 * EXT, :]
    planes = {x: before(x * EXT, (x + 1) * EXT) for x in range(OVER)}
    planes[7] = planes[7] + flux_a * flags[0]
    planes[8] = part[0:EXT, :] - flux_a
    planes[47] = part[(C - 1) * EXT : C * EXT, :] + flux_b
    planes.update({48 + x: after(x * EXT, (x + 1) * EXT) for x in range(OVER)})
    planes[48] = planes[48] - flux_b * flags[1]
    first[9 * EXT : 47 * EXT, :] = inner[...]
    order = sorted(planes)
    for x, then in zip(order[0::2], order[1::2]):
        value = along_rows(table, beside(planes[x], planes[then]))
        first[x * EXT : (x + 1) * EXT, :] = value[:, :CZ]
        first[then * EXT : (then + 1) * EXT, :] = value[:, CZ:]

    def visit_x(c, _):
        for i in range(14):
            y = 2 * (c * 14 + i)
            value = beside(first[pl.ds(y, EXT, stride=EXT), :], first[pl.ds(y + 1, EXT, stride=EXT), :])
            value = along_rows(table, value)
            out[rows_at(y * EXT, EXT), :] = value[:, :CZ]
            out[rows_at((y + 1) * EXT, EXT), :] = value[:, CZ:]
        return 0

    lax.fori_loop(0, 2, visit_x, 0)


def face_terms(own_z, far_z):
    both = own_z[...] + far_z[...]
    half = 0.5 * roll(both, -1, 1)
    return half, half * (far_z[...] - own_z[...])


STEP = 28


def solve_kernel(
    flags, own_z, far_z, main, plane, forward, inverse, scale_a, scale_b,
    second_a, second_b, sol, strip, first, second, halo, right, left,
):
    gz = lax.axis_index("gz")
    table = plane[...]
    _, flux = face_terms(own_z, far_z)
    pack = jnp.where(lax.rem(lanes(ZROWS), 10) == 0, flux, far_z[...])
    blocks = [pack[q * EXT : (q + 1) * EXT] for q in range(BLOCKS_Z)]
    done = []
    for q in range(0, BLOCKS_Z - 1, 2):
        value = along_rows(table, beside(blocks[q], blocks[q + 1]))
        done += [value[:, :CZ], value[:, CZ:]]
    done.append(along_rows(table, blocks[-1]))
    for x in range(EXT):
        q, j = x // PER_Z, x % PER_Z
        halo[x * EXT : (x + 1) * EXT, :] = roll(done[q], -10 * j, 1)

    forward_table = forward[gz]
    inverse_table = inverse[gz]

    def visit(c, _):
        parts = []
        for i in range(0, STEP, 2):
            y = c * STEP + i
            value = beside(halo[pl.ds(y, EXT, stride=EXT), :], halo[pl.ds(y + 1, EXT, stride=EXT), :])
            value = along_rows(table, value)
            parts.append(beside(main[rows_at(y * EXT, EXT), :], value[:, :CZ]))
            parts.append(beside(main[rows_at((y + 1) * EXT, EXT), :], value[:, CZ:]))
        value = along_lanes(jnp.concatenate(parts, axis=0), forward_table)
        at = rows_at(c * STEP * EXT, STEP * EXT)
        value = value * beside(scale_a[at, :], scale_b[at, :])
        for i in range(STEP):
            part = along_rows(table, value[i * EXT : (i + 1) * EXT])
            to = pl.ds(c * STEP + i, EXT, stride=EXT)
            second_a[to, :] = part[:, :CZ]
            second_b[to, :] = part[:, CZ:]
        return 0

    lax.fori_loop(0, EXT // STEP, visit, 0)

    for k, (message, start) in enumerate(((left, 0), (right, 47))):
        inverse_planes(table, inverse_table, second_a, second_b, sol, strip, range(start, start + 9), 9 * k)
        message[0 : 9 * EXT, :] = sol[9 * k * EXT : 9 * (k + 1) * EXT, :]
        tiles = [strip[pl.ds((9 * k * TILES + j) * 8, 8), :] for j in range(63)]
        pack_tiles(message, 9 * EXT, tiles)
    first[...] = choose(flags[4], right[...], left[...])
    second[...] = choose(flags[4], left[...], right[...])


def inverse_planes(table, inverse_table, second_a, second_b, sol, strip, planes, to):
    parts = []
    for x in planes:
        at = pl.ds(x * EXT, EXT)
        parts.append(along_rows(table, beside(second_a[at, :], second_b[at, :])))
    value = along_lanes(jnp.concatenate(parts, axis=0), inverse_table)
    at = pl.ds(to * EXT, len(planes) * EXT)
    sol[at, :] = value[:, :CZ]
    strip[at, :] = value[:, CZ:]


def rest_kernel(plane, inverse, second_a, second_b, sides, side_strip, sol, strip):
    table, inverse_table = plane[...], inverse[lax.axis_index("gz")]
    for first, last in ((9, 19), (19, 29), (29, 38), (38, 47)):
        inverse_planes(
            table, inverse_table, second_a, second_b, sol, strip, range(first, last), first - 7
        )
    for target, source in ((sol, sides), (strip, side_strip)):
        target[0 : 2 * EXT, :] = source[7 * EXT : 9 * EXT, :]
        target[40 * EXT : 42 * EXT, :] = source[9 * EXT : 11 * EXT, :]


def own_kernel(flags, h, low, high, one, two, part, fluxes, own_z, far_z, resid, c_x, c_down, c_up, c_z, c_face, cond):
    face, outer = face_lane(), outer_lane()
    half, flux = face_terms(own_z, far_z)
    half, flux = roll(half, face, 1), roll(flux, face, 1)
    lane8 = lanes(8)
    for x in range(C):
        q, j = (x + OVER) // PER_Z, (x + OVER) % PER_Z
        for t in range(5):
            at = q * EXT + 8 * (t + 1)
            to = x * C + 8 * t
            source = x * EXT + 8 * (t + 1)
            moved = jnp.where(lane8 == face, roll(flux[at : at + 8], -10 * j, 1), 0.0)
            if x == 0:
                moved = moved - fluxes[source : source + 8, :]
            elif x == C - 1:
                moved = moved + fluxes[source + EXT - x * EXT : source + EXT - x * EXT + 8, :]
            resid[to : to + 8, :] = part[source : source + 8, :] + moved
            c_face[to : to + 8, :] = jnp.where(
                lane8 == face, roll(half[at : at + 8], -10 * j, 1), 0.0
            )
    before, after = by_parity(flags, one, two)
    cond[0:C, :] = before(512, 552)
    cond[C : C + C * C, :] = h[...]
    cond[C + C * C :, :] = after(512, 552)
    z_half = jnp.where(lanes(C) < CZ - 1, 0.5, 0.0)
    row = lax.broadcasted_iota(jnp.int32, (C, CZ), 0)
    for x in range(C):
        at = x * C
        hi = h[at : at + C, :]
        c_x[at : at + C, :] = 0.5 * (cond[at : at + C, :] + hi)
        below = jnp.where(row == 0, low[360 + x : 361 + x, :], roll(hi, 1, 0))
        above = jnp.where(row == C - 1, high[360 + x : 361 + x, :], roll(hi, -1, 0))
        c_down[at : at + C, :] = 0.5 * (hi + below)
        c_up[at : at + C, :] = 0.5 * (hi + above)
        c_z[at : at + C, :] = z_half * (hi + roll(hi, -1, 1))
    c_x[C * C :, :] = 0.5 * (cond[C * C : C * C + C, :] + cond[C * C + C :, :])


def pack_tiles(message, at, values):
    for q in range(-(-len(values) // PER)):
        acc = values[q * PER]
        for j, value in enumerate(values[q * PER + 1 : (q + 1) * PER], 1):
            acc = acc + roll(value, 9 * j, 1)
        message[at + 8 * q : at + 8 * q + 8, :] = acc


def unpack_tile(message, at, index):
    q = index // PER
    return roll(message[rows_at(at + 8 * q, 8), :], -9 * (index - q * PER), 1)


def fold_x_kernel(
    flags, sol, strip, one, two, _, out, out_strip, up, down, across, across_up, across_down, line
):
    size = 42 * EXT
    narrow = lanes(8) < 9
    before, after = by_parity(flags, one, two)
    out[0 : 9 * EXT, :] = out[0 : 9 * EXT, :] + before(0, 9 * EXT)
    tail = 33 * EXT
    out[tail:size, :] = out[tail:size, :] + after(0, 9 * EXT)
    packs = [side(9 * EXT, XROWS2) for side in (before, after)]

    for j in range(63):
        q, i = divmod(j, PER)
        for pack, at in ((packs[0], 8 * j), (packs[1], tail + 8 * j)):
            value = jnp.where(narrow, roll(pack[8 * q : 8 * q + 8], -9 * i, 1), 0.0)
            out_strip[at : at + 8, :] = out_strip[at : at + 8, :] + value

    for array in (out, out_strip):
        array[0:EXT, :] = array[0:EXT, :] * flags[0]
        array[41 * EXT : size, :] = array[41 * EXT : size, :] * flags[1]

    for message, tile, single in ((up, 6, 47), (down, 0, 8)):
        for p in range(42):
            message[8 * p : 8 * p + 8, :] = out[p * EXT + 8 * tile : p * EXT + 8 * tile + 8, :]
        message[376:384, :] = jnp.zeros((8, CZ), F32)
        message[336:378, :] = out[pl.ds(single, 42, stride=EXT), :]
        line[40:48, :] = jnp.zeros((8, CZ), F32)
        line[0:42, :] = out_strip[pl.ds(single, 42, stride=EXT), :]
        values = [out_strip[p * EXT + 8 * tile : p * EXT + 8 * tile + 8, :] for p in range(42)]
        values += [line[8 * j : 8 * j + 8, :] for j in range(6)]
        pack_tiles(message, 384, values)
    across_up[...] = up[384:416, :]
    across_down[...] = down[384:416, :]
    values = []
    for p in range(42):
        for t in range(1, 6):
            at = p * EXT + 8 * t
            values.append(out_strip[at : at + 8, :])
    for k, single in enumerate((7, 48)):
        at = 48 * (k + 1)
        line[at + 40 : at + 48, :] = jnp.zeros((8, CZ), F32)
        line[at : at + 42, :] = out_strip[pl.ds(single, 42, stride=EXT), :] * flags[2 + k]
        values += [line[at + 8 * j : at + 8 * j + 8, :] for j in range(6)]
    pack_tiles(across, 0, values)


def fold_y_kernel(flags, sol, low, high, out):
    for p in range(42):
        for message, tile in ((low, 1), (high, 5)):
            at = p * EXT + 8 * tile
            out[at : at + 8, :] = out[at : at + 8, :] + message[8 * p : 8 * p + 8, :]
    for k, (single, message) in enumerate(((7, low), (48, high))):
        at = pl.ds(single, 42, stride=EXT)
        out[at, :] = (out[at, :] + message[336:378, :]) * flags[2 + k]


def apply_kernel(
    sol, low, high, own_z, far_z, far_low, far_high, resid, c_x, c_down, c_up, c_z, c_face, h,
    out, applied, sums, field, pack, line,
):
    gz = lax.axis_index("gz")
    end = YROWS2 - 384
    lane = lanes(ZROWS2 + 2 * end)
    at_face = lax.rem(lane, 9) == jnp.where(gz == 0, 8, 0)
    shift = jnp.where(gz == 0, 7, 121)
    near = jnp.concatenate([own_z[...], low[384:YROWS2, :], high[384:YROWS2, :]], axis=0)
    got = jnp.concatenate([far_z[...], far_low[...], far_high[...]], axis=0)
    got = got + jnp.where(at_face, roll(near, shift, 1), 0.0)
    pack[...] = roll(got, jnp.where(gz == 0, 120, 127), 1)
    toward = jnp.where(gz == 0, 127, 1)
    lane8 = lanes(8)
    folded = jnp.where(gz == 0, lane8 - 120, 7 - lane8) >= 0

    def tile(index, start=0):
        q, j = divmod(index, PER)
        return roll(pack[start + 8 * q : start + 8 * q + 8, :], -9 * j, 1)

    def along_z(p, t):
        value = tile(p * 5 + t - 1)
        if t == 1:
            value = value + tile(p, ZROWS2)
        if t == 5:
            value = value + tile(p, ZROWS2 + end)
        return value

    for p in range(42):
        for t in range(1, 6):
            at = p * EXT + 8 * t
            value = sol[at : at + 8, :] + jnp.where(folded, along_z(p, t), 0.0)
            field[at : at + 8, :] = value
    for k, single in enumerate((7, 48)):
        for j in range(6):
            value = tile(210 + 6 * k + j) + tile(42 + j, ZROWS2 + k * end)
            line[8 * j : 8 * j + 8, :] = jnp.where(folded, value, 0.0)
        at = pl.ds(single, 42, stride=EXT)
        field[at, :] = sol[at, :] + line[0:42, :]
    pack[...] = roll(pack[...], toward, 1)

    outer = jnp.where(lanes(C) == outer_lane(), 0.5, 0.0)
    flux_x = c_x[0:C, :] * (field[EXT + 8 : EXT + 48, :] - field[8:48, :])
    sum_a = jnp.zeros((8, CZ), F32)
    sum_b = jnp.zeros((8, CZ), F32)
    def visit(x, carry):
        flux_x, sum_a, sum_b = carry
        at = (x + 1) * EXT
        to = rows_at(x * C, C)
        z = field[rows_at(at + 8, C), :]
        next_x = c_x[rows_at(x * C + C, C), :] * (field[rows_at(at + EXT + 8, C), :] - z)
        net = next_x - flux_x
        net = net + c_up[to, :] * (field[pl.ds(at + 9, C), :] - z)
        net = net - c_down[to, :] * (z - field[pl.ds(at + 7, C), :])
        flux_z = c_z[to, :] * (roll(z, -1, 1) - z)
        net = net + (flux_z - roll(flux_z, 1, 1)) + c_face[to, :] * (out[to, :] - z)
        image = mass_term * z - net + outer * h[to, :] * z
        out[to, :] = z
        applied[to, :] = image
        a, b = resid[to, :] * z, z * image
        for t in range(5):
            sum_a = sum_a + a[8 * t : 8 * t + 8]
            sum_b = sum_b + b[8 * t : 8 * t + 8]
        return next_x, sum_a, sum_b

    for x in range(C):
        for t in range(5):
            out[x * C + 8 * t : x * C + 8 * t + 8, :] = along_z(x + 1, t + 1)
    _, sum_a, sum_b = lax.fori_loop(0, C, visit, (flux_x, sum_a, sum_b), unroll=8)
    total_a = jnp.sum(sum_a, axis=0, keepdims=True)
    total_b = jnp.sum(sum_b, axis=0, keepdims=True)
    total_a = total_a + roll(total_a, CZ // 2, 1)
    total_b = total_b + roll(total_b, CZ // 2, 1)
    total = jnp.where(lanes(1) < CZ // 2, total_a, total_b)
    sums[...] = jnp.broadcast_to(total, sums.shape)


def gather_kernel(sums, out):
    out[...] = jnp.broadcast_to(jnp.sum(sums[...], axis=0, keepdims=True), out.shape)


def update_kernel(sums, guess, resid, field, applied, solution_out, resid_out):
    total = jnp.sum(sums[...], axis=0, keepdims=True)
    first = lanes(1) < CZ // 2
    above = jnp.sum(jnp.where(first, total, 0.0), axis=1, keepdims=True)
    below = jnp.sum(jnp.where(first, 0.0, total), axis=1, keepdims=True)
    step = above / below
    solution_out[...] = guess[...] + step * field[...]
    resid_out[...] = resid[...] - step * applied[...]


def on_device(gx, splits, right_side, guess_field, conduct_field):
    shape = right_side.shape
    b, v, h = (a.reshape(C * C, CZ) for a in (right_side, guess_field, conduct_field))
    n_gx, n_gy = lax.axis_size(gx), lax.axis_size("gy")
    at_x, at_y = lax.axis_index(gx), lax.axis_index("gy")
    flags = jnp.stack([at_x > 0, at_x < n_gx - 1, at_y > 0, at_y < n_gy - 1, at_x % 2 == 1]).astype(F32)

    def exchange(axis, up, down):
        n = lax.axis_size(axis)
        forward = [(i, i + 1) for i in range(n - 1)]
        backward = [(i + 1, i) for i in range(n - 1)]
        return lax.ppermute(up, axis, forward), lax.ppermute(down, axis, backward)

    def exchange_x(first, second):
        pairs = [[(i + k, i + 1 - k) for i in range(start, n_gx - 1, 2) for k in (0, 1)] for start in (1, 0)]
        return lax.ppermute(first, gx, pairs[0]), lax.ppermute(second, gx, pairs[1])

    def swap(value):
        return lax.ppermute(value, "gz", [(0, 1), (1, 0)])

    plane, forward, inverse, denom, eigen = tables()
    own = C * C
    box = EXT * EXT

    def buffer(rows):
        return pltpu.VMEM((rows, CZ), F32)

    up, down = call(
        strips_kernel, (YROWS, YROWS), guess_field, conduct_field, right_side,
        scratch=[pltpu.VMEM((C, C, CZ), F32)] * 3 + [pltpu.SemaphoreType.DMA((3, 2))],
        hbm=(0, 1, 2), limit=56, name="strips", work=2,
    )
    part, edge = call(residual_kernel, (own, 160), v, h, b, name="residual", work=2)
    low, high = exchange("gy", up, down)
    pairs, scale_a, scale_b = call(
        prepare_kernel, (own, box, box), eigen, v, h, denom, smem=(0,), name="prepare", work=2
    )
    right, left, faces = call(
        extend_y_kernel, (XROWS, XROWS, 4 * EXT),
        flags, part, pairs, up, down, edge, low, high,
        scratch=[buffer(XROWS)] * 2, smem=(0,), name="extend_y", work=1,
    )
    one, two = exchange_x(right, left)
    inner, part = call(
        inner_kernel, (38 * EXT, C * EXT),
        flags, plane, part, up, down, low, high, smem=(0,), name="inner", work=1,
    )
    (packed,) = call(pack_z_kernel, (ZROWS,), part, pairs, low, high, name="pack_z", work=2)
    own_z, fluxes = call(
        extend_x_kernel, (ZROWS, 2 * EXT), flags, packed, faces, one, two, inner,
        smem=(0,), name="extend_x", work=1,
    )
    far_z = swap(own_z)
    (main,) = call(
        forward_kernel, (box,), flags, plane, part, inner, fluxes, one, two,
        scratch=[buffer(box)], smem=(0,), name="forward", work=2,
    )
    second_a, second_b, sides, side_strip, right, left = call(
        solve_kernel, (box, box, 18 * EXT, 18 * EXT, XROWS2, XROWS2),
        flags, own_z, far_z, main, plane, forward, inverse, scale_a, scale_b,
        scratch=[buffer(box), buffer(XROWS2), buffer(XROWS2)], smem=(0,), name="solve", work=6,
    )
    resid, c_x, c_down, c_up, c_z, c_face = call(
        own_kernel, (own, own + C, own, own, own, own),
        flags, h, low, high, one, two, part, fluxes, own_z, far_z,
        scratch=[buffer(own + 2 * C)], smem=(0,), name="own", work=2,
    )
    one, two = exchange_x(right, left)
    sol, strip = call(
        rest_kernel, (42 * EXT, 42 * EXT),
        plane, inverse, second_a, second_b, sides, side_strip, name="rest", work=2,
    )
    sol, _, up, down, own_z, across_up, across_down = call(
        fold_x_kernel, (42 * EXT, 42 * EXT, YROWS2, YROWS2, ZROWS2, 32, 32),
        flags, sol, strip, one, two, resid,
        scratch=[buffer(144)], smem=(0,), alias={1: 0, 2: 1}, name="fold_x", work=1,
    )
    low, high = exchange("gy", up, down)
    far_z = swap(own_z)
    diagonal = [((j, k), (j + 1, 1 - k)) for j in range(n_gy - 1) for k in range(2)]
    pairs = [(2 * a + b, 2 * c + d) for (a, b), (c, d) in diagonal]
    far_low = lax.ppermute(across_up, ("gy", "gz"), pairs)
    far_high = lax.ppermute(across_down, ("gy", "gz"), [(b, a) for a, b in pairs])
    (sol,) = call(
        fold_y_kernel, (42 * EXT,), flags, sol, low, high, smem=(0,), alias={1: 0}, name="fold_y", work=1
    )
    first, last = splits
    field, applied, sums = call(
        apply_kernel, (own, own, lax.axis_size(first)),
        sol, low, high, own_z, far_z, far_low, far_high, resid, c_x, c_down, c_up, c_z, c_face, h,
        scratch=[buffer(42 * EXT), buffer(ZROWS2 + 64), buffer(48)], name="apply", work=3,
    )
    sums = lax.all_to_all(sums, first, 0, 0, tiled=True)
    (sums,) = call(gather_kernel, (lax.axis_size(last),), sums, name="gather")
    sums = lax.all_to_all(sums, last, 0, 0, tiled=True)
    out, resid = call(update_kernel, (own, own), sums, v, resid, field, applied, name="update", work=2)
    return out.reshape(shape), resid.reshape(shape)


def solution(mesh):
    n_gx, n_gy, n_gz = mesh.devices.shape
    if n_gx == 64:
        mesh = Mesh(mesh.devices.reshape(4, 8, 2, n_gy, n_gz), ("gx_x", "gx_y", "gx_c", "gy", "gz"))
        gx = ("gx_x", "gx_y", "gx_c")
        splits = (("gx_x", "gx_y"), ("gx_c", "gy", "gz"))
    else:
        gx = "gx"
        splits = (("gx",), ("gy", "gz"))
    placed = P(gx, "gy", "gz")
    return jax.shard_map(
        functools.partial(on_device, gx, splits),
        mesh=mesh,
        in_specs=(placed,) * 3,
        out_specs=(placed,) * 2,
        check_vma=False,
    )
```

```python
import functools

import jax
import jax.numpy as jnp
import ml_dtypes
import numpy as np
from jax import lax
from jax.experimental import pallas as pl
from jax.experimental.pallas import tpu as pltpu
from jax.sharding import Mesh
from jax.sharding import PartitionSpec as P

OVER = 8
C = 40
CZ = 128
EXT = C + 2 * OVER
EXTZ = CZ + 2 * OVER
TILES = EXT // 8
stiff_scale = 3.0
mass_term = 0.001

F32 = jnp.float32
BF16 = jnp.bfloat16
VMEM = pl.BlockSpec(memory_space=pltpu.VMEM)
SMEM = pl.BlockSpec(memory_space=pltpu.SMEM)
HBM = pl.BlockSpec(memory_space=pltpu.HBM)

YROWS = 440
XROWS = 616
PER_Z = 12
BLOCKS_Z = -(-EXT // PER_Z)
ZROWS = BLOCKS_Z * EXT
PER = 14
XROWS2 = 9 * EXT + 40
YROWS2 = 416
ZGROUPS2 = 42 * 5 + 12
ZROWS2 = 8 * -(-ZGROUPS2 // PER)


def sine_table(count):
    k = np.arange(1, count + 1)
    basis = np.sqrt(2.0 / (count + 1)) * np.sin(np.pi * k[:, None] * k[None, :] / (count + 1))
    eigen = 2.0 - 2.0 * np.cos(np.pi * k / (count + 1))
    return basis, eigen


def two_parts(table):
    high = table.astype(ml_dtypes.bfloat16)
    low = (table - high.astype(np.float64)).astype(ml_dtypes.bfloat16)
    return high, low


@functools.cache
def tables():
    basis, eigen = sine_table(EXT)
    basis_z, eigen_z = sine_table(EXTZ)
    high, low = two_parts(basis)
    plane = np.zeros((EXT, 192), ml_dtypes.bfloat16)
    plane[:, 0:EXT] = high
    plane[:, 64 : 64 + EXT] = low
    plane[:, 128 : 128 + EXT] = high
    forward = np.zeros((2, 256, 256))
    inverse = np.zeros((2, 256, 256))
    for gz in range(2):
        own = basis_z[8 : 8 + CZ]
        strip = basis_z[136:144] if gz == 0 else basis_z[0:8]
        face_own, face_far = (135, 136) if gz == 0 else (8, 7)
        forward[gz, :CZ, :EXTZ] = own
        forward[gz, CZ, :EXTZ] = basis_z[face_own] - basis_z[face_far]
        forward[gz, CZ + 2 : CZ + 10, :EXTZ] = strip
        inverse[gz, :EXTZ, :CZ] = own.T
        inverse[gz, :EXTZ, CZ : CZ + 9] = (basis_z[135:144] if gz == 0 else basis_z[0:9]).T

    def stacked(table):
        high, low = two_parts(table)
        return np.concatenate([high, high, low], axis=1)

    denom = np.full((EXT, 256), 1.0)
    denom[:, :EXTZ] = stiff_scale * (eigen[:, None] + eigen_z[None, :]) + mass_term
    return (
        plane,
        stacked(forward),
        stacked(inverse),
        denom.astype(np.float32),
        (stiff_scale * eigen).astype(np.float32),
    )


def roll(value, shift, axis):
    if isinstance(shift, int):
        shift = shift % value.shape[axis]
        return value if shift == 0 else pltpu.roll(value, shift, axis)
    return pltpu.roll(value, lax.rem(shift + 2 * value.shape[axis], value.shape[axis]), axis)


def lanes(rows):
    return lax.broadcasted_iota(jnp.int32, (rows, CZ), 1)


def rows_at(start, size):
    return pl.ds(pl.multiple_of(start, 8), size)


def tile_at(index):
    return rows_at(index * 8, 8)


def call(body, out_rows, *args, scratch=(), limit=16, name=None, smem=(), hbm=(), work=0):
    place = {**{i: SMEM for i in smem}, **{i: HBM for i in hbm}}
    return pl.pallas_call(
        body,
        out_shape=[jax.ShapeDtypeStruct((rows, CZ), F32) for rows in out_rows],
        in_specs=[place.get(i, VMEM) for i in range(len(args))],
        out_specs=[VMEM] * len(out_rows),
        scratch_shapes=list(scratch),
        compiler_params=pltpu.CompilerParams(vmem_limit_bytes=limit * 2**20),
        cost_estimate=pl.CostEstimate(
            flops=int(work * 1e9), bytes_accessed=int(work * 2e6), transcendentals=0
        )
        if work
        else None,
        name=name,
    )(*args)


def strip_base():
    return jnp.where(lax.axis_index("gz") == 0, 118, 126)


def face_lane():
    return jnp.where(lax.axis_index("gz") == 0, 127, 0)


def outer_lane():
    return jnp.where(lax.axis_index("gz") == 0, 0, 127)


def pair_of(v, h, lane, base, face):
    return jnp.where(lane == base, roll(v, base - face, 1), 0.0) + jnp.where(
        lane == base + 1, roll(h, base + 1 - face, 1), 0.0
    )


def strips_kernel(v_in, h_in, b_in, up, down, v, h, b, sems):
    copies = []
    for k, (source, target, size) in enumerate(((v_in, v, 16), (h_in, h, 16), (b_in, b, 8))):
        for side, first in enumerate((0, C - size)):
            at = pl.ds(first, size)
            copies.append(
                pltpu.make_async_copy(source.at[:, at, :], target.at[:, at, :], sems.at[k, side])
            )
            copies[-1].start()
    base, face = strip_base(), face_lane()
    lane = lanes(8)
    row = lax.broadcasted_iota(jnp.int32, (8, CZ), 0)
    z_half = jnp.where(lane < CZ - 1, 0.5, 0.0)
    outer = jnp.where(lane == outer_lane(), 0.5, 0.0)
    last = C - 1
    for copy in copies:
        copy.wait()

    def tile(x, start, beyond, sign, flux_x):
        following = jnp.minimum(x + 1, last)
        at, to = pl.ds(start, 8), pl.ds(beyond, 8)
        vi, hi = v[x, at, :], h[x, at, :]
        next_x = 0.5 * (hi + h[following, at, :]) * (v[following, at, :] - vi)
        flux_y = 0.5 * (hi + h[x, to, :]) * (v[x, to, :] - vi)
        edge = 0 if sign > 0 else 7
        net_y = flux_y - jnp.where(row == edge, 0.0, roll(flux_y, sign, 0))
        flux_z = z_half * (hi + roll(hi, -1, 1)) * (roll(vi, -1, 1) - vi)
        applied = (
            mass_term * vi
            - (next_x - flux_x)
            - net_y
            - (flux_z - roll(flux_z, 1, 1))
            + outer * hi * vi
        )
        return b[x, at, :] - applied, next_x, vi, hi

    def visit(x, carry):
        flux_up, flux_down, pack_up, pack_down = carry
        resid, flux_down, vi, hi = tile(x, 0, 1, 1, flux_down)
        down[tile_at(x), :] = resid
        down[pl.ds(320 + x, 1), :] = vi[0:1]
        down[pl.ds(360 + x, 1), :] = hi[0:1]
        pack_down = pack_down + roll(pair_of(vi, hi, lane, base, face), 2 * x - base, 1)
        resid, flux_up, vi, hi = tile(x, 32, 31, -1, flux_up)
        up[tile_at(x), :] = resid
        up[pl.ds(320 + x, 1), :] = vi[7:8]
        up[pl.ds(360 + x, 1), :] = hi[7:8]
        pack_up = pack_up + roll(pair_of(vi, hi, lane, base, face), 2 * x - base, 1)
        return flux_up, flux_down, pack_up, pack_down

    zero = jnp.zeros((8, CZ), F32)
    _, _, pack_up, pack_down = lax.fori_loop(0, C, visit, (zero,) * 4, unroll=8)
    up[432:440, :] = pack_up
    down[432:440, :] = pack_down
    for message, first in ((up, 32), (down, 0)):
        at = pl.ds(first, 8)
        message[400:408, :] = v[0, at, :]
        message[408:416, :] = h[0, at, :]
        message[416:424, :] = v[last, at, :]
        message[424:432, :] = h[last, at, :]


def residual_kernel(v, h, b, part, edge):
    lane = lanes(C)
    row = lax.broadcasted_iota(jnp.int32, (C, CZ), 0)
    y_half = jnp.where(row > 0, 0.5, 0.0)
    z_half = jnp.where(lane < CZ - 1, 0.5, 0.0)
    outer = jnp.where(lane == outer_lane(), 0.5, 0.0)

    def visit(x, flux_x):
        own = rows_at(x * C, C)
        following = rows_at(jnp.minimum(x + 1, C - 1) * C, C)
        vi, hi = v[own, :], h[own, :]
        next_x = 0.5 * (hi + h[following, :]) * (v[following, :] - vi)
        flux_y = y_half * (hi + roll(hi, 1, 0)) * (vi - roll(vi, 1, 0))
        flux_z = z_half * (hi + roll(hi, -1, 1)) * (roll(vi, -1, 1) - vi)
        applied = (
            mass_term * vi
            - (next_x - flux_x)
            - (roll(flux_y, -1, 0) - flux_y)
            - (flux_z - roll(flux_z, 1, 1))
            + outer * hi * vi
        )
        part[own, :] = b[own, :] - applied
        return next_x

    lax.fori_loop(0, C, visit, jnp.zeros((C, CZ), F32), unroll=4)
    last = (C - 1) * C
    edge[0:40, :] = v[0:40, :]
    edge[40:80, :] = h[0:40, :]
    edge[80:120, :] = v[last : last + 40, :]
    edge[120:160, :] = h[last : last + 40, :]


def prepare_kernel(eigen, v, h, denom, out, out_a, out_b):
    base, face = strip_base(), face_lane()
    lane = lanes(C)

    def visit_pair(x, _):
        at = rows_at(x * C, C)
        out[at, :] = pair_of(v[at, :], h[at, :], lane, base, face)
        return 0

    lax.fori_loop(0, C, visit_pair, 0, unroll=8)

    def visit(y, _):
        value = 1.0 / (denom[...] + eigen[y])
        at = rows_at(y * EXT, EXT)
        out_a[at, :] = value[:, :CZ]
        out_b[at, :] = value[:, CZ:]
        return 0

    lax.fori_loop(0, EXT, visit, 0, unroll=4)


def choose(flag, a, b):
    return jnp.where(flag > 0.5, a, b)


def by_parity(flags, first, second):
    def before(start, stop):
        return choose(flags[4], second[start:stop, :], first[start:stop, :])

    def after(start, stop):
        return choose(flags[4], first[start:stop, :], second[start:stop, :])

    return before, after


def pick(pack, index, to):
    pair = lax.div(lanes(8), 2) == index
    return roll(jnp.where(pair, pack, 0.0), to - 2 * index, 1)


def strip_mask():
    lane = lanes(8)
    return jnp.where(lax.axis_index("gz") == 0, lane - 120, 7 - lane) >= 0


def y_fluxes(up, down, low, high):
    flux_a = 0.5 * (low[360:400, :] + down[360:400, :]) * (down[320:360, :] - low[320:360, :])
    flux_b = 0.5 * (up[360:400, :] + high[360:400, :]) * (high[320:360, :] - up[320:360, :])
    return flux_a, flux_b


def extend_y(flags, fluxes, part, low, high, out, start, stop):
    for x in range(start, stop):
        at = (x - start) * EXT
        out[at : at + 8, :] = low[8 * x : 8 * x + 8, :]
        out[at + 8 : at + 48, :] = part[x * C : x * C + C, :]
        out[at + 48 : at + 56, :] = high[8 * x : 8 * x + 8, :]
    flux_a, flux_b = (flux[start:stop] for flux in fluxes)
    for row, value in ((8, -flux_a), (7, flux_a * flags[2]), (47, flux_b), (48, -flux_b * flags[3])):
        at = pl.ds(row, stop - start, stride=EXT)
        out[at, :] = out[at, :] + value


def extend_y_kernel(flags, part, vh, up, down, edge, low, high, first, second, faces, right, left):
    base, strip_lanes = strip_base(), strip_mask()
    fluxes = y_fluxes(up, down, low, high)
    for message, start, strip, own in ((left, 0, 400, 0), (right, 32, 416, 80)):
        extend_y(flags, fluxes, part, low, high, message, start, start + OVER)
        for k in range(2):
            at = 448 + k * EXT
            message[at : at + 8, :] = low[strip + 8 * k : strip + 8 * k + 8, :]
            message[at + 8 : at + 48, :] = edge[own + 40 * k : own + 40 * k + 40, :]
            message[at + 48 : at + 56, :] = high[strip + 8 * k : strip + 8 * k + 8, :]
        for t in range(TILES):
            near = jnp.zeros((8, CZ), F32)
            taken = jnp.zeros((8, CZ), F32)
            for i in range(OVER):
                x = start + i
                at = i * EXT + 8 * t
                value = jnp.where(strip_lanes, message[at : at + 8, :], 0.0)
                if t == 0:
                    taken = taken + pick(low[432:440, :], x, 10 * i)
                elif t == 6:
                    taken = taken + pick(high[432:440, :], x, 10 * i)
                else:
                    value = value + vh[x * C + 8 * t - 8 : x * C + 8 * t, :]
                near = near + roll(value, 10 * i, 1)
            message[560 + 8 * t : 568 + 8 * t, :] = roll(near, -base, 1) + taken
    faces[0:112, :] = left[448:560, :]
    faces[112:224, :] = right[448:560, :]
    first[...] = choose(flags[4], right[...], left[...])
    second[...] = choose(flags[4], left[...], right[...])


def pack_z_kernel(part, vh, low, high, message):
    base, strip_lanes = strip_base(), strip_mask()
    for q in range(BLOCKS_Z):
        for t in range(TILES):
            near = jnp.zeros((8, CZ), F32)
            taken = jnp.zeros((8, CZ), F32)
            for j in range(PER_Z):
                x = q * PER_Z + j - OVER
                if not 0 <= x < C:
                    continue
                value = jnp.where(strip_lanes, part[x * EXT + 8 * t : x * EXT + 8 * t + 8, :], 0.0)
                if t == 0:
                    taken = taken + pick(low[432:440, :], x, 10 * j)
                elif t == 6:
                    taken = taken + pick(high[432:440, :], x, 10 * j)
                else:
                    value = value + vh[x * C + 8 * t - 8 : x * C + 8 * t, :]
                near = near + roll(value, 10 * j, 1)
            at = q * EXT + 8 * t
            message[at : at + 8, :] = roll(near, -base, 1) + taken


def extend_x_kernel(flags, packed, faces, first, second, inner, message, fluxes):
    base, strip_lanes = strip_base(), strip_mask()
    before, after = by_parity(flags, first, second)
    flux_a = 0.5 * (before(504, 560) + faces[56:112, :]) * (faces[0:56, :] - before(448, 504))
    flux_b = 0.5 * (faces[168:224, :] + after(504, 560)) * (after(448, 504) - faces[112:168, :])
    fluxes[0:EXT, :] = flux_a
    fluxes[EXT : 2 * EXT, :] = flux_b
    message[...] = packed[...]
    end = (BLOCKS_Z - 1) * EXT
    message[0:EXT, :] = message[0:EXT, :] + before(560, 616)
    message[end : end + EXT, :] = message[end : end + EXT, :] + after(560, 616)

    def add(x, t, value):
        q, j = divmod(x, PER_Z)
        at = q * EXT + 8 * t
        message[at : at + 8, :] = message[at : at + 8, :] + roll(value, 10 * j, 1)

    for t in range(TILES):
        a = roll(jnp.where(strip_lanes, flux_a[8 * t : 8 * t + 8], 0.0), -base, 1)
        b = roll(jnp.where(strip_lanes, flux_b[8 * t : 8 * t + 8], 0.0), -base, 1)
        add(OVER - 1, t, a * flags[0])
        add(OVER, t, -a)
        add(OVER + C - 1, t, b)
        add(OVER + C, t, -b * flags[1])


def halves(value):
    high = value.astype(BF16)
    return high, (value - high.astype(F32)).astype(BF16)


def dot(a, b):
    return jnp.dot(a, b, preferred_element_type=F32)


def along_lanes(value, table):
    high, low = halves(value)
    return dot(jnp.concatenate([high, low, high], axis=1), table)


def along_rows(table, value):
    padded = jnp.concatenate([value, jnp.zeros((8, value.shape[1]), F32)], axis=0)
    high, low = halves(padded)
    return dot(table, jnp.concatenate([high, high, low], axis=0))


def beside(a, b):
    return jnp.concatenate([a, b], axis=1)


def inner_kernel(flags, plane, box, up, down, low, high, out, part):
    table = plane[...]
    extend_y(flags, y_fluxes(up, down, low, high), box, low, high, part, 0, C)
    for x in range(1, C - 1, 2):
        at, then = pl.ds(x * EXT, EXT), pl.ds((x + 1) * EXT, EXT)
        value = along_rows(table, beside(part[at, :], part[then, :]))
        out[(x - 1) * EXT : x * EXT, :] = value[:, :CZ]
        out[x * EXT : (x + 1) * EXT, :] = value[:, CZ:]


def forward_kernel(flags, plane, part, inner, fluxes, one, two, out, first):
    before, after = by_parity(flags, one, two)
    table = plane[...]
    flux_a, flux_b = fluxes[0:EXT, :], fluxes[EXT : 2 * EXT, :]
    planes = {x: before(x * EXT, (x + 1) * EXT) for x in range(OVER)}
    planes[7] = planes[7] + flux_a * flags[0]
    planes[8] = part[0:EXT, :] - flux_a
    planes[47] = part[(C - 1) * EXT : C * EXT, :] + flux_b
    planes.update({48 + x: after(x * EXT, (x + 1) * EXT) for x in range(OVER)})
    planes[48] = planes[48] - flux_b * flags[1]
    first[9 * EXT : 47 * EXT, :] = inner[...]
    order = sorted(planes)
    for x, then in zip(order[0::2], order[1::2]):
        value = along_rows(table, beside(planes[x], planes[then]))
        first[x * EXT : (x + 1) * EXT, :] = value[:, :CZ]
        first[then * EXT : (then + 1) * EXT, :] = value[:, CZ:]

    def visit_x(c, _):
        for i in range(14):
            y = 2 * (c * 14 + i)
            value = beside(first[pl.ds(y, EXT, stride=EXT), :], first[pl.ds(y + 1, EXT, stride=EXT), :])
            value = along_rows(table, value)
            out[rows_at(y * EXT, EXT), :] = value[:, :CZ]
            out[rows_at((y + 1) * EXT, EXT), :] = value[:, CZ:]
        return 0

    lax.fori_loop(0, 2, visit_x, 0)


def face_terms(own_z, far_z):
    both = own_z[...] + far_z[...]
    half = 0.5 * roll(both, -1, 1)
    return half, half * (far_z[...] - own_z[...])


STEP = 28


def solve_kernel(
    flags, own_z, far_z, main, plane, forward, inverse, scale_a, scale_b,
    second_a, second_b, sol, strip, first, second, halo, right, left,
):
    gz = lax.axis_index("gz")
    table = plane[...]
    _, flux = face_terms(own_z, far_z)
    pack = jnp.where(lax.rem(lanes(ZROWS), 10) == 0, flux, far_z[...])
    blocks = [pack[q * EXT : (q + 1) * EXT] for q in range(BLOCKS_Z)]
    done = []
    for q in range(0, BLOCKS_Z - 1, 2):
        value = along_rows(table, beside(blocks[q], blocks[q + 1]))
        done += [value[:, :CZ], value[:, CZ:]]
    done.append(along_rows(table, blocks[-1]))
    for x in range(EXT):
        q, j = x // PER_Z, x % PER_Z
        halo[x * EXT : (x + 1) * EXT, :] = roll(done[q], -10 * j, 1)

    forward_table = forward[gz]
    inverse_table = inverse[gz]

    def visit(c, _):
        parts = []
        for i in range(0, STEP, 2):
            y = c * STEP + i
            value = beside(halo[pl.ds(y, EXT, stride=EXT), :], halo[pl.ds(y + 1, EXT, stride=EXT), :])
            value = along_rows(table, value)
            parts.append(beside(main[rows_at(y * EXT, EXT), :], value[:, :CZ]))
            parts.append(beside(main[rows_at((y + 1) * EXT, EXT), :], value[:, CZ:]))
        value = along_lanes(jnp.concatenate(parts, axis=0), forward_table)
        at = rows_at(c * STEP * EXT, STEP * EXT)
        value = value * beside(scale_a[at, :], scale_b[at, :])
        for i in range(STEP):
            part = along_rows(table, value[i * EXT : (i + 1) * EXT])
            to = pl.ds(c * STEP + i, EXT, stride=EXT)
            second_a[to, :] = part[:, :CZ]
            second_b[to, :] = part[:, CZ:]
        return 0

    lax.fori_loop(0, EXT // STEP, visit, 0)

    for k, (message, start) in enumerate(((left, 0), (right, 47))):
        inverse_planes(table, inverse_table, second_a, second_b, sol, strip, range(start, start + 9), 9 * k)
        message[0 : 9 * EXT, :] = sol[9 * k * EXT : 9 * (k + 1) * EXT, :]
        tiles = [strip[pl.ds((9 * k * TILES + j) * 8, 8), :] for j in range(63)]
        pack_tiles(message, 9 * EXT, tiles)
    first[...] = choose(flags[4], right[...], left[...])
    second[...] = choose(flags[4], left[...], right[...])


def inverse_planes(table, inverse_table, second_a, second_b, sol, strip, planes, to):
    parts = []
    for x in planes:
        at = pl.ds(x * EXT, EXT)
        parts.append(along_rows(table, beside(second_a[at, :], second_b[at, :])))
    value = along_lanes(jnp.concatenate(parts, axis=0), inverse_table)
    at = pl.ds(to * EXT, len(planes) * EXT)
    sol[at, :] = value[:, :CZ]
    strip[at, :] = value[:, CZ:]


def rest_kernel(plane, inverse, second_a, second_b, sides, side_strip, sol, strip):
    table, inverse_table = plane[...], inverse[lax.axis_index("gz")]
    for first, last in ((9, 19), (19, 29), (29, 38), (38, 47)):
        inverse_planes(
            table, inverse_table, second_a, second_b, sol, strip, range(first, last), first - 7
        )
    for target, source in ((sol, sides), (strip, side_strip)):
        target[0 : 2 * EXT, :] = source[7 * EXT : 9 * EXT, :]
        target[40 * EXT : 42 * EXT, :] = source[9 * EXT : 11 * EXT, :]


def own_kernel(flags, h, low, high, one, two, part, fluxes, own_z, far_z, resid, c_x, c_down, c_up, c_z, c_face, cond):
    face, outer = face_lane(), outer_lane()
    half, flux = face_terms(own_z, far_z)
    half, flux = roll(half, face, 1), roll(flux, face, 1)
    lane8 = lanes(8)
    for x in range(C):
        q, j = (x + OVER) // PER_Z, (x + OVER) % PER_Z
        for t in range(5):
            at = q * EXT + 8 * (t + 1)
            to = x * C + 8 * t
            source = x * EXT + 8 * (t + 1)
            moved = jnp.where(lane8 == face, roll(flux[at : at + 8], -10 * j, 1), 0.0)
            if x == 0:
                moved = moved - fluxes[source : source + 8, :]
            elif x == C - 1:
                moved = moved + fluxes[source + EXT - x * EXT : source + EXT - x * EXT + 8, :]
            resid[to : to + 8, :] = part[source : source + 8, :] + moved
            c_face[to : to + 8, :] = jnp.where(
                lane8 == face, roll(half[at : at + 8], -10 * j, 1), 0.0
            )
    before, after = by_parity(flags, one, two)
    cond[0:C, :] = before(512, 552)
    cond[C : C + C * C, :] = h[...]
    cond[C + C * C :, :] = after(512, 552)
    z_half = jnp.where(lanes(C) < CZ - 1, 0.5, 0.0)
    row = lax.broadcasted_iota(jnp.int32, (C, CZ), 0)
    for x in range(C):
        at = x * C
        hi = h[at : at + C, :]
        c_x[at : at + C, :] = 0.5 * (cond[at : at + C, :] + hi)
        below = jnp.where(row == 0, low[360 + x : 361 + x, :], roll(hi, 1, 0))
        above = jnp.where(row == C - 1, high[360 + x : 361 + x, :], roll(hi, -1, 0))
        c_down[at : at + C, :] = 0.5 * (hi + below)
        c_up[at : at + C, :] = 0.5 * (hi + above)
        c_z[at : at + C, :] = z_half * (hi + roll(hi, -1, 1))
    c_x[C * C :, :] = 0.5 * (cond[C * C : C * C + C, :] + cond[C * C + C :, :])


def pack_tiles(message, at, values):
    for q in range(-(-len(values) // PER)):
        acc = values[q * PER]
        for j, value in enumerate(values[q * PER + 1 : (q + 1) * PER], 1):
            acc = acc + roll(value, 9 * j, 1)
        message[at + 8 * q : at + 8 * q + 8, :] = acc


def unpack_tile(message, at, index):
    q = index // PER
    return roll(message[rows_at(at + 8 * q, 8), :], -9 * (index - q * PER), 1)


def fold_x_kernel(flags, sol, strip, one, two, _, out, out_strip, up, down, line):
    size = 42 * EXT
    narrow = lanes(8) < 9
    before, after = by_parity(flags, one, two)
    tail = 33 * EXT
    out[0 : 9 * EXT, :] = sol[0 : 9 * EXT, :] + before(0, 9 * EXT)
    out[9 * EXT : tail, :] = sol[9 * EXT : tail, :]
    out[tail:size, :] = sol[tail:size, :] + after(0, 9 * EXT)
    out_strip[9 * EXT : tail, :] = strip[9 * EXT : tail, :]
    packs = [side(9 * EXT, XROWS2) for side in (before, after)]

    for j in range(63):
        q, i = divmod(j, PER)
        for pack, at in ((packs[0], 8 * j), (packs[1], tail + 8 * j)):
            value = jnp.where(narrow, roll(pack[8 * q : 8 * q + 8], -9 * i, 1), 0.0)
            out_strip[at : at + 8, :] = strip[at : at + 8, :] + value

    for array in (out, out_strip):
        array[0:EXT, :] = array[0:EXT, :] * flags[0]
        array[41 * EXT : size, :] = array[41 * EXT : size, :] * flags[1]

    for message, tile, single in ((up, 6, 47), (down, 0, 8)):
        for p in range(42):
            message[8 * p : 8 * p + 8, :] = out[p * EXT + 8 * tile : p * EXT + 8 * tile + 8, :]
        message[376:384, :] = jnp.zeros((8, CZ), F32)
        message[336:378, :] = out[pl.ds(single, 42, stride=EXT), :]
        line[40:48, :] = jnp.zeros((8, CZ), F32)
        line[0:42, :] = out_strip[pl.ds(single, 42, stride=EXT), :]
        values = [out_strip[p * EXT + 8 * tile : p * EXT + 8 * tile + 8, :] for p in range(42)]
        values += [line[8 * j : 8 * j + 8, :] for j in range(6)]
        pack_tiles(message, 384, values)


def pack_own_kernel(flags, strip, message, line):
    values = []
    for p in range(42):
        for t in range(1, 6):
            at = p * EXT + 8 * t
            values.append(strip[at : at + 8, :])
    for k, single in enumerate((7, 48)):
        at = 48 * k
        line[at + 40 : at + 48, :] = jnp.zeros((8, CZ), F32)
        line[at : at + 42, :] = strip[pl.ds(single, 42, stride=EXT), :] * flags[2 + k]
        values += [line[at + 8 * j : at + 8 * j + 8, :] for j in range(6)]
    pack_tiles(message, 0, values)


def add_y_kernel(flags, packed, low, high, message):
    place = lax.div(lanes(8), 9)
    rows = [packed[8 * q : 8 * q + 8, :] for q in range(ZROWS2 // 8)]

    def add(source, index, target, factor=None):
        q, j = divmod(index, PER)
        to, k = divmod(target, PER)
        value = roll(jnp.where(place == j, source[384 + 8 * q : 392 + 8 * q, :], 0.0), 9 * (k - j), 1)
        rows[to] = rows[to] + (value if factor is None else value * factor)

    for source, t, single, flag in ((low, 1, 210, 2), (high, 5, 216, 3)):
        for p in range(42):
            add(source, p, p * 5 + t - 1)
        for j in range(6):
            add(source, 42 + j, single + j, flags[flag])
    for q, value in enumerate(rows):
        message[8 * q : 8 * q + 8, :] = value


def fold_y_kernel(flags, sol, low, high, out):
    for p in range(42):
        for message, tile in ((low, 1), (high, 5)):
            at = p * EXT + 8 * tile
            out[at : at + 8, :] = sol[at : at + 8, :] + message[8 * p : 8 * p + 8, :]
        at = p * EXT
        out[at : at + 8, :] = sol[at : at + 8, :]
        out[at + 16 : at + 40, :] = sol[at + 16 : at + 40, :]
        out[at + 48 : at + 56, :] = sol[at + 48 : at + 56, :]
    for k, (single, message) in enumerate(((7, low), (48, high))):
        at = pl.ds(single, 42, stride=EXT)
        out[at, :] = (out[at, :] + message[336:378, :]) * flags[2 + k]


def apply_kernel(
    sol, own_z, far_z, resid, c_x, c_down, c_up, c_z, c_face, h,
    out, applied, sums, field, pack, line,
):
    gz = lax.axis_index("gz")
    lane = lanes(ZROWS2)
    at_face = lax.rem(lane, 9) == jnp.where(gz == 0, 8, 0)
    shift = jnp.where(gz == 0, 7, 121)
    packed = far_z[...] + jnp.where(at_face, roll(own_z[...], shift, 1), 0.0)
    pack[...] = roll(packed, jnp.where(gz == 0, 120, 127), 1)
    toward = jnp.where(gz == 0, 127, 1)
    lane8 = lanes(8)
    folded = jnp.where(gz == 0, lane8 - 120, 7 - lane8) >= 0

    def tile(index):
        q, j = divmod(index, PER)
        return roll(pack[8 * q : 8 * q + 8, :], -9 * j, 1)

    for p in range(42):
        for t in range(5):
            at = p * EXT + 8 * t + 8
            field[at : at + 8, :] = sol[at : at + 8, :] + jnp.where(folded, tile(p * 5 + t), 0.0)
    for k, single in enumerate((7, 48)):
        for j in range(6):
            line[8 * j : 8 * j + 8, :] = jnp.where(folded, tile(210 + 6 * k + j), 0.0)
        at = pl.ds(single, 42, stride=EXT)
        field[at, :] = sol[at, :] + line[0:42, :]
    pack[...] = roll(pack[...], toward, 1)

    outer = jnp.where(lanes(C) == outer_lane(), 0.5, 0.0)
    flux_x = c_x[0:C, :] * (field[EXT + 8 : EXT + 48, :] - field[8:48, :])
    sum_a = jnp.zeros((8, CZ), F32)
    sum_b = jnp.zeros((8, CZ), F32)
    def visit(x, carry):
        flux_x, sum_a, sum_b = carry
        at = (x + 1) * EXT
        to = rows_at(x * C, C)
        z = field[rows_at(at + 8, C), :]
        next_x = c_x[rows_at(x * C + C, C), :] * (field[rows_at(at + EXT + 8, C), :] - z)
        net = next_x - flux_x
        net = net + c_up[to, :] * (field[pl.ds(at + 9, C), :] - z)
        net = net - c_down[to, :] * (z - field[pl.ds(at + 7, C), :])
        flux_z = c_z[to, :] * (roll(z, -1, 1) - z)
        net = net + (flux_z - roll(flux_z, 1, 1)) + c_face[to, :] * (out[to, :] - z)
        image = mass_term * z - net + outer * h[to, :] * z
        out[to, :] = z
        applied[to, :] = image
        a, b = resid[to, :] * z, z * image
        for t in range(5):
            sum_a = sum_a + a[8 * t : 8 * t + 8]
            sum_b = sum_b + b[8 * t : 8 * t + 8]
        return next_x, sum_a, sum_b

    for x in range(C):
        for t in range(5):
            out[x * C + 8 * t : x * C + 8 * t + 8, :] = tile((x + 1) * 5 + t)
    _, sum_a, sum_b = lax.fori_loop(0, C, visit, (flux_x, sum_a, sum_b), unroll=8)
    total_a = jnp.sum(sum_a, axis=0, keepdims=True)
    total_b = jnp.sum(sum_b, axis=0, keepdims=True)
    total_a = total_a + roll(total_a, CZ // 2, 1)
    total_b = total_b + roll(total_b, CZ // 2, 1)
    total = jnp.where(lanes(1) < CZ // 2, total_a, total_b)
    sums[...] = jnp.broadcast_to(total, sums.shape)


def gather_kernel(sums, out):
    out[...] = jnp.broadcast_to(jnp.sum(sums[...], axis=0, keepdims=True), out.shape)


def update_kernel(sums, guess, resid, field, applied, solution_out, resid_out):
    total = jnp.sum(sums[...], axis=0, keepdims=True)
    first = lanes(1) < CZ // 2
    above = jnp.sum(jnp.where(first, total, 0.0), axis=1, keepdims=True)
    below = jnp.sum(jnp.where(first, 0.0, total), axis=1, keepdims=True)
    step = above / below
    solution_out[...] = guess[...] + step * field[...]
    resid_out[...] = resid[...] - step * applied[...]


def on_device(gx, splits, right_side, guess_field, conduct_field):
    shape = right_side.shape
    b, v, h = (a.reshape(C * C, CZ) for a in (right_side, guess_field, conduct_field))
    n_gx, n_gy = lax.axis_size(gx), lax.axis_size("gy")
    at_x, at_y = lax.axis_index(gx), lax.axis_index("gy")
    flags = jnp.stack([at_x > 0, at_x < n_gx - 1, at_y > 0, at_y < n_gy - 1, at_x % 2 == 1]).astype(F32)

    def exchange(axis, up, down):
        n = lax.axis_size(axis)
        forward = [(i, i + 1) for i in range(n - 1)]
        backward = [(i + 1, i) for i in range(n - 1)]
        return lax.ppermute(up, axis, forward), lax.ppermute(down, axis, backward)

    def exchange_x(first, second):
        pairs = [[(i + k, i + 1 - k) for i in range(start, n_gx - 1, 2) for k in (0, 1)] for start in (1, 0)]
        return lax.ppermute(first, gx, pairs[0]), lax.ppermute(second, gx, pairs[1])

    def swap(value):
        return lax.ppermute(value, "gz", [(0, 1), (1, 0)])

    plane, forward, inverse, denom, eigen = tables()
    own = C * C
    box = EXT * EXT

    def buffer(rows):
        return pltpu.VMEM((rows, CZ), F32)

    up, down = call(
        strips_kernel, (YROWS, YROWS), guess_field, conduct_field, right_side,
        scratch=[pltpu.VMEM((C, C, CZ), F32)] * 3 + [pltpu.SemaphoreType.DMA((3, 2))],
        hbm=(0, 1, 2), limit=56, name="strips", work=2,
    )
    part, edge = call(residual_kernel, (own, 160), v, h, b, name="residual", work=2)
    low, high = exchange("gy", up, down)
    pairs, scale_a, scale_b = call(
        prepare_kernel, (own, box, box), eigen, v, h, denom, smem=(0,), name="prepare", work=2
    )
    right, left, faces = call(
        extend_y_kernel, (XROWS, XROWS, 4 * EXT),
        flags, part, pairs, up, down, edge, low, high,
        scratch=[buffer(XROWS)] * 2, smem=(0,), name="extend_y", work=1,
    )
    one, two = exchange_x(right, left)
    inner, part = call(
        inner_kernel, (38 * EXT, C * EXT),
        flags, plane, part, up, down, low, high, smem=(0,), name="inner", work=1,
    )
    (packed,) = call(pack_z_kernel, (ZROWS,), part, pairs, low, high, name="pack_z", work=2)
    own_z, fluxes = call(
        extend_x_kernel, (ZROWS, 2 * EXT), flags, packed, faces, one, two, inner,
        smem=(0,), name="extend_x", work=1,
    )
    far_z = swap(own_z)
    (main,) = call(
        forward_kernel, (box,), flags, plane, part, inner, fluxes, one, two,
        scratch=[buffer(box)], smem=(0,), name="forward", work=2,
    )
    second_a, second_b, sides, side_strip, right, left = call(
        solve_kernel, (box, box, 18 * EXT, 18 * EXT, XROWS2, XROWS2),
        flags, own_z, far_z, main, plane, forward, inverse, scale_a, scale_b,
        scratch=[buffer(box), buffer(XROWS2), buffer(XROWS2)], smem=(0,), name="solve", work=6,
    )
    resid, c_x, c_down, c_up, c_z, c_face = call(
        own_kernel, (own, own + C, own, own, own, own),
        flags, h, low, high, one, two, part, fluxes, own_z, far_z,
        scratch=[buffer(own + 2 * C)], smem=(0,), name="own", work=2,
    )
    one, two = exchange_x(right, left)
    sol, strip = call(
        rest_kernel, (42 * EXT, 42 * EXT),
        plane, inverse, second_a, second_b, sides, side_strip, name="rest", work=2,
    )
    sol, strip, up, down = call(
        fold_x_kernel, (42 * EXT, 42 * EXT, YROWS2, YROWS2),
        flags, sol, strip, one, two, resid,
        scratch=[buffer(48)], smem=(0,), name="fold_x", work=1,
    )
    low, high = exchange("gy", up, down)
    (packed,) = call(
        pack_own_kernel, (ZROWS2,), flags, strip,
        scratch=[buffer(96)], smem=(0,), name="pack_own", work=1,
    )
    (own_z,) = call(
        add_y_kernel, (ZROWS2,), flags, packed, low, high, smem=(0,), name="add_y", work=1
    )
    far_z = swap(own_z)
    (sol,) = call(
        fold_y_kernel, (42 * EXT,), flags, sol, low, high, smem=(0,), name="fold_y", work=1
    )
    first, last = splits
    field, applied, sums = call(
        apply_kernel, (own, own, lax.axis_size(first)),
        sol, own_z, far_z, resid, c_x, c_down, c_up, c_z, c_face, h,
        scratch=[buffer(42 * EXT), buffer(ZROWS2), buffer(48)], name="apply", work=3,
    )
    sums = lax.all_to_all(sums, first, 0, 0, tiled=True)
    (sums,) = call(gather_kernel, (lax.axis_size(last),), sums, name="gather")
    sums = lax.all_to_all(sums, last, 0, 0, tiled=True)
    out, resid = call(update_kernel, (own, own), sums, v, resid, field, applied, name="update", work=2)
    return out.reshape(shape), resid.reshape(shape)


def solution(mesh):
    n_gx, n_gy, n_gz = mesh.devices.shape
    if n_gx == 64:
        mesh = Mesh(mesh.devices.reshape(4, 8, 2, n_gy, n_gz), ("gx_x", "gx_y", "gx_c", "gy", "gz"))
        gx = ("gx_x", "gx_y", "gx_c")
        splits = (("gx_x", "gx_y"), ("gx_c", "gy", "gz"))
    else:
        gx = "gx"
        splits = (("gx",), ("gy", "gz"))
    placed = P(gx, "gy", "gz")
    return jax.shard_map(
        functools.partial(on_device, gx, splits),
        mesh=mesh,
        in_specs=(placed,) * 3,
        out_specs=(placed,) * 2,
        check_vma=False,
    )
```

```python
import functools

import jax
import jax.numpy as jnp
import ml_dtypes
import numpy as np
from jax import lax
from jax.experimental import pallas as pl
from jax.experimental.pallas import tpu as pltpu
from jax.sharding import Mesh
from jax.sharding import PartitionSpec as P

OVER = 8
C = 40
CZ = 128
EXT = C + 2 * OVER
EXTZ = CZ + 2 * OVER
TILES = EXT // 8
stiff_scale = 3.0
mass_term = 0.001

F32 = jnp.float32
BF16 = jnp.bfloat16
VMEM = pl.BlockSpec(memory_space=pltpu.VMEM)
SMEM = pl.BlockSpec(memory_space=pltpu.SMEM)
HBM = pl.BlockSpec(memory_space=pltpu.HBM)

YROWS = 440
XROWS = 616
PER_Z = 12
BLOCKS_Z = -(-EXT // PER_Z)
ZROWS = BLOCKS_Z * EXT
PER = 14
XROWS2 = 9 * EXT + 40
YROWS2 = 416
ZGROUPS2 = 42 * 5 + 12
ZROWS2 = 8 * -(-ZGROUPS2 // PER)


def sine_table(count):
    k = np.arange(1, count + 1)
    basis = np.sqrt(2.0 / (count + 1)) * np.sin(np.pi * k[:, None] * k[None, :] / (count + 1))
    eigen = 2.0 - 2.0 * np.cos(np.pi * k / (count + 1))
    return basis, eigen


def two_parts(table):
    high = table.astype(ml_dtypes.bfloat16)
    low = (table - high.astype(np.float64)).astype(ml_dtypes.bfloat16)
    return high, low


@functools.cache
def tables():
    basis, eigen = sine_table(EXT)
    basis_z, eigen_z = sine_table(EXTZ)
    high, low = two_parts(basis)
    plane = np.zeros((EXT, 192), ml_dtypes.bfloat16)
    plane[:, 0:EXT] = high
    plane[:, 64 : 64 + EXT] = low
    plane[:, 128 : 128 + EXT] = high
    forward = np.zeros((2, 256, 256))
    inverse = np.zeros((2, 256, 256))
    for gz in range(2):
        own = basis_z[8 : 8 + CZ]
        strip = basis_z[136:144] if gz == 0 else basis_z[0:8]
        face_own, face_far = (135, 136) if gz == 0 else (8, 7)
        forward[gz, :CZ, :EXTZ] = own
        forward[gz, CZ, :EXTZ] = basis_z[face_own] - basis_z[face_far]
        forward[gz, CZ + 2 : CZ + 10, :EXTZ] = strip
        inverse[gz, :EXTZ, :CZ] = own.T
        inverse[gz, :EXTZ, CZ : CZ + 9] = (basis_z[135:144] if gz == 0 else basis_z[0:9]).T

    def stacked(table):
        high, low = two_parts(table)
        return np.concatenate([high, high, low], axis=1)

    denom = np.full((EXT, 256), 1.0)
    denom[:, :EXTZ] = stiff_scale * (eigen[:, None] + eigen_z[None, :]) + mass_term
    return (
        plane,
        stacked(forward),
        stacked(inverse),
        denom.astype(np.float32),
        (stiff_scale * eigen).astype(np.float32),
    )


def roll(value, shift, axis):
    if isinstance(shift, int):
        shift = shift % value.shape[axis]
        return value if shift == 0 else pltpu.roll(value, shift, axis)
    return pltpu.roll(value, lax.rem(shift + 2 * value.shape[axis], value.shape[axis]), axis)


def lanes(rows):
    return lax.broadcasted_iota(jnp.int32, (rows, CZ), 1)


def rows_at(start, size):
    return pl.ds(pl.multiple_of(start, 8), size)


def tile_at(index):
    return rows_at(index * 8, 8)


def call(body, out_rows, *args, scratch=(), limit=16, name=None, smem=(), hbm=(), work=0):
    place = {**{i: SMEM for i in smem}, **{i: HBM for i in hbm}}
    return pl.pallas_call(
        body,
        out_shape=[jax.ShapeDtypeStruct((rows, CZ), F32) for rows in out_rows],
        in_specs=[place.get(i, VMEM) for i in range(len(args))],
        out_specs=[VMEM] * len(out_rows),
        scratch_shapes=list(scratch),
        compiler_params=pltpu.CompilerParams(vmem_limit_bytes=limit * 2**20),
        cost_estimate=pl.CostEstimate(
            flops=int(work * 1e9), bytes_accessed=int(work * 2e6), transcendentals=0
        )
        if work
        else None,
        name=name,
    )(*args)


def strip_base():
    return jnp.where(lax.axis_index("gz") == 0, 118, 126)


def face_lane():
    return jnp.where(lax.axis_index("gz") == 0, 127, 0)


def outer_lane():
    return jnp.where(lax.axis_index("gz") == 0, 0, 127)


def pair_of(v, h, lane, base, face):
    return jnp.where(lane == base, roll(v, base - face, 1), 0.0) + jnp.where(
        lane == base + 1, roll(h, base + 1 - face, 1), 0.0
    )


def strips_kernel(v_in, h_in, b_in, up, down, v, h, b, sems):
    copies = []
    for k, (source, target, size) in enumerate(((v_in, v, 16), (h_in, h, 16), (b_in, b, 8))):
        for side, first in enumerate((0, C - size)):
            at = pl.ds(first, size)
            copies.append(
                pltpu.make_async_copy(source.at[:, at, :], target.at[:, at, :], sems.at[k, side])
            )
            copies[-1].start()
    base, face = strip_base(), face_lane()
    lane = lanes(8)
    row = lax.broadcasted_iota(jnp.int32, (8, CZ), 0)
    z_half = jnp.where(lane < CZ - 1, 0.5, 0.0)
    outer = jnp.where(lane == outer_lane(), 0.5, 0.0)
    last = C - 1
    for copy in copies:
        copy.wait()

    def tile(x, start, beyond, sign, flux_x):
        following = jnp.minimum(x + 1, last)
        at, to = pl.ds(start, 8), pl.ds(beyond, 8)
        vi, hi = v[x, at, :], h[x, at, :]
        next_x = 0.5 * (hi + h[following, at, :]) * (v[following, at, :] - vi)
        flux_y = 0.5 * (hi + h[x, to, :]) * (v[x, to, :] - vi)
        edge = 0 if sign > 0 else 7
        net_y = flux_y - jnp.where(row == edge, 0.0, roll(flux_y, sign, 0))
        flux_z = z_half * (hi + roll(hi, -1, 1)) * (roll(vi, -1, 1) - vi)
        applied = (
            mass_term * vi
            - (next_x - flux_x)
            - net_y
            - (flux_z - roll(flux_z, 1, 1))
            + outer * hi * vi
        )
        return b[x, at, :] - applied, next_x, vi, hi

    def visit(x, carry):
        flux_up, flux_down, pack_up, pack_down = carry
        resid, flux_down, vi, hi = tile(x, 0, 1, 1, flux_down)
        down[tile_at(x), :] = resid
        down[pl.ds(320 + x, 1), :] = vi[0:1]
        down[pl.ds(360 + x, 1), :] = hi[0:1]
        pack_down = pack_down + roll(pair_of(vi, hi, lane, base, face), 2 * x - base, 1)
        resid, flux_up, vi, hi = tile(x, 32, 31, -1, flux_up)
        up[tile_at(x), :] = resid
        up[pl.ds(320 + x, 1), :] = vi[7:8]
        up[pl.ds(360 + x, 1), :] = hi[7:8]
        pack_up = pack_up + roll(pair_of(vi, hi, lane, base, face), 2 * x - base, 1)
        return flux_up, flux_down, pack_up, pack_down

    zero = jnp.zeros((8, CZ), F32)
    _, _, pack_up, pack_down = lax.fori_loop(0, C, visit, (zero,) * 4, unroll=8)
    up[432:440, :] = pack_up
    down[432:440, :] = pack_down
    for message, first in ((up, 32), (down, 0)):
        at = pl.ds(first, 8)
        message[400:408, :] = v[0, at, :]
        message[408:416, :] = h[0, at, :]
        message[416:424, :] = v[last, at, :]
        message[424:432, :] = h[last, at, :]


def residual_kernel(v, h, b, part, edge):
    lane = lanes(C)
    row = lax.broadcasted_iota(jnp.int32, (C, CZ), 0)
    y_half = jnp.where(row > 0, 0.5, 0.0)
    z_half = jnp.where(lane < CZ - 1, 0.5, 0.0)
    outer = jnp.where(lane == outer_lane(), 0.5, 0.0)

    def visit(x, flux_x):
        own = rows_at(x * C, C)
        following = rows_at(jnp.minimum(x + 1, C - 1) * C, C)
        vi, hi = v[own, :], h[own, :]
        next_x = 0.5 * (hi + h[following, :]) * (v[following, :] - vi)
        flux_y = y_half * (hi + roll(hi, 1, 0)) * (vi - roll(vi, 1, 0))
        flux_z = z_half * (hi + roll(hi, -1, 1)) * (roll(vi, -1, 1) - vi)
        applied = (
            mass_term * vi
            - (next_x - flux_x)
            - (roll(flux_y, -1, 0) - flux_y)
            - (flux_z - roll(flux_z, 1, 1))
            + outer * hi * vi
        )
        part[own, :] = b[own, :] - applied
        return next_x

    lax.fori_loop(0, C, visit, jnp.zeros((C, CZ), F32), unroll=4)
    last = (C - 1) * C
    edge[0:40, :] = v[0:40, :]
    edge[40:80, :] = h[0:40, :]
    edge[80:120, :] = v[last : last + 40, :]
    edge[120:160, :] = h[last : last + 40, :]


def prepare_kernel(eigen, v, h, denom, out, out_a, out_b):
    base, face = strip_base(), face_lane()
    lane = lanes(C)

    def visit_pair(x, _):
        at = rows_at(x * C, C)
        out[at, :] = pair_of(v[at, :], h[at, :], lane, base, face)
        return 0

    lax.fori_loop(0, C, visit_pair, 0, unroll=8)

    def visit(y, _):
        value = 1.0 / (denom[...] + eigen[y])
        at = rows_at(y * EXT, EXT)
        out_a[at, :] = value[:, :CZ]
        out_b[at, :] = value[:, CZ:]
        return 0

    lax.fori_loop(0, EXT, visit, 0, unroll=4)


def choose(flag, a, b):
    return jnp.where(flag > 0.5, a, b)


def by_parity(flags, first, second):
    def before(start, stop):
        return choose(flags[4], second[start:stop, :], first[start:stop, :])

    def after(start, stop):
        return choose(flags[4], first[start:stop, :], second[start:stop, :])

    return before, after


def pick(pack, index, to):
    pair = lax.div(lanes(8), 2) == index
    return roll(jnp.where(pair, pack, 0.0), to - 2 * index, 1)


def strip_mask():
    lane = lanes(8)
    return jnp.where(lax.axis_index("gz") == 0, lane - 120, 7 - lane) >= 0


def y_fluxes(up, down, low, high):
    flux_a = 0.5 * (low[360:400, :] + down[360:400, :]) * (down[320:360, :] - low[320:360, :])
    flux_b = 0.5 * (up[360:400, :] + high[360:400, :]) * (high[320:360, :] - up[320:360, :])
    return flux_a, flux_b


def extend_y(flags, fluxes, part, low, high, out, start, stop):
    for x in range(start, stop):
        at = (x - start) * EXT
        out[at : at + 8, :] = low[8 * x : 8 * x + 8, :]
        out[at + 8 : at + 48, :] = part[x * C : x * C + C, :]
        out[at + 48 : at + 56, :] = high[8 * x : 8 * x + 8, :]
    flux_a, flux_b = (flux[start:stop] for flux in fluxes)
    for row, value in ((8, -flux_a), (7, flux_a * flags[2]), (47, flux_b), (48, -flux_b * flags[3])):
        at = pl.ds(row, stop - start, stride=EXT)
        out[at, :] = out[at, :] + value


def extend_y_kernel(flags, part, vh, up, down, edge, low, high, first, second, faces, right, left):
    base, strip_lanes = strip_base(), strip_mask()
    fluxes = y_fluxes(up, down, low, high)
    for message, start, strip, own in ((left, 0, 400, 0), (right, 32, 416, 80)):
        extend_y(flags, fluxes, part, low, high, message, start, start + OVER)
        for k in range(2):
            at = 448 + k * EXT
            message[at : at + 8, :] = low[strip + 8 * k : strip + 8 * k + 8, :]
            message[at + 8 : at + 48, :] = edge[own + 40 * k : own + 40 * k + 40, :]
            message[at + 48 : at + 56, :] = high[strip + 8 * k : strip + 8 * k + 8, :]
        for t in range(TILES):
            near = jnp.zeros((8, CZ), F32)
            taken = jnp.zeros((8, CZ), F32)
            for i in range(OVER):
                x = start + i
                at = i * EXT + 8 * t
                value = jnp.where(strip_lanes, message[at : at + 8, :], 0.0)
                if t == 0:
                    taken = taken + pick(low[432:440, :], x, 10 * i)
                elif t == 6:
                    taken = taken + pick(high[432:440, :], x, 10 * i)
                else:
                    value = value + vh[x * C + 8 * t - 8 : x * C + 8 * t, :]
                near = near + roll(value, 10 * i, 1)
            message[560 + 8 * t : 568 + 8 * t, :] = roll(near, -base, 1) + taken
    faces[0:112, :] = left[448:560, :]
    faces[112:224, :] = right[448:560, :]
    first[...] = choose(flags[4], right[...], left[...])
    second[...] = choose(flags[4], left[...], right[...])


def pack_z_kernel(part, vh, low, high, message):
    base, strip_lanes = strip_base(), strip_mask()
    for q in range(BLOCKS_Z):
        for t in range(TILES):
            near = jnp.zeros((8, CZ), F32)
            taken = jnp.zeros((8, CZ), F32)
            for j in range(PER_Z):
                x = q * PER_Z + j - OVER
                if not 0 <= x < C:
                    continue
                value = jnp.where(strip_lanes, part[x * EXT + 8 * t : x * EXT + 8 * t + 8, :], 0.0)
                if t == 0:
                    taken = taken + pick(low[432:440, :], x, 10 * j)
                elif t == 6:
                    taken = taken + pick(high[432:440, :], x, 10 * j)
                else:
                    value = value + vh[x * C + 8 * t - 8 : x * C + 8 * t, :]
                near = near + roll(value, 10 * j, 1)
            at = q * EXT + 8 * t
            message[at : at + 8, :] = roll(near, -base, 1) + taken


def extend_x_kernel(flags, packed, faces, first, second, inner, message, fluxes):
    base, strip_lanes = strip_base(), strip_mask()
    before, after = by_parity(flags, first, second)
    flux_a = 0.5 * (before(504, 560) + faces[56:112, :]) * (faces[0:56, :] - before(448, 504))
    flux_b = 0.5 * (faces[168:224, :] + after(504, 560)) * (after(448, 504) - faces[112:168, :])
    fluxes[0:EXT, :] = flux_a
    fluxes[EXT : 2 * EXT, :] = flux_b
    message[...] = packed[...]
    end = (BLOCKS_Z - 1) * EXT
    message[0:EXT, :] = message[0:EXT, :] + before(560, 616)
    message[end : end + EXT, :] = message[end : end + EXT, :] + after(560, 616)

    def add(x, t, value):
        q, j = divmod(x, PER_Z)
        at = q * EXT + 8 * t
        message[at : at + 8, :] = message[at : at + 8, :] + roll(value, 10 * j, 1)

    for t in range(TILES):
        a = roll(jnp.where(strip_lanes, flux_a[8 * t : 8 * t + 8], 0.0), -base, 1)
        b = roll(jnp.where(strip_lanes, flux_b[8 * t : 8 * t + 8], 0.0), -base, 1)
        add(OVER - 1, t, a * flags[0])
        add(OVER, t, -a)
        add(OVER + C - 1, t, b)
        add(OVER + C, t, -b * flags[1])


def halves(value):
    high = value.astype(BF16)
    return high, (value - high.astype(F32)).astype(BF16)


def dot(a, b):
    return jnp.dot(a, b, preferred_element_type=F32)


def along_lanes(value, table):
    high, low = halves(value)
    return dot(jnp.concatenate([high, low, high], axis=1), table)


def along_rows(table, value):
    padded = jnp.concatenate([value, jnp.zeros((8, value.shape[1]), F32)], axis=0)
    high, low = halves(padded)
    return dot(table, jnp.concatenate([high, high, low], axis=0))


def beside(a, b):
    return jnp.concatenate([a, b], axis=1)


def inner_kernel(flags, plane, box, up, down, low, high, out, part):
    table = plane[...]
    extend_y(flags, y_fluxes(up, down, low, high), box, low, high, part, 0, C)
    for x in range(1, C - 1, 2):
        at, then = pl.ds(x * EXT, EXT), pl.ds((x + 1) * EXT, EXT)
        value = along_rows(table, beside(part[at, :], part[then, :]))
        out[(x - 1) * EXT : x * EXT, :] = value[:, :CZ]
        out[x * EXT : (x + 1) * EXT, :] = value[:, CZ:]


def forward_kernel(flags, plane, part, inner, fluxes, one, two, out, first):
    before, after = by_parity(flags, one, two)
    table = plane[...]
    flux_a, flux_b = fluxes[0:EXT, :], fluxes[EXT : 2 * EXT, :]
    planes = {x: before(x * EXT, (x + 1) * EXT) for x in range(OVER)}
    planes[7] = planes[7] + flux_a * flags[0]
    planes[8] = part[0:EXT, :] - flux_a
    planes[47] = part[(C - 1) * EXT : C * EXT, :] + flux_b
    planes.update({48 + x: after(x * EXT, (x + 1) * EXT) for x in range(OVER)})
    planes[48] = planes[48] - flux_b * flags[1]
    first[9 * EXT : 47 * EXT, :] = inner[...]
    order = sorted(planes)
    for x, then in zip(order[0::2], order[1::2]):
        value = along_rows(table, beside(planes[x], planes[then]))
        first[x * EXT : (x + 1) * EXT, :] = value[:, :CZ]
        first[then * EXT : (then + 1) * EXT, :] = value[:, CZ:]

    def visit_x(c, _):
        for i in range(14):
            y = 2 * (c * 14 + i)
            value = beside(first[pl.ds(y, EXT, stride=EXT), :], first[pl.ds(y + 1, EXT, stride=EXT), :])
            value = along_rows(table, value)
            out[rows_at(y * EXT, EXT), :] = value[:, :CZ]
            out[rows_at((y + 1) * EXT, EXT), :] = value[:, CZ:]
        return 0

    lax.fori_loop(0, 2, visit_x, 0)


def face_terms(own_z, far_z):
    both = own_z[...] + far_z[...]
    half = 0.5 * roll(both, -1, 1)
    return half, half * (far_z[...] - own_z[...])


STEP = 28


def solve_kernel(
    flags, own_z, far_z, main, plane, forward, inverse, scale_a, scale_b,
    second_a, second_b, sol, strip, first, second, halo, right, left,
):
    gz = lax.axis_index("gz")
    table = plane[...]
    _, flux = face_terms(own_z, far_z)
    pack = jnp.where(lax.rem(lanes(ZROWS), 10) == 0, flux, far_z[...])
    blocks = [pack[q * EXT : (q + 1) * EXT] for q in range(BLOCKS_Z)]
    done = []
    for q in range(0, BLOCKS_Z - 1, 2):
        value = along_rows(table, beside(blocks[q], blocks[q + 1]))
        done += [value[:, :CZ], value[:, CZ:]]
    done.append(along_rows(table, blocks[-1]))
    for x in range(EXT):
        q, j = x // PER_Z, x % PER_Z
        halo[x * EXT : (x + 1) * EXT, :] = roll(done[q], -10 * j, 1)

    forward_table = forward[gz]
    inverse_table = inverse[gz]

    def visit(c, _):
        parts = []
        for i in range(0, STEP, 2):
            y = c * STEP + i
            value = beside(halo[pl.ds(y, EXT, stride=EXT), :], halo[pl.ds(y + 1, EXT, stride=EXT), :])
            value = along_rows(table, value)
            parts.append(beside(main[rows_at(y * EXT, EXT), :], value[:, :CZ]))
            parts.append(beside(main[rows_at((y + 1) * EXT, EXT), :], value[:, CZ:]))
        value = along_lanes(jnp.concatenate(parts, axis=0), forward_table)
        at = rows_at(c * STEP * EXT, STEP * EXT)
        value = value * beside(scale_a[at, :], scale_b[at, :])
        for i in range(STEP):
            part = along_rows(table, value[i * EXT : (i + 1) * EXT])
            to = pl.ds(c * STEP + i, EXT, stride=EXT)
            second_a[to, :] = part[:, :CZ]
            second_b[to, :] = part[:, CZ:]
        return 0

    lax.fori_loop(0, EXT // STEP, visit, 0)

    for k, (message, start) in enumerate(((left, 0), (right, 47))):
        inverse_planes(table, inverse_table, second_a, second_b, sol, strip, range(start, start + 9), 9 * k)
        message[0 : 9 * EXT, :] = sol[9 * k * EXT : 9 * (k + 1) * EXT, :]
        tiles = [strip[pl.ds((9 * k * TILES + j) * 8, 8), :] for j in range(63)]
        pack_tiles(message, 9 * EXT, tiles)
    first[...] = choose(flags[4], right[...], left[...])
    second[...] = choose(flags[4], left[...], right[...])


def inverse_planes(table, inverse_table, second_a, second_b, sol, strip, planes, to):
    parts = []
    for x in planes:
        at = pl.ds(x * EXT, EXT)
        parts.append(along_rows(table, beside(second_a[at, :], second_b[at, :])))
    value = along_lanes(jnp.concatenate(parts, axis=0), inverse_table)
    at = pl.ds(to * EXT, len(planes) * EXT)
    sol[at, :] = value[:, :CZ]
    strip[at, :] = value[:, CZ:]


def rest_kernel(plane, inverse, second_a, second_b, sides, side_strip, sol, strip):
    table, inverse_table = plane[...], inverse[lax.axis_index("gz")]
    for first, last in ((9, 19), (19, 29), (29, 38), (38, 47)):
        inverse_planes(
            table, inverse_table, second_a, second_b, sol, strip, range(first, last), first - 7
        )
    for target, source in ((sol, sides), (strip, side_strip)):
        target[0 : 2 * EXT, :] = source[7 * EXT : 9 * EXT, :]
        target[40 * EXT : 42 * EXT, :] = source[9 * EXT : 11 * EXT, :]


def own_kernel(flags, h, low, high, one, two, part, fluxes, own_z, far_z, resid, c_x, c_down, c_up, c_z, c_face, cond):
    face, outer = face_lane(), outer_lane()
    half, flux = face_terms(own_z, far_z)
    half, flux = roll(half, face, 1), roll(flux, face, 1)
    lane8 = lanes(8)
    for x in range(C):
        q, j = (x + OVER) // PER_Z, (x + OVER) % PER_Z
        for t in range(5):
            at = q * EXT + 8 * (t + 1)
            to = x * C + 8 * t
            source = x * EXT + 8 * (t + 1)
            moved = jnp.where(lane8 == face, roll(flux[at : at + 8], -10 * j, 1), 0.0)
            if x == 0:
                moved = moved - fluxes[source : source + 8, :]
            elif x == C - 1:
                moved = moved + fluxes[source + EXT - x * EXT : source + EXT - x * EXT + 8, :]
            resid[to : to + 8, :] = part[source : source + 8, :] + moved
            c_face[to : to + 8, :] = jnp.where(
                lane8 == face, roll(half[at : at + 8], -10 * j, 1), 0.0
            )
    before, after = by_parity(flags, one, two)
    cond[0:C, :] = before(512, 552)
    cond[C : C + C * C, :] = h[...]
    cond[C + C * C :, :] = after(512, 552)
    z_half = jnp.where(lanes(C) < CZ - 1, 0.5, 0.0)
    row = lax.broadcasted_iota(jnp.int32, (C, CZ), 0)
    for x in range(C):
        at = x * C
        hi = h[at : at + C, :]
        c_x[at : at + C, :] = 0.5 * (cond[at : at + C, :] + hi)
        below = jnp.where(row == 0, low[360 + x : 361 + x, :], roll(hi, 1, 0))
        above = jnp.where(row == C - 1, high[360 + x : 361 + x, :], roll(hi, -1, 0))
        c_down[at : at + C, :] = 0.5 * (hi + below)
        c_up[at : at + C, :] = 0.5 * (hi + above)
        c_z[at : at + C, :] = z_half * (hi + roll(hi, -1, 1))
    c_x[C * C :, :] = 0.5 * (cond[C * C : C * C + C, :] + cond[C * C + C :, :])


def pack_tiles(message, at, values):
    for q in range(-(-len(values) // PER)):
        acc = values[q * PER]
        for j, value in enumerate(values[q * PER + 1 : (q + 1) * PER], 1):
            acc = acc + roll(value, 9 * j, 1)
        message[at + 8 * q : at + 8 * q + 8, :] = acc


def unpack_tile(message, at, index):
    q = index // PER
    return roll(message[rows_at(at + 8 * q, 8), :], -9 * (index - q * PER), 1)


def fold_x_kernel(
    flags, sol, strip, one, two, _, out, up, down, across, across_up, across_down, out_strip, line
):
    size = 42 * EXT
    narrow = lanes(8) < 9
    before, after = by_parity(flags, one, two)
    tail = 33 * EXT
    out[0 : 9 * EXT, :] = sol[0 : 9 * EXT, :] + before(0, 9 * EXT)
    out[9 * EXT : tail, :] = sol[9 * EXT : tail, :]
    out[tail:size, :] = sol[tail:size, :] + after(0, 9 * EXT)
    out_strip[9 * EXT : tail, :] = strip[9 * EXT : tail, :]
    packs = [side(9 * EXT, XROWS2) for side in (before, after)]

    for j in range(63):
        q, i = divmod(j, PER)
        for pack, at in ((packs[0], 8 * j), (packs[1], tail + 8 * j)):
            value = jnp.where(narrow, roll(pack[8 * q : 8 * q + 8], -9 * i, 1), 0.0)
            out_strip[at : at + 8, :] = strip[at : at + 8, :] + value

    for array in (out, out_strip):
        array[0:EXT, :] = array[0:EXT, :] * flags[0]
        array[41 * EXT : size, :] = array[41 * EXT : size, :] * flags[1]

    for message, tile, single in ((up, 6, 47), (down, 0, 8)):
        for p in range(42):
            message[8 * p : 8 * p + 8, :] = out[p * EXT + 8 * tile : p * EXT + 8 * tile + 8, :]
        message[376:384, :] = jnp.zeros((8, CZ), F32)
        message[336:378, :] = out[pl.ds(single, 42, stride=EXT), :]
        line[40:48, :] = jnp.zeros((8, CZ), F32)
        line[0:42, :] = out_strip[pl.ds(single, 42, stride=EXT), :]
        values = [out_strip[p * EXT + 8 * tile : p * EXT + 8 * tile + 8, :] for p in range(42)]
        values += [line[8 * j : 8 * j + 8, :] for j in range(6)]
        pack_tiles(message, 384, values)
    across_up[...] = up[384:416, :]
    across_down[...] = down[384:416, :]
    values = []
    for p in range(42):
        for t in range(1, 6):
            at = p * EXT + 8 * t
            values.append(out_strip[at : at + 8, :])
    for k, single in enumerate((7, 48)):
        at = 48 * (k + 1)
        line[at + 40 : at + 48, :] = jnp.zeros((8, CZ), F32)
        line[at : at + 42, :] = out_strip[pl.ds(single, 42, stride=EXT), :] * flags[2 + k]
        values += [line[at + 8 * j : at + 8 * j + 8, :] for j in range(6)]
    pack_tiles(across, 0, values)


def fold_y_kernel(flags, sol, low, high, out):
    for p in range(42):
        for message, tile in ((low, 1), (high, 5)):
            at = p * EXT + 8 * tile
            out[at : at + 8, :] = sol[at : at + 8, :] + message[8 * p : 8 * p + 8, :]
        at = p * EXT
        out[at : at + 8, :] = sol[at : at + 8, :]
        out[at + 16 : at + 40, :] = sol[at + 16 : at + 40, :]
        out[at + 48 : at + 56, :] = sol[at + 48 : at + 56, :]
    for k, (single, message) in enumerate(((7, low), (48, high))):
        at = pl.ds(single, 42, stride=EXT)
        out[at, :] = (out[at, :] + message[336:378, :]) * flags[2 + k]


def apply_kernel(
    sol, low, high, own_z, far_z, far_low, far_high, resid, c_x, c_down, c_up, c_z, c_face, h,
    out, applied, sums, field, pack, line,
):
    gz = lax.axis_index("gz")
    end = YROWS2 - 384
    lane = lanes(ZROWS2 + 2 * end)
    at_face = lax.rem(lane, 9) == jnp.where(gz == 0, 8, 0)
    shift = jnp.where(gz == 0, 7, 121)
    near = jnp.concatenate([own_z[...], low[384:YROWS2, :], high[384:YROWS2, :]], axis=0)
    got = jnp.concatenate([far_z[...], far_low[...], far_high[...]], axis=0)
    got = got + jnp.where(at_face, roll(near, shift, 1), 0.0)
    pack[...] = roll(got, jnp.where(gz == 0, 120, 127), 1)
    toward = jnp.where(gz == 0, 127, 1)
    lane8 = lanes(8)
    folded = jnp.where(gz == 0, lane8 - 120, 7 - lane8) >= 0

    def tile(index, start=0):
        q, j = divmod(index, PER)
        return roll(pack[start + 8 * q : start + 8 * q + 8, :], -9 * j, 1)

    def along_z(p, t):
        value = tile(p * 5 + t - 1)
        if t == 1:
            value = value + tile(p, ZROWS2)
        if t == 5:
            value = value + tile(p, ZROWS2 + end)
        return value

    for p in range(42):
        for t in range(1, 6):
            at = p * EXT + 8 * t
            value = sol[at : at + 8, :] + jnp.where(folded, along_z(p, t), 0.0)
            field[at : at + 8, :] = value
    for k, single in enumerate((7, 48)):
        for j in range(6):
            value = tile(210 + 6 * k + j) + tile(42 + j, ZROWS2 + k * end)
            line[8 * j : 8 * j + 8, :] = jnp.where(folded, value, 0.0)
        at = pl.ds(single, 42, stride=EXT)
        field[at, :] = sol[at, :] + line[0:42, :]
    pack[...] = roll(pack[...], toward, 1)

    outer = jnp.where(lanes(C) == outer_lane(), 0.5, 0.0)
    flux_x = c_x[0:C, :] * (field[EXT + 8 : EXT + 48, :] - field[8:48, :])
    sum_a = jnp.zeros((8, CZ), F32)
    sum_b = jnp.zeros((8, CZ), F32)
    def visit(x, carry):
        flux_x, sum_a, sum_b = carry
        at = (x + 1) * EXT
        to = rows_at(x * C, C)
        z = field[rows_at(at + 8, C), :]
        next_x = c_x[rows_at(x * C + C, C), :] * (field[rows_at(at + EXT + 8, C), :] - z)
        net = next_x - flux_x
        net = net + c_up[to, :] * (field[pl.ds(at + 9, C), :] - z)
        net = net - c_down[to, :] * (z - field[pl.ds(at + 7, C), :])
        flux_z = c_z[to, :] * (roll(z, -1, 1) - z)
        net = net + (flux_z - roll(flux_z, 1, 1)) + c_face[to, :] * (out[to, :] - z)
        image = mass_term * z - net + outer * h[to, :] * z
        out[to, :] = z
        applied[to, :] = image
        a, b = resid[to, :] * z, z * image
        for t in range(5):
            sum_a = sum_a + a[8 * t : 8 * t + 8]
            sum_b = sum_b + b[8 * t : 8 * t + 8]
        return next_x, sum_a, sum_b

    for x in range(C):
        for t in range(5):
            out[x * C + 8 * t : x * C + 8 * t + 8, :] = along_z(x + 1, t + 1)
    _, sum_a, sum_b = lax.fori_loop(0, C, visit, (flux_x, sum_a, sum_b), unroll=8)
    total_a = jnp.sum(sum_a, axis=0, keepdims=True)
    total_b = jnp.sum(sum_b, axis=0, keepdims=True)
    total_a = total_a + roll(total_a, CZ // 2, 1)
    total_b = total_b + roll(total_b, CZ // 2, 1)
    total = jnp.where(lanes(1) < CZ // 2, total_a, total_b)
    sums[...] = jnp.broadcast_to(total, sums.shape)


def gather_kernel(sums, out):
    out[...] = jnp.broadcast_to(jnp.sum(sums[...], axis=0, keepdims=True), out.shape)


def update_kernel(sums, guess, resid, field, applied, solution_out, resid_out):
    total = jnp.sum(sums[...], axis=0, keepdims=True)
    first = lanes(1) < CZ // 2
    above = jnp.sum(jnp.where(first, total, 0.0), axis=1, keepdims=True)
    below = jnp.sum(jnp.where(first, 0.0, total), axis=1, keepdims=True)
    step = above / below
    solution_out[...] = guess[...] + step * field[...]
    resid_out[...] = resid[...] - step * applied[...]


def on_device(gx, splits, right_side, guess_field, conduct_field):
    shape = right_side.shape
    b, v, h = (a.reshape(C * C, CZ) for a in (right_side, guess_field, conduct_field))
    n_gx, n_gy = lax.axis_size(gx), lax.axis_size("gy")
    at_x, at_y = lax.axis_index(gx), lax.axis_index("gy")
    flags = jnp.stack([at_x > 0, at_x < n_gx - 1, at_y > 0, at_y < n_gy - 1, at_x % 2 == 1]).astype(F32)

    def exchange(axis, up, down):
        n = lax.axis_size(axis)
        forward = [(i, i + 1) for i in range(n - 1)]
        backward = [(i + 1, i) for i in range(n - 1)]
        return lax.ppermute(up, axis, forward), lax.ppermute(down, axis, backward)

    def exchange_x(first, second):
        pairs = [[(i + k, i + 1 - k) for i in range(start, n_gx - 1, 2) for k in (0, 1)] for start in (1, 0)]
        return lax.ppermute(first, gx, pairs[0]), lax.ppermute(second, gx, pairs[1])

    def swap(value):
        return lax.ppermute(value, "gz", [(0, 1), (1, 0)])

    plane, forward, inverse, denom, eigen = tables()
    own = C * C
    box = EXT * EXT

    def buffer(rows):
        return pltpu.VMEM((rows, CZ), F32)

    up, down = call(
        strips_kernel, (YROWS, YROWS), guess_field, conduct_field, right_side,
        scratch=[pltpu.VMEM((C, C, CZ), F32)] * 3 + [pltpu.SemaphoreType.DMA((3, 2))],
        hbm=(0, 1, 2), limit=56, name="strips", work=2,
    )
    part, edge = call(residual_kernel, (own, 160), v, h, b, name="residual", work=2)
    low, high = exchange("gy", up, down)
    pairs, scale_a, scale_b = call(
        prepare_kernel, (own, box, box), eigen, v, h, denom, smem=(0,), name="prepare", work=2
    )
    right, left, faces = call(
        extend_y_kernel, (XROWS, XROWS, 4 * EXT),
        flags, part, pairs, up, down, edge, low, high,
        scratch=[buffer(XROWS)] * 2, smem=(0,), name="extend_y", work=1,
    )
    one, two = exchange_x(right, left)
    inner, part = call(
        inner_kernel, (38 * EXT, C * EXT),
        flags, plane, part, up, down, low, high, smem=(0,), name="inner", work=1,
    )
    (packed,) = call(pack_z_kernel, (ZROWS,), part, pairs, low, high, name="pack_z", work=2)
    own_z, fluxes = call(
        extend_x_kernel, (ZROWS, 2 * EXT), flags, packed, faces, one, two, inner,
        smem=(0,), name="extend_x", work=1,
    )
    far_z = swap(own_z)
    (main,) = call(
        forward_kernel, (box,), flags, plane, part, inner, fluxes, one, two,
        scratch=[buffer(box)], smem=(0,), name="forward", work=2,
    )
    second_a, second_b, sides, side_strip, right, left = call(
        solve_kernel, (box, box, 18 * EXT, 18 * EXT, XROWS2, XROWS2),
        flags, own_z, far_z, main, plane, forward, inverse, scale_a, scale_b,
        scratch=[buffer(box), buffer(XROWS2), buffer(XROWS2)], smem=(0,), name="solve", work=6,
    )
    resid, c_x, c_down, c_up, c_z, c_face = call(
        own_kernel, (own, own + C, own, own, own, own),
        flags, h, low, high, one, two, part, fluxes, own_z, far_z,
        scratch=[buffer(own + 2 * C)], smem=(0,), name="own", work=2,
    )
    one, two = exchange_x(right, left)
    sol, strip = call(
        rest_kernel, (42 * EXT, 42 * EXT),
        plane, inverse, second_a, second_b, sides, side_strip, name="rest", work=2,
    )
    sol, up, down, own_z, across_up, across_down = call(
        fold_x_kernel, (42 * EXT, YROWS2, YROWS2, ZROWS2, 32, 32),
        flags, sol, strip, one, two, resid,
        scratch=[buffer(42 * EXT), buffer(144)], smem=(0,), name="fold_x", work=1,
    )
    low, high = exchange("gy", up, down)
    far_z = swap(own_z)
    diagonal = [((j, k), (j + 1, 1 - k)) for j in range(n_gy - 1) for k in range(2)]
    pairs = [(2 * a + b, 2 * c + d) for (a, b), (c, d) in diagonal]
    far_low = lax.ppermute(across_up, ("gy", "gz"), pairs)
    far_high = lax.ppermute(across_down, ("gy", "gz"), [(b, a) for a, b in pairs])
    (sol,) = call(
        fold_y_kernel, (42 * EXT,), flags, sol, low, high, smem=(0,), name="fold_y", work=1
    )
    first, last = splits
    field, applied, sums = call(
        apply_kernel, (own, own, lax.axis_size(first)),
        sol, low, high, own_z, far_z, far_low, far_high, resid, c_x, c_down, c_up, c_z, c_face, h,
        scratch=[buffer(42 * EXT), buffer(ZROWS2 + 64), buffer(48)], name="apply", work=3,
    )
    sums = lax.all_to_all(sums, first, 0, 0, tiled=True)
    (sums,) = call(gather_kernel, (lax.axis_size(last),), sums, name="gather")
    sums = lax.all_to_all(sums, last, 0, 0, tiled=True)
    out, resid = call(update_kernel, (own, own), sums, v, resid, field, applied, name="update", work=2)
    return out.reshape(shape), resid.reshape(shape)


def solution(mesh):
    n_gx, n_gy, n_gz = mesh.devices.shape
    if n_gx == 64:
        mesh = Mesh(mesh.devices.reshape(4, 8, 2, n_gy, n_gz), ("gx_x", "gx_y", "gx_c", "gy", "gz"))
        gx = ("gx_x", "gx_y", "gx_c")
        splits = (("gx_c", "gy", "gz"), ("gx_x", "gx_y"))
    else:
        gx = "gx"
        splits = (("gx",), ("gy", "gz"))
    placed = P(gx, "gy", "gz")
    return jax.shard_map(
        functools.partial(on_device, gx, splits),
        mesh=mesh,
        in_specs=(placed,) * 3,
        out_specs=(placed,) * 2,
        check_vma=False,
    )
```

```python
import functools

import jax
import jax.numpy as jnp
import ml_dtypes
import numpy as np
from jax import lax
from jax.experimental import pallas as pl
from jax.experimental.pallas import tpu as pltpu
from jax.sharding import Mesh
from jax.sharding import PartitionSpec as P

OVER = 8
C = 40
CZ = 128
EXT = C + 2 * OVER
EXTZ = CZ + 2 * OVER
TILES = EXT // 8
stiff_scale = 3.0
mass_term = 0.001

F32 = jnp.float32
BF16 = jnp.bfloat16
VMEM = pl.BlockSpec(memory_space=pltpu.VMEM)
SMEM = pl.BlockSpec(memory_space=pltpu.SMEM)
HBM = pl.BlockSpec(memory_space=pltpu.HBM)

YROWS = 440
XROWS = 616
PER_Z = 12
BLOCKS_Z = -(-EXT // PER_Z)
ZROWS = BLOCKS_Z * EXT
PER = 14
XROWS2 = 9 * EXT + 40
YROWS2 = 416
ZGROUPS2 = 42 * 5 + 12
ZROWS2 = 8 * -(-ZGROUPS2 // PER)


def sine_table(count):
    k = np.arange(1, count + 1)
    basis = np.sqrt(2.0 / (count + 1)) * np.sin(np.pi * k[:, None] * k[None, :] / (count + 1))
    eigen = 2.0 - 2.0 * np.cos(np.pi * k / (count + 1))
    return basis, eigen


def two_parts(table):
    high = table.astype(ml_dtypes.bfloat16)
    low = (table - high.astype(np.float64)).astype(ml_dtypes.bfloat16)
    return high, low


@functools.cache
def tables():
    basis, eigen = sine_table(EXT)
    basis_z, eigen_z = sine_table(EXTZ)
    high, low = two_parts(basis)
    plane = np.zeros((EXT, 192), ml_dtypes.bfloat16)
    plane[:, 0:EXT] = high
    plane[:, 64 : 64 + EXT] = low
    plane[:, 128 : 128 + EXT] = high
    forward = np.zeros((2, 256, 256))
    inverse = np.zeros((2, 256, 256))
    for gz in range(2):
        own = basis_z[8 : 8 + CZ]
        strip = basis_z[136:144] if gz == 0 else basis_z[0:8]
        face_own, face_far = (135, 136) if gz == 0 else (8, 7)
        forward[gz, :CZ, :EXTZ] = own
        forward[gz, CZ, :EXTZ] = basis_z[face_own] - basis_z[face_far]
        forward[gz, CZ + 2 : CZ + 10, :EXTZ] = strip
        inverse[gz, :EXTZ, :CZ] = own.T
        inverse[gz, :EXTZ, CZ : CZ + 9] = (basis_z[135:144] if gz == 0 else basis_z[0:9]).T

    def stacked(table):
        high, low = two_parts(table)
        return np.concatenate([high, high, low], axis=1)

    denom = np.full((EXT, 256), 1.0)
    denom[:, :EXTZ] = stiff_scale * (eigen[:, None] + eigen_z[None, :]) + mass_term
    return (
        plane,
        stacked(forward),
        stacked(inverse),
        denom.astype(np.float32),
        (stiff_scale * eigen).astype(np.float32),
    )


def roll(value, shift, axis):
    if isinstance(shift, int):
        shift = shift % value.shape[axis]
        return value if shift == 0 else pltpu.roll(value, shift, axis)
    return pltpu.roll(value, lax.rem(shift + 2 * value.shape[axis], value.shape[axis]), axis)


def lanes(rows):
    return lax.broadcasted_iota(jnp.int32, (rows, CZ), 1)


def rows_at(start, size):
    return pl.ds(pl.multiple_of(start, 8), size)


def tile_at(index):
    return rows_at(index * 8, 8)


def call(body, out_rows, *args, scratch=(), limit=16, name=None, smem=(), hbm=(), work=0):
    place = {**{i: SMEM for i in smem}, **{i: HBM for i in hbm}}
    return pl.pallas_call(
        body,
        out_shape=[jax.ShapeDtypeStruct((rows, CZ), F32) for rows in out_rows],
        in_specs=[place.get(i, VMEM) for i in range(len(args))],
        out_specs=[VMEM] * len(out_rows),
        scratch_shapes=list(scratch),
        compiler_params=pltpu.CompilerParams(vmem_limit_bytes=limit * 2**20),
        cost_estimate=pl.CostEstimate(
            flops=int(work * 1e9), bytes_accessed=int(work * 2e6), transcendentals=0
        )
        if work
        else None,
        name=name,
    )(*args)


def strip_base():
    return jnp.where(lax.axis_index("gz") == 0, 118, 126)


def face_lane():
    return jnp.where(lax.axis_index("gz") == 0, 127, 0)


def outer_lane():
    return jnp.where(lax.axis_index("gz") == 0, 0, 127)


def pair_of(v, h, lane, base, face):
    return jnp.where(lane == base, roll(v, base - face, 1), 0.0) + jnp.where(
        lane == base + 1, roll(h, base + 1 - face, 1), 0.0
    )


def strips_kernel(v_in, h_in, b_in, up, down, v, h, b, sems):
    copies = []
    for k, (source, target, size) in enumerate(((v_in, v, 16), (h_in, h, 16), (b_in, b, 8))):
        for side, first in enumerate((0, C - size)):
            at = pl.ds(first, size)
            copies.append(
                pltpu.make_async_copy(source.at[:, at, :], target.at[:, at, :], sems.at[k, side])
            )
            copies[-1].start()
    base, face = strip_base(), face_lane()
    lane = lanes(8)
    row = lax.broadcasted_iota(jnp.int32, (8, CZ), 0)
    z_half = jnp.where(lane < CZ - 1, 0.5, 0.0)
    outer = jnp.where(lane == outer_lane(), 0.5, 0.0)
    last = C - 1
    for copy in copies:
        copy.wait()

    def tile(x, start, beyond, sign, flux_x):
        following = jnp.minimum(x + 1, last)
        at, to = pl.ds(start, 8), pl.ds(beyond, 8)
        vi, hi = v[x, at, :], h[x, at, :]
        next_x = 0.5 * (hi + h[following, at, :]) * (v[following, at, :] - vi)
        flux_y = 0.5 * (hi + h[x, to, :]) * (v[x, to, :] - vi)
        edge = 0 if sign > 0 else 7
        net_y = flux_y - jnp.where(row == edge, 0.0, roll(flux_y, sign, 0))
        flux_z = z_half * (hi + roll(hi, -1, 1)) * (roll(vi, -1, 1) - vi)
        applied = (
            mass_term * vi
            - (next_x - flux_x)
            - net_y
            - (flux_z - roll(flux_z, 1, 1))
            + outer * hi * vi
        )
        return b[x, at, :] - applied, next_x, vi, hi

    def visit(x, carry):
        flux_up, flux_down, pack_up, pack_down = carry
        resid, flux_down, vi, hi = tile(x, 0, 1, 1, flux_down)
        down[tile_at(x), :] = resid
        down[pl.ds(320 + x, 1), :] = vi[0:1]
        down[pl.ds(360 + x, 1), :] = hi[0:1]
        pack_down = pack_down + roll(pair_of(vi, hi, lane, base, face), 2 * x - base, 1)
        resid, flux_up, vi, hi = tile(x, 32, 31, -1, flux_up)
        up[tile_at(x), :] = resid
        up[pl.ds(320 + x, 1), :] = vi[7:8]
        up[pl.ds(360 + x, 1), :] = hi[7:8]
        pack_up = pack_up + roll(pair_of(vi, hi, lane, base, face), 2 * x - base, 1)
        return flux_up, flux_down, pack_up, pack_down

    zero = jnp.zeros((8, CZ), F32)
    _, _, pack_up, pack_down = lax.fori_loop(0, C, visit, (zero,) * 4, unroll=8)
    up[432:440, :] = pack_up
    down[432:440, :] = pack_down
    for message, first in ((up, 32), (down, 0)):
        at = pl.ds(first, 8)
        message[400:408, :] = v[0, at, :]
        message[408:416, :] = h[0, at, :]
        message[416:424, :] = v[last, at, :]
        message[424:432, :] = h[last, at, :]


def residual_kernel(v, h, b, part, edge):
    lane = lanes(C)
    row = lax.broadcasted_iota(jnp.int32, (C, CZ), 0)
    y_half = jnp.where(row > 0, 0.5, 0.0)
    z_half = jnp.where(lane < CZ - 1, 0.5, 0.0)
    outer = jnp.where(lane == outer_lane(), 0.5, 0.0)

    def visit(x, flux_x):
        own = rows_at(x * C, C)
        following = rows_at(jnp.minimum(x + 1, C - 1) * C, C)
        vi, hi = v[own, :], h[own, :]
        next_x = 0.5 * (hi + h[following, :]) * (v[following, :] - vi)
        flux_y = y_half * (hi + roll(hi, 1, 0)) * (vi - roll(vi, 1, 0))
        flux_z = z_half * (hi + roll(hi, -1, 1)) * (roll(vi, -1, 1) - vi)
        applied = (
            mass_term * vi
            - (next_x - flux_x)
            - (roll(flux_y, -1, 0) - flux_y)
            - (flux_z - roll(flux_z, 1, 1))
            + outer * hi * vi
        )
        part[own, :] = b[own, :] - applied
        return next_x

    lax.fori_loop(0, C, visit, jnp.zeros((C, CZ), F32), unroll=4)
    last = (C - 1) * C
    edge[0:40, :] = v[0:40, :]
    edge[40:80, :] = h[0:40, :]
    edge[80:120, :] = v[last : last + 40, :]
    edge[120:160, :] = h[last : last + 40, :]


def prepare_kernel(eigen, v, h, denom, out, out_a, out_b):
    base, face = strip_base(), face_lane()
    lane = lanes(C)

    def visit_pair(x, _):
        at = rows_at(x * C, C)
        out[at, :] = pair_of(v[at, :], h[at, :], lane, base, face)
        return 0

    lax.fori_loop(0, C, visit_pair, 0, unroll=8)

    def visit(y, _):
        value = 1.0 / (denom[...] + eigen[y])
        at = rows_at(y * EXT, EXT)
        out_a[at, :] = value[:, :CZ]
        out_b[at, :] = value[:, CZ:]
        return 0

    lax.fori_loop(0, EXT, visit, 0, unroll=4)


def choose(flag, a, b):
    return jnp.where(flag > 0.5, a, b)


def by_parity(flags, first, second):
    def before(start, stop):
        return choose(flags[4], second[start:stop, :], first[start:stop, :])

    def after(start, stop):
        return choose(flags[4], first[start:stop, :], second[start:stop, :])

    return before, after


def pick(pack, index, to):
    pair = lax.div(lanes(8), 2) == index
    return roll(jnp.where(pair, pack, 0.0), to - 2 * index, 1)


def strip_mask():
    lane = lanes(8)
    return jnp.where(lax.axis_index("gz") == 0, lane - 120, 7 - lane) >= 0


def y_fluxes(up, down, low, high):
    flux_a = 0.5 * (low[360:400, :] + down[360:400, :]) * (down[320:360, :] - low[320:360, :])
    flux_b = 0.5 * (up[360:400, :] + high[360:400, :]) * (high[320:360, :] - up[320:360, :])
    return flux_a, flux_b


def extend_y(flags, fluxes, part, low, high, out, start, stop):
    for x in range(start, stop):
        at = (x - start) * EXT
        out[at : at + 8, :] = low[8 * x : 8 * x + 8, :]
        out[at + 8 : at + 48, :] = part[x * C : x * C + C, :]
        out[at + 48 : at + 56, :] = high[8 * x : 8 * x + 8, :]
    flux_a, flux_b = (flux[start:stop] for flux in fluxes)
    for row, value in ((8, -flux_a), (7, flux_a * flags[2]), (47, flux_b), (48, -flux_b * flags[3])):
        at = pl.ds(row, stop - start, stride=EXT)
        out[at, :] = out[at, :] + value


def extend_y_kernel(flags, part, vh, up, down, edge, low, high, _, first, second, faces, right, left):
    base, strip_lanes = strip_base(), strip_mask()
    fluxes = y_fluxes(up, down, low, high)
    for message, start, strip, own in ((left, 0, 400, 0), (right, 32, 416, 80)):
        extend_y(flags, fluxes, part, low, high, message, start, start + OVER)
        for k in range(2):
            at = 448 + k * EXT
            message[at : at + 8, :] = low[strip + 8 * k : strip + 8 * k + 8, :]
            message[at + 8 : at + 48, :] = edge[own + 40 * k : own + 40 * k + 40, :]
            message[at + 48 : at + 56, :] = high[strip + 8 * k : strip + 8 * k + 8, :]
        for t in range(TILES):
            near = jnp.zeros((8, CZ), F32)
            taken = jnp.zeros((8, CZ), F32)
            for i in range(OVER):
                x = start + i
                at = i * EXT + 8 * t
                value = jnp.where(strip_lanes, message[at : at + 8, :], 0.0)
                if t == 0:
                    taken = taken + pick(low[432:440, :], x, 10 * i)
                elif t == 6:
                    taken = taken + pick(high[432:440, :], x, 10 * i)
                else:
                    value = value + vh[x * C + 8 * t - 8 : x * C + 8 * t, :]
                near = near + roll(value, 10 * i, 1)
            message[560 + 8 * t : 568 + 8 * t, :] = roll(near, -base, 1) + taken
    faces[0:112, :] = left[448:560, :]
    faces[112:224, :] = right[448:560, :]
    first[...] = choose(flags[4], right[...], left[...])
    second[...] = choose(flags[4], left[...], right[...])


def pack_planes(tiles, value_of, taken_of):
    base = strip_base()
    packs = {}
    for q in range(BLOCKS_Z):
        for t in tiles:
            near = jnp.zeros((8, CZ), F32)
            taken = jnp.zeros((8, CZ), F32)
            for j in range(PER_Z):
                x = q * PER_Z + j - OVER
                if 0 <= x < C:
                    near = near + roll(value_of(x, t), 10 * j, 1)
                    if t in (0, 6):
                        taken = taken + taken_of(x, t, 10 * j)
            packs[q, t] = roll(near, -base, 1) + taken
    return packs


def pack_middle_kernel(part, vh, out):
    strip_lanes = strip_mask()

    def value_of(x, t):
        at = pl.ds(x * C + 8 * t - 8, 8)
        return jnp.where(strip_lanes, part[at, :], 0.0) + vh[at, :]

    for (q, t), value in pack_planes((2, 3, 4), value_of, None).items():
        at = q * 24 + 8 * (t - 2)
        out[at : at + 8, :] = value


def pack_z_kernel(part, vh, low, high, middle, message):
    strip_lanes = strip_mask()

    def value_of(x, t):
        value = jnp.where(strip_lanes, part[x * EXT + 8 * t : x * EXT + 8 * t + 8, :], 0.0)
        if t in (1, 5):
            value = value + vh[x * C + 8 * t - 8 : x * C + 8 * t, :]
        return value

    def taken_of(x, t, lane):
        return pick((low if t == 0 else high)[432:440, :], x, lane)

    for q in range(BLOCKS_Z):
        message[q * EXT + 16 : q * EXT + 40, :] = middle[24 * q : 24 * q + 24, :]
    for (q, t), value in pack_planes((0, 1, 5, 6), value_of, taken_of).items():
        at = q * EXT + 8 * t
        message[at : at + 8, :] = value


def extend_x_kernel(flags, packed, faces, first, second, inner, message, fluxes):
    base, strip_lanes = strip_base(), strip_mask()
    before, after = by_parity(flags, first, second)
    flux_a = 0.5 * (before(504, 560) + faces[56:112, :]) * (faces[0:56, :] - before(448, 504))
    flux_b = 0.5 * (faces[168:224, :] + after(504, 560)) * (after(448, 504) - faces[112:168, :])
    fluxes[0:EXT, :] = flux_a
    fluxes[EXT : 2 * EXT, :] = flux_b
    message[...] = packed[...]
    end = (BLOCKS_Z - 1) * EXT
    message[0:EXT, :] = message[0:EXT, :] + before(560, 616)
    message[end : end + EXT, :] = message[end : end + EXT, :] + after(560, 616)

    def add(x, t, value):
        q, j = divmod(x, PER_Z)
        at = q * EXT + 8 * t
        message[at : at + 8, :] = message[at : at + 8, :] + roll(value, 10 * j, 1)

    for t in range(TILES):
        a = roll(jnp.where(strip_lanes, flux_a[8 * t : 8 * t + 8], 0.0), -base, 1)
        b = roll(jnp.where(strip_lanes, flux_b[8 * t : 8 * t + 8], 0.0), -base, 1)
        add(OVER - 1, t, a * flags[0])
        add(OVER, t, -a)
        add(OVER + C - 1, t, b)
        add(OVER + C, t, -b * flags[1])


def halves(value):
    high = value.astype(BF16)
    return high, (value - high.astype(F32)).astype(BF16)


def dot(a, b):
    return jnp.dot(a, b, preferred_element_type=F32)


def along_lanes(value, table):
    high, low = halves(value)
    return dot(jnp.concatenate([high, low, high], axis=1), table)


def along_rows(table, value):
    padded = jnp.concatenate([value, jnp.zeros((8, value.shape[1]), F32)], axis=0)
    high, low = halves(padded)
    return dot(table, jnp.concatenate([high, high, low], axis=0))


def beside(a, b):
    return jnp.concatenate([a, b], axis=1)


def inner_kernel(flags, plane, box, up, down, low, high, out, part):
    table = plane[...]
    extend_y(flags, y_fluxes(up, down, low, high), box, low, high, part, 0, C)
    for x in range(1, C - 1, 2):
        at, then = pl.ds(x * EXT, EXT), pl.ds((x + 1) * EXT, EXT)
        value = along_rows(table, beside(part[at, :], part[then, :]))
        out[(x - 1) * EXT : x * EXT, :] = value[:, :CZ]
        out[x * EXT : (x + 1) * EXT, :] = value[:, CZ:]


def forward_kernel(flags, plane, part, inner, fluxes, one, two, out, first):
    before, after = by_parity(flags, one, two)
    table = plane[...]
    flux_a, flux_b = fluxes[0:EXT, :], fluxes[EXT : 2 * EXT, :]
    planes = {x: before(x * EXT, (x + 1) * EXT) for x in range(OVER)}
    planes[7] = planes[7] + flux_a * flags[0]
    planes[8] = part[0:EXT, :] - flux_a
    planes[47] = part[(C - 1) * EXT : C * EXT, :] + flux_b
    planes.update({48 + x: after(x * EXT, (x + 1) * EXT) for x in range(OVER)})
    planes[48] = planes[48] - flux_b * flags[1]
    first[9 * EXT : 47 * EXT, :] = inner[...]
    order = sorted(planes)
    for x, then in zip(order[0::2], order[1::2]):
        value = along_rows(table, beside(planes[x], planes[then]))
        first[x * EXT : (x + 1) * EXT, :] = value[:, :CZ]
        first[then * EXT : (then + 1) * EXT, :] = value[:, CZ:]

    def visit_x(c, _):
        for i in range(14):
            y = 2 * (c * 14 + i)
            value = beside(first[pl.ds(y, EXT, stride=EXT), :], first[pl.ds(y + 1, EXT, stride=EXT), :])
            value = along_rows(table, value)
            out[rows_at(y * EXT, EXT), :] = value[:, :CZ]
            out[rows_at((y + 1) * EXT, EXT), :] = value[:, CZ:]
        return 0

    lax.fori_loop(0, 2, visit_x, 0)


def face_terms(own_z, far_z):
    both = own_z[...] + far_z[...]
    half = 0.5 * roll(both, -1, 1)
    return half, half * (far_z[...] - own_z[...])


STEP = 28


def solve_kernel(
    flags, own_z, far_z, main, plane, forward, inverse, scale_a, scale_b,
    second_a, second_b, sol, strip, first, second, halo, right, left,
):
    gz = lax.axis_index("gz")
    table = plane[...]
    _, flux = face_terms(own_z, far_z)
    pack = jnp.where(lax.rem(lanes(ZROWS), 10) == 0, flux, far_z[...])
    blocks = [pack[q * EXT : (q + 1) * EXT] for q in range(BLOCKS_Z)]
    done = []
    for q in range(0, BLOCKS_Z - 1, 2):
        value = along_rows(table, beside(blocks[q], blocks[q + 1]))
        done += [value[:, :CZ], value[:, CZ:]]
    done.append(along_rows(table, blocks[-1]))
    for x in range(EXT):
        q, j = x // PER_Z, x % PER_Z
        halo[x * EXT : (x + 1) * EXT, :] = roll(done[q], -10 * j, 1)

    forward_table = forward[gz]
    inverse_table = inverse[gz]

    def visit(c, _):
        parts = []
        for i in range(0, STEP, 2):
            y = c * STEP + i
            value = beside(halo[pl.ds(y, EXT, stride=EXT), :], halo[pl.ds(y + 1, EXT, stride=EXT), :])
            value = along_rows(table, value)
            parts.append(beside(main[rows_at(y * EXT, EXT), :], value[:, :CZ]))
            parts.append(beside(main[rows_at((y + 1) * EXT, EXT), :], value[:, CZ:]))
        value = along_lanes(jnp.concatenate(parts, axis=0), forward_table)
        at = rows_at(c * STEP * EXT, STEP * EXT)
        value = value * beside(scale_a[at, :], scale_b[at, :])
        for i in range(STEP):
            part = along_rows(table, value[i * EXT : (i + 1) * EXT])
            to = pl.ds(c * STEP + i, EXT, stride=EXT)
            second_a[to, :] = part[:, :CZ]
            second_b[to, :] = part[:, CZ:]
        return 0

    lax.fori_loop(0, EXT // STEP, visit, 0)

    for k, (message, start) in enumerate(((left, 0), (right, 47))):
        inverse_planes(table, inverse_table, second_a, second_b, sol, strip, range(start, start + 9), 9 * k)
        message[0 : 9 * EXT, :] = sol[9 * k * EXT : 9 * (k + 1) * EXT, :]
        tiles = [strip[pl.ds((9 * k * TILES + j) * 8, 8), :] for j in range(63)]
        pack_tiles(message, 9 * EXT, tiles)
    first[...] = choose(flags[4], right[...], left[...])
    second[...] = choose(flags[4], left[...], right[...])


def inverse_planes(table, inverse_table, second_a, second_b, sol, strip, planes, to):
    parts = []
    for x in planes:
        at = pl.ds(x * EXT, EXT)
        parts.append(along_rows(table, beside(second_a[at, :], second_b[at, :])))
    value = along_lanes(jnp.concatenate(parts, axis=0), inverse_table)
    at = pl.ds(to * EXT, len(planes) * EXT)
    sol[at, :] = value[:, :CZ]
    strip[at, :] = value[:, CZ:]


def rest_kernel(plane, inverse, second_a, second_b, sides, side_strip, sol, strip):
    table, inverse_table = plane[...], inverse[lax.axis_index("gz")]
    for first, last in ((9, 19), (19, 29), (29, 38), (38, 47)):
        inverse_planes(
            table, inverse_table, second_a, second_b, sol, strip, range(first, last), first - 7
        )
    for target, source in ((sol, sides), (strip, side_strip)):
        target[0 : 2 * EXT, :] = source[7 * EXT : 9 * EXT, :]
        target[40 * EXT : 42 * EXT, :] = source[9 * EXT : 11 * EXT, :]


def own_kernel(flags, h, low, high, one, two, part, fluxes, own_z, far_z, resid, c_x, c_down, c_up, c_z, c_face, cond):
    face, outer = face_lane(), outer_lane()
    half, flux = face_terms(own_z, far_z)
    half, flux = roll(half, face, 1), roll(flux, face, 1)
    lane8 = lanes(8)
    for x in range(C):
        q, j = (x + OVER) // PER_Z, (x + OVER) % PER_Z
        for t in range(5):
            at = q * EXT + 8 * (t + 1)
            to = x * C + 8 * t
            source = x * EXT + 8 * (t + 1)
            moved = jnp.where(lane8 == face, roll(flux[at : at + 8], -10 * j, 1), 0.0)
            if x == 0:
                moved = moved - fluxes[source : source + 8, :]
            elif x == C - 1:
                moved = moved + fluxes[source + EXT - x * EXT : source + EXT - x * EXT + 8, :]
            resid[to : to + 8, :] = part[source : source + 8, :] + moved
            c_face[to : to + 8, :] = jnp.where(
                lane8 == face, roll(half[at : at + 8], -10 * j, 1), 0.0
            )
    before, after = by_parity(flags, one, two)
    cond[0:C, :] = before(512, 552)
    cond[C : C + C * C, :] = h[...]
    cond[C + C * C :, :] = after(512, 552)
    z_half = jnp.where(lanes(C) < CZ - 1, 0.5, 0.0)
    row = lax.broadcasted_iota(jnp.int32, (C, CZ), 0)
    for x in range(C):
        at = x * C
        hi = h[at : at + C, :]
        c_x[at : at + C, :] = 0.5 * (cond[at : at + C, :] + hi)
        below = jnp.where(row == 0, low[360 + x : 361 + x, :], roll(hi, 1, 0))
        above = jnp.where(row == C - 1, high[360 + x : 361 + x, :], roll(hi, -1, 0))
        c_down[at : at + C, :] = 0.5 * (hi + below)
        c_up[at : at + C, :] = 0.5 * (hi + above)
        c_z[at : at + C, :] = z_half * (hi + roll(hi, -1, 1))
    c_x[C * C :, :] = 0.5 * (cond[C * C : C * C + C, :] + cond[C * C + C :, :])


def pack_tiles(message, at, values):
    for q in range(-(-len(values) // PER)):
        acc = values[q * PER]
        for j, value in enumerate(values[q * PER + 1 : (q + 1) * PER], 1):
            acc = acc + roll(value, 9 * j, 1)
        message[at + 8 * q : at + 8 * q + 8, :] = acc


def unpack_tile(message, at, index):
    q = index // PER
    return roll(message[rows_at(at + 8 * q, 8), :], -9 * (index - q * PER), 1)


def fold_x_kernel(
    flags, sol, strip, one, two, _, out, up, down, across, across_up, across_down, out_strip, line
):
    size = 42 * EXT
    narrow = lanes(8) < 9
    before, after = by_parity(flags, one, two)
    tail = 33 * EXT
    out[0 : 9 * EXT, :] = sol[0 : 9 * EXT, :] + before(0, 9 * EXT)
    out[9 * EXT : tail, :] = sol[9 * EXT : tail, :]
    out[tail:size, :] = sol[tail:size, :] + after(0, 9 * EXT)
    out_strip[9 * EXT : tail, :] = strip[9 * EXT : tail, :]
    packs = [side(9 * EXT, XROWS2) for side in (before, after)]

    for j in range(63):
        q, i = divmod(j, PER)
        for pack, at in ((packs[0], 8 * j), (packs[1], tail + 8 * j)):
            value = jnp.where(narrow, roll(pack[8 * q : 8 * q + 8], -9 * i, 1), 0.0)
            out_strip[at : at + 8, :] = strip[at : at + 8, :] + value

    for array in (out, out_strip):
        array[0:EXT, :] = array[0:EXT, :] * flags[0]
        array[41 * EXT : size, :] = array[41 * EXT : size, :] * flags[1]

    for message, tile, single in ((up, 6, 47), (down, 0, 8)):
        for p in range(42):
            message[8 * p : 8 * p + 8, :] = out[p * EXT + 8 * tile : p * EXT + 8 * tile + 8, :]
        message[376:384, :] = jnp.zeros((8, CZ), F32)
        message[336:378, :] = out[pl.ds(single, 42, stride=EXT), :]
        line[40:48, :] = jnp.zeros((8, CZ), F32)
        line[0:42, :] = out_strip[pl.ds(single, 42, stride=EXT), :]
        values = [out_strip[p * EXT + 8 * tile : p * EXT + 8 * tile + 8, :] for p in range(42)]
        values += [line[8 * j : 8 * j + 8, :] for j in range(6)]
        pack_tiles(message, 384, values)
    across_up[...] = up[384:416, :]
    across_down[...] = down[384:416, :]
    values = []
    for p in range(42):
        for t in range(1, 6):
            at = p * EXT + 8 * t
            values.append(out_strip[at : at + 8, :])
    for k, single in enumerate((7, 48)):
        at = 48 * (k + 1)
        line[at + 40 : at + 48, :] = jnp.zeros((8, CZ), F32)
        line[at : at + 42, :] = out_strip[pl.ds(single, 42, stride=EXT), :] * flags[2 + k]
        values += [line[at + 8 * j : at + 8 * j + 8, :] for j in range(6)]
    pack_tiles(across, 0, values)


def fold_y_kernel(flags, sol, low, high, out):
    for p in range(42):
        for message, tile in ((low, 1), (high, 5)):
            at = p * EXT + 8 * tile
            out[at : at + 8, :] = sol[at : at + 8, :] + message[8 * p : 8 * p + 8, :]
        at = p * EXT
        out[at : at + 8, :] = sol[at : at + 8, :]
        out[at + 16 : at + 40, :] = sol[at + 16 : at + 40, :]
        out[at + 48 : at + 56, :] = sol[at + 48 : at + 56, :]
    for k, (single, message) in enumerate(((7, low), (48, high))):
        at = pl.ds(single, 42, stride=EXT)
        out[at, :] = (out[at, :] + message[336:378, :]) * flags[2 + k]


def apply_kernel(
    sol, low, high, own_z, far_z, far_low, far_high, resid, c_x, c_down, c_up, c_z, c_face, h,
    out, applied, sums, field, pack, line,
):
    gz = lax.axis_index("gz")
    end = YROWS2 - 384
    lane = lanes(ZROWS2 + 2 * end)
    at_face = lax.rem(lane, 9) == jnp.where(gz == 0, 8, 0)
    shift = jnp.where(gz == 0, 7, 121)
    near = jnp.concatenate([own_z[...], low[384:YROWS2, :], high[384:YROWS2, :]], axis=0)
    got = jnp.concatenate([far_z[...], far_low[...], far_high[...]], axis=0)
    got = got + jnp.where(at_face, roll(near, shift, 1), 0.0)
    pack[...] = roll(got, jnp.where(gz == 0, 120, 127), 1)
    toward = jnp.where(gz == 0, 127, 1)
    lane8 = lanes(8)
    folded = jnp.where(gz == 0, lane8 - 120, 7 - lane8) >= 0

    def tile(index, start=0):
        q, j = divmod(index, PER)
        return roll(pack[start + 8 * q : start + 8 * q + 8, :], -9 * j, 1)

    def along_z(p, t):
        value = tile(p * 5 + t - 1)
        if t == 1:
            value = value + tile(p, ZROWS2)
        if t == 5:
            value = value + tile(p, ZROWS2 + end)
        return value

    for p in range(42):
        for t in range(1, 6):
            at = p * EXT + 8 * t
            value = sol[at : at + 8, :] + jnp.where(folded, along_z(p, t), 0.0)
            field[at : at + 8, :] = value
    for k, single in enumerate((7, 48)):
        for j in range(6):
            value = tile(210 + 6 * k + j) + tile(42 + j, ZROWS2 + k * end)
            line[8 * j : 8 * j + 8, :] = jnp.where(folded, value, 0.0)
        at = pl.ds(single, 42, stride=EXT)
        field[at, :] = sol[at, :] + line[0:42, :]
    pack[...] = roll(pack[...], toward, 1)

    outer = jnp.where(lanes(C) == outer_lane(), 0.5, 0.0)
    flux_x = c_x[0:C, :] * (field[EXT + 8 : EXT + 48, :] - field[8:48, :])
    sum_a = jnp.zeros((8, CZ), F32)
    sum_b = jnp.zeros((8, CZ), F32)
    def visit(x, carry):
        flux_x, sum_a, sum_b = carry
        at = (x + 1) * EXT
        to = rows_at(x * C, C)
        z = field[rows_at(at + 8, C), :]
        next_x = c_x[rows_at(x * C + C, C), :] * (field[rows_at(at + EXT + 8, C), :] - z)
        net = next_x - flux_x
        net = net + c_up[to, :] * (field[pl.ds(at + 9, C), :] - z)
        net = net - c_down[to, :] * (z - field[pl.ds(at + 7, C), :])
        flux_z = c_z[to, :] * (roll(z, -1, 1) - z)
        net = net + (flux_z - roll(flux_z, 1, 1)) + c_face[to, :] * (out[to, :] - z)
        image = mass_term * z - net + outer * h[to, :] * z
        out[to, :] = z
        applied[to, :] = image
        a, b = resid[to, :] * z, z * image
        for t in range(5):
            sum_a = sum_a + a[8 * t : 8 * t + 8]
            sum_b = sum_b + b[8 * t : 8 * t + 8]
        return next_x, sum_a, sum_b

    for x in range(C):
        for t in range(5):
            out[x * C + 8 * t : x * C + 8 * t + 8, :] = along_z(x + 1, t + 1)
    _, sum_a, sum_b = lax.fori_loop(0, C, visit, (flux_x, sum_a, sum_b), unroll=8)
    total_a = jnp.sum(sum_a, axis=0, keepdims=True)
    total_b = jnp.sum(sum_b, axis=0, keepdims=True)
    total_a = total_a + roll(total_a, CZ // 2, 1)
    total_b = total_b + roll(total_b, CZ // 2, 1)
    total = jnp.where(lanes(1) < CZ // 2, total_a, total_b)
    sums[...] = jnp.broadcast_to(total, sums.shape)


def gather_kernel(sums, out):
    out[...] = jnp.broadcast_to(jnp.sum(sums[...], axis=0, keepdims=True), out.shape)


def update_kernel(sums, guess, resid, field, applied, solution_out, resid_out):
    total = jnp.sum(sums[...], axis=0, keepdims=True)
    first = lanes(1) < CZ // 2
    above = jnp.sum(jnp.where(first, total, 0.0), axis=1, keepdims=True)
    below = jnp.sum(jnp.where(first, 0.0, total), axis=1, keepdims=True)
    step = above / below
    solution_out[...] = guess[...] + step * field[...]
    resid_out[...] = resid[...] - step * applied[...]


def on_device(gx, splits, right_side, guess_field, conduct_field):
    shape = right_side.shape
    b, v, h = (a.reshape(C * C, CZ) for a in (right_side, guess_field, conduct_field))
    n_gx, n_gy = lax.axis_size(gx), lax.axis_size("gy")
    at_x, at_y = lax.axis_index(gx), lax.axis_index("gy")
    flags = jnp.stack([at_x > 0, at_x < n_gx - 1, at_y > 0, at_y < n_gy - 1, at_x % 2 == 1]).astype(F32)

    def exchange(axis, up, down):
        n = lax.axis_size(axis)
        forward = [(i, i + 1) for i in range(n - 1)]
        backward = [(i + 1, i) for i in range(n - 1)]
        return lax.ppermute(up, axis, forward), lax.ppermute(down, axis, backward)

    def exchange_x(first, second):
        pairs = [[(i + k, i + 1 - k) for i in range(start, n_gx - 1, 2) for k in (0, 1)] for start in (1, 0)]
        return lax.ppermute(first, gx, pairs[0]), lax.ppermute(second, gx, pairs[1])

    def swap(value):
        return lax.ppermute(value, "gz", [(0, 1), (1, 0)])

    plane, forward, inverse, denom, eigen = tables()
    own = C * C
    box = EXT * EXT

    def buffer(rows):
        return pltpu.VMEM((rows, CZ), F32)

    up, down = call(
        strips_kernel, (YROWS, YROWS), guess_field, conduct_field, right_side,
        scratch=[pltpu.VMEM((C, C, CZ), F32)] * 3 + [pltpu.SemaphoreType.DMA((3, 2))],
        hbm=(0, 1, 2), limit=56, name="strips", work=2,
    )
    part, edge = call(residual_kernel, (own, 160), v, h, b, name="residual", work=2)
    low, high = exchange("gy", up, down)
    pairs, scale_a, scale_b = call(
        prepare_kernel, (own, box, box), eigen, v, h, denom, smem=(0,), name="prepare", work=2
    )
    (middle,) = call(pack_middle_kernel, (24 * BLOCKS_Z,), part, pairs, name="pack_middle", work=1)
    right, left, faces = call(
        extend_y_kernel, (XROWS, XROWS, 4 * EXT),
        flags, part, pairs, up, down, edge, low, high, middle,
        scratch=[buffer(XROWS)] * 2, smem=(0,), name="extend_y", work=1,
    )
    one, two = exchange_x(right, left)
    inner, part = call(
        inner_kernel, (38 * EXT, C * EXT),
        flags, plane, part, up, down, low, high, smem=(0,), name="inner", work=1,
    )
    (packed,) = call(pack_z_kernel, (ZROWS,), part, pairs, low, high, middle, name="pack_z", work=2)
    own_z, fluxes = call(
        extend_x_kernel, (ZROWS, 2 * EXT), flags, packed, faces, one, two, inner,
        smem=(0,), name="extend_x", work=1,
    )
    far_z = swap(own_z)
    (main,) = call(
        forward_kernel, (box,), flags, plane, part, inner, fluxes, one, two,
        scratch=[buffer(box)], smem=(0,), name="forward", work=2,
    )
    second_a, second_b, sides, side_strip, right, left = call(
        solve_kernel, (box, box, 18 * EXT, 18 * EXT, XROWS2, XROWS2),
        flags, own_z, far_z, main, plane, forward, inverse, scale_a, scale_b,
        scratch=[buffer(box), buffer(XROWS2), buffer(XROWS2)], smem=(0,), name="solve", work=6,
    )
    resid, c_x, c_down, c_up, c_z, c_face = call(
        own_kernel, (own, own + C, own, own, own, own),
        flags, h, low, high, one, two, part, fluxes, own_z, far_z,
        scratch=[buffer(own + 2 * C)], smem=(0,), name="own", work=2,
    )
    one, two = exchange_x(right, left)
    sol, strip = call(
        rest_kernel, (42 * EXT, 42 * EXT),
        plane, inverse, second_a, second_b, sides, side_strip, name="rest", work=2,
    )
    sol, up, down, own_z, across_up, across_down = call(
        fold_x_kernel, (42 * EXT, YROWS2, YROWS2, ZROWS2, 32, 32),
        flags, sol, strip, one, two, resid,
        scratch=[buffer(42 * EXT), buffer(144)], smem=(0,), name="fold_x", work=1,
    )
    low, high = exchange("gy", up, down)
    far_z = swap(own_z)
    diagonal = [((j, k), (j + 1, 1 - k)) for j in range(n_gy - 1) for k in range(2)]
    pairs = [(2 * a + b, 2 * c + d) for (a, b), (c, d) in diagonal]
    far_low = lax.ppermute(across_up, ("gy", "gz"), pairs)
    far_high = lax.ppermute(across_down, ("gy", "gz"), [(b, a) for a, b in pairs])
    (sol,) = call(
        fold_y_kernel, (42 * EXT,), flags, sol, low, high, smem=(0,), name="fold_y", work=1
    )
    first, last = splits
    field, applied, sums = call(
        apply_kernel, (own, own, lax.axis_size(first)),
        sol, low, high, own_z, far_z, far_low, far_high, resid, c_x, c_down, c_up, c_z, c_face, h,
        scratch=[buffer(42 * EXT), buffer(ZROWS2 + 64), buffer(48)], name="apply", work=3,
    )
    sums = lax.all_to_all(sums, first, 0, 0, tiled=True)
    (sums,) = call(gather_kernel, (lax.axis_size(last),), sums, name="gather")
    sums = lax.all_to_all(sums, last, 0, 0, tiled=True)
    out, resid = call(update_kernel, (own, own), sums, v, resid, field, applied, name="update", work=2)
    return out.reshape(shape), resid.reshape(shape)


def solution(mesh):
    n_gx, n_gy, n_gz = mesh.devices.shape
    if n_gx == 64:
        mesh = Mesh(mesh.devices.reshape(4, 8, 2, n_gy, n_gz), ("gx_x", "gx_y", "gx_c", "gy", "gz"))
        gx = ("gx_x", "gx_y", "gx_c")
        splits = (("gx_c", "gy", "gz"), ("gx_x", "gx_y"))
    else:
        gx = "gx"
        splits = (("gx",), ("gy", "gz"))
    placed = P(gx, "gy", "gz")
    return jax.shard_map(
        functools.partial(on_device, gx, splits),
        mesh=mesh,
        in_specs=(placed,) * 3,
        out_specs=(placed,) * 2,
        check_vma=False,
    )
```

```python
import functools

import jax
import jax.numpy as jnp
import ml_dtypes
import numpy as np
from jax import lax
from jax.experimental import pallas as pl
from jax.experimental.pallas import tpu as pltpu
from jax.sharding import Mesh
from jax.sharding import PartitionSpec as P

OVER = 8
C = 40
CZ = 128
EXT = C + 2 * OVER
EXTZ = CZ + 2 * OVER
TILES = EXT // 8
stiff_scale = 3.0
mass_term = 0.001

F32 = jnp.float32
BF16 = jnp.bfloat16
VMEM = pl.BlockSpec(memory_space=pltpu.VMEM)
SMEM = pl.BlockSpec(memory_space=pltpu.SMEM)
HBM = pl.BlockSpec(memory_space=pltpu.HBM)

YROWS = 440
XROWS = 616
PER_Z = 12
BLOCKS_Z = -(-EXT // PER_Z)
ZROWS = BLOCKS_Z * EXT
PER = 14
XROWS2 = 9 * EXT + 40
YROWS2 = 416
ZGROUPS2 = 42 * 5 + 12
ZROWS2 = 8 * -(-ZGROUPS2 // PER)


def sine_table(count):
    k = np.arange(1, count + 1)
    basis = np.sqrt(2.0 / (count + 1)) * np.sin(np.pi * k[:, None] * k[None, :] / (count + 1))
    eigen = 2.0 - 2.0 * np.cos(np.pi * k / (count + 1))
    return basis, eigen


def two_parts(table):
    high = table.astype(ml_dtypes.bfloat16)
    low = (table - high.astype(np.float64)).astype(ml_dtypes.bfloat16)
    return high, low


@functools.cache
def tables():
    basis, eigen = sine_table(EXT)
    basis_z, eigen_z = sine_table(EXTZ)
    high, low = two_parts(basis)
    plane = np.zeros((EXT, 192), ml_dtypes.bfloat16)
    plane[:, 0:EXT] = high
    plane[:, 64 : 64 + EXT] = low
    plane[:, 128 : 128 + EXT] = high
    forward = np.zeros((2, 256, 256))
    inverse = np.zeros((2, 256, 256))
    for gz in range(2):
        own = basis_z[8 : 8 + CZ]
        strip = basis_z[136:144] if gz == 0 else basis_z[0:8]
        face_own, face_far = (135, 136) if gz == 0 else (8, 7)
        forward[gz, :CZ, :EXTZ] = own
        forward[gz, CZ, :EXTZ] = basis_z[face_own] - basis_z[face_far]
        forward[gz, CZ + 2 : CZ + 10, :EXTZ] = strip
        inverse[gz, :EXTZ, :CZ] = own.T
        inverse[gz, :EXTZ, CZ : CZ + 9] = (basis_z[135:144] if gz == 0 else basis_z[0:9]).T

    def stacked(table):
        high, low = two_parts(table)
        return np.concatenate([high, high, low], axis=1)

    denom = np.full((EXT, 256), 1.0)
    denom[:, :EXTZ] = stiff_scale * (eigen[:, None] + eigen_z[None, :]) + mass_term
    return (
        plane,
        stacked(forward),
        stacked(inverse),
        denom.astype(np.float32),
        (stiff_scale * eigen).astype(np.float32),
    )


def roll(value, shift, axis):
    if isinstance(shift, int):
        shift = shift % value.shape[axis]
        return value if shift == 0 else pltpu.roll(value, shift, axis)
    return pltpu.roll(value, lax.rem(shift + 2 * value.shape[axis], value.shape[axis]), axis)


def lanes(rows):
    return lax.broadcasted_iota(jnp.int32, (rows, CZ), 1)


def rows_at(start, size):
    return pl.ds(pl.multiple_of(start, 8), size)


def tile_at(index):
    return rows_at(index * 8, 8)


def call(body, out_rows, *args, scratch=(), limit=16, name=None, smem=(), hbm=(), work=0):
    place = {**{i: SMEM for i in smem}, **{i: HBM for i in hbm}}
    return pl.pallas_call(
        body,
        out_shape=[jax.ShapeDtypeStruct((rows, CZ), F32) for rows in out_rows],
        in_specs=[place.get(i, VMEM) for i in range(len(args))],
        out_specs=[VMEM] * len(out_rows),
        scratch_shapes=list(scratch),
        compiler_params=pltpu.CompilerParams(vmem_limit_bytes=limit * 2**20),
        cost_estimate=pl.CostEstimate(
            flops=int(work * 1e9), bytes_accessed=int(work * 2e6), transcendentals=0
        )
        if work
        else None,
        name=name,
    )(*args)


def strip_base():
    return jnp.where(lax.axis_index("gz") == 0, 118, 126)


def face_lane():
    return jnp.where(lax.axis_index("gz") == 0, 127, 0)


def outer_lane():
    return jnp.where(lax.axis_index("gz") == 0, 0, 127)


def pair_of(v, h, lane, base, face):
    return jnp.where(lane == base, roll(v, base - face, 1), 0.0) + jnp.where(
        lane == base + 1, roll(h, base + 1 - face, 1), 0.0
    )


def strips_kernel(v_in, h_in, b_in, up, down, v, h, b, sems):
    copies = []
    for k, (source, target, size) in enumerate(((v_in, v, 16), (h_in, h, 16), (b_in, b, 8))):
        for side, first in enumerate((0, C - size)):
            at = pl.ds(first, size)
            copies.append(
                pltpu.make_async_copy(source.at[:, at, :], target.at[:, at, :], sems.at[k, side])
            )
            copies[-1].start()
    base, face = strip_base(), face_lane()
    lane = lanes(8)
    row = lax.broadcasted_iota(jnp.int32, (8, CZ), 0)
    z_half = jnp.where(lane < CZ - 1, 0.5, 0.0)
    outer = jnp.where(lane == outer_lane(), 0.5, 0.0)
    last = C - 1
    for copy in copies:
        copy.wait()

    def tile(x, start, beyond, sign, flux_x):
        following = jnp.minimum(x + 1, last)
        at, to = pl.ds(start, 8), pl.ds(beyond, 8)
        vi, hi = v[x, at, :], h[x, at, :]
        next_x = 0.5 * (hi + h[following, at, :]) * (v[following, at, :] - vi)
        flux_y = 0.5 * (hi + h[x, to, :]) * (v[x, to, :] - vi)
        edge = 0 if sign > 0 else 7
        net_y = flux_y - jnp.where(row == edge, 0.0, roll(flux_y, sign, 0))
        flux_z = z_half * (hi + roll(hi, -1, 1)) * (roll(vi, -1, 1) - vi)
        applied = (
            mass_term * vi
            - (next_x - flux_x)
            - net_y
            - (flux_z - roll(flux_z, 1, 1))
            + outer * hi * vi
        )
        return b[x, at, :] - applied, next_x, vi, hi

    def visit(x, carry):
        flux_up, flux_down, pack_up, pack_down = carry
        resid, flux_down, vi, hi = tile(x, 0, 1, 1, flux_down)
        down[tile_at(x), :] = resid
        down[pl.ds(320 + x, 1), :] = vi[0:1]
        down[pl.ds(360 + x, 1), :] = hi[0:1]
        pack_down = pack_down + roll(pair_of(vi, hi, lane, base, face), 2 * x - base, 1)
        resid, flux_up, vi, hi = tile(x, 32, 31, -1, flux_up)
        up[tile_at(x), :] = resid
        up[pl.ds(320 + x, 1), :] = vi[7:8]
        up[pl.ds(360 + x, 1), :] = hi[7:8]
        pack_up = pack_up + roll(pair_of(vi, hi, lane, base, face), 2 * x - base, 1)
        return flux_up, flux_down, pack_up, pack_down

    zero = jnp.zeros((8, CZ), F32)
    _, _, pack_up, pack_down = lax.fori_loop(0, C, visit, (zero,) * 4, unroll=8)
    up[432:440, :] = pack_up
    down[432:440, :] = pack_down
    for message, first in ((up, 32), (down, 0)):
        at = pl.ds(first, 8)
        message[400:408, :] = v[0, at, :]
        message[408:416, :] = h[0, at, :]
        message[416:424, :] = v[last, at, :]
        message[424:432, :] = h[last, at, :]


def residual_kernel(v, h, b, part, edge):
    lane = lanes(C)
    row = lax.broadcasted_iota(jnp.int32, (C, CZ), 0)
    y_half = jnp.where(row > 0, 0.5, 0.0)
    z_half = jnp.where(lane < CZ - 1, 0.5, 0.0)
    outer = jnp.where(lane == outer_lane(), 0.5, 0.0)

    def visit(x, flux_x):
        own = rows_at(x * C, C)
        following = rows_at(jnp.minimum(x + 1, C - 1) * C, C)
        vi, hi = v[own, :], h[own, :]
        next_x = 0.5 * (hi + h[following, :]) * (v[following, :] - vi)
        flux_y = y_half * (hi + roll(hi, 1, 0)) * (vi - roll(vi, 1, 0))
        flux_z = z_half * (hi + roll(hi, -1, 1)) * (roll(vi, -1, 1) - vi)
        applied = (
            mass_term * vi
            - (next_x - flux_x)
            - (roll(flux_y, -1, 0) - flux_y)
            - (flux_z - roll(flux_z, 1, 1))
            + outer * hi * vi
        )
        part[own, :] = b[own, :] - applied
        return next_x

    lax.fori_loop(0, C, visit, jnp.zeros((C, CZ), F32), unroll=4)
    last = (C - 1) * C
    edge[0:40, :] = v[0:40, :]
    edge[40:80, :] = h[0:40, :]
    edge[80:120, :] = v[last : last + 40, :]
    edge[120:160, :] = h[last : last + 40, :]


def prepare_kernel(eigen, v, h, denom, out, out_a, out_b):
    base, face = strip_base(), face_lane()
    lane = lanes(C)

    def visit_pair(x, _):
        at = rows_at(x * C, C)
        out[at, :] = pair_of(v[at, :], h[at, :], lane, base, face)
        return 0

    lax.fori_loop(0, C, visit_pair, 0, unroll=8)

    def visit(y, _):
        value = 1.0 / (denom[...] + eigen[y])
        at = rows_at(y * EXT, EXT)
        out_a[at, :] = value[:, :CZ]
        out_b[at, :] = value[:, CZ:]
        return 0

    lax.fori_loop(0, EXT, visit, 0, unroll=4)


def choose(flag, a, b):
    return jnp.where(flag > 0.5, a, b)


def by_parity(flags, first, second):
    def before(start, stop):
        return choose(flags[4], second[start:stop, :], first[start:stop, :])

    def after(start, stop):
        return choose(flags[4], first[start:stop, :], second[start:stop, :])

    return before, after


def pick(pack, index, to):
    pair = lax.div(lanes(8), 2) == index
    return roll(jnp.where(pair, pack, 0.0), to - 2 * index, 1)


def strip_mask():
    lane = lanes(8)
    return jnp.where(lax.axis_index("gz") == 0, lane - 120, 7 - lane) >= 0


def y_fluxes(up, down, low, high):
    flux_a = 0.5 * (low[360:400, :] + down[360:400, :]) * (down[320:360, :] - low[320:360, :])
    flux_b = 0.5 * (up[360:400, :] + high[360:400, :]) * (high[320:360, :] - up[320:360, :])
    return flux_a, flux_b


def extend_y(flags, fluxes, part, low, high, out, start, stop):
    for x in range(start, stop):
        at = (x - start) * EXT
        out[at : at + 8, :] = low[8 * x : 8 * x + 8, :]
        out[at + 8 : at + 48, :] = part[x * C : x * C + C, :]
        out[at + 48 : at + 56, :] = high[8 * x : 8 * x + 8, :]
    flux_a, flux_b = (flux[start:stop] for flux in fluxes)
    for row, value in ((8, -flux_a), (7, flux_a * flags[2]), (47, flux_b), (48, -flux_b * flags[3])):
        at = pl.ds(row, stop - start, stride=EXT)
        out[at, :] = out[at, :] + value


def extend_y_kernel(flags, part, vh, up, down, edge, low, high, _, first, second, faces, right, left):
    base, strip_lanes = strip_base(), strip_mask()
    fluxes = y_fluxes(up, down, low, high)
    for message, start, strip, own in ((left, 0, 400, 0), (right, 32, 416, 80)):
        extend_y(flags, fluxes, part, low, high, message, start, start + OVER)
        for k in range(2):
            at = 448 + k * EXT
            message[at : at + 8, :] = low[strip + 8 * k : strip + 8 * k + 8, :]
            message[at + 8 : at + 48, :] = edge[own + 40 * k : own + 40 * k + 40, :]
            message[at + 48 : at + 56, :] = high[strip + 8 * k : strip + 8 * k + 8, :]
        for t in range(TILES):
            near = jnp.zeros((8, CZ), F32)
            taken = jnp.zeros((8, CZ), F32)
            for i in range(OVER):
                x = start + i
                at = i * EXT + 8 * t
                value = jnp.where(strip_lanes, message[at : at + 8, :], 0.0)
                if t == 0:
                    taken = taken + pick(low[432:440, :], x, 10 * i)
                elif t == 6:
                    taken = taken + pick(high[432:440, :], x, 10 * i)
                else:
                    value = value + vh[x * C + 8 * t - 8 : x * C + 8 * t, :]
                near = near + roll(value, 10 * i, 1)
            message[560 + 8 * t : 568 + 8 * t, :] = roll(near, -base, 1) + taken
    faces[0:112, :] = left[448:560, :]
    faces[112:224, :] = right[448:560, :]
    first[...] = choose(flags[4], right[...], left[...])
    second[...] = choose(flags[4], left[...], right[...])


def pack_planes(tiles, value_of, taken_of):
    base = strip_base()
    packs = {}
    for q in range(BLOCKS_Z):
        for t in tiles:
            near = jnp.zeros((8, CZ), F32)
            taken = jnp.zeros((8, CZ), F32)
            for j in range(PER_Z):
                x = q * PER_Z + j - OVER
                if 0 <= x < C:
                    near = near + roll(value_of(x, t), 10 * j, 1)
                    if t in (0, 6):
                        taken = taken + taken_of(x, t, 10 * j)
            packs[q, t] = roll(near, -base, 1) + taken
    return packs


def pack_middle_kernel(part, vh, out):
    strip_lanes = strip_mask()

    def value_of(x, t):
        at = pl.ds(x * C + 8 * t - 8, 8)
        return jnp.where(strip_lanes, part[at, :], 0.0) + vh[at, :]

    for (q, t), value in pack_planes((2, 3, 4), value_of, None).items():
        at = q * 24 + 8 * (t - 2)
        out[at : at + 8, :] = value


def pack_z_kernel(part, vh, low, high, middle, message):
    strip_lanes = strip_mask()

    def value_of(x, t):
        value = jnp.where(strip_lanes, part[x * EXT + 8 * t : x * EXT + 8 * t + 8, :], 0.0)
        if t in (1, 5):
            value = value + vh[x * C + 8 * t - 8 : x * C + 8 * t, :]
        return value

    def taken_of(x, t, lane):
        return pick((low if t == 0 else high)[432:440, :], x, lane)

    for q in range(BLOCKS_Z):
        message[q * EXT + 16 : q * EXT + 40, :] = middle[24 * q : 24 * q + 24, :]
    for (q, t), value in pack_planes((0, 1, 5, 6), value_of, taken_of).items():
        at = q * EXT + 8 * t
        message[at : at + 8, :] = value


def extend_x_kernel(flags, packed, faces, first, second, inner, message, fluxes):
    base, strip_lanes = strip_base(), strip_mask()
    before, after = by_parity(flags, first, second)
    flux_a = 0.5 * (before(504, 560) + faces[56:112, :]) * (faces[0:56, :] - before(448, 504))
    flux_b = 0.5 * (faces[168:224, :] + after(504, 560)) * (after(448, 504) - faces[112:168, :])
    fluxes[0:EXT, :] = flux_a
    fluxes[EXT : 2 * EXT, :] = flux_b
    message[...] = packed[...]
    end = (BLOCKS_Z - 1) * EXT
    message[0:EXT, :] = message[0:EXT, :] + before(560, 616)
    message[end : end + EXT, :] = message[end : end + EXT, :] + after(560, 616)

    def add(x, t, value):
        q, j = divmod(x, PER_Z)
        at = q * EXT + 8 * t
        message[at : at + 8, :] = message[at : at + 8, :] + roll(value, 10 * j, 1)

    for t in range(TILES):
        a = roll(jnp.where(strip_lanes, flux_a[8 * t : 8 * t + 8], 0.0), -base, 1)
        b = roll(jnp.where(strip_lanes, flux_b[8 * t : 8 * t + 8], 0.0), -base, 1)
        add(OVER - 1, t, a * flags[0])
        add(OVER, t, -a)
        add(OVER + C - 1, t, b)
        add(OVER + C, t, -b * flags[1])


def halves(value):
    high = value.astype(BF16)
    return high, (value - high.astype(F32)).astype(BF16)


def dot(a, b):
    return jnp.dot(a, b, preferred_element_type=F32)


def along_lanes(value, table):
    high, low = halves(value)
    return dot(jnp.concatenate([high, low, high], axis=1), table)


def along_rows(table, value):
    padded = jnp.concatenate([value, jnp.zeros((8, value.shape[1]), F32)], axis=0)
    high, low = halves(padded)
    return dot(table, jnp.concatenate([high, high, low], axis=0))


def beside(a, b):
    return jnp.concatenate([a, b], axis=1)


def inner_kernel(flags, plane, box, up, down, low, high, out, part):
    table = plane[...]
    extend_y(flags, y_fluxes(up, down, low, high), box, low, high, part, 0, C)
    for x in range(1, C - 1, 2):
        at, then = pl.ds(x * EXT, EXT), pl.ds((x + 1) * EXT, EXT)
        value = along_rows(table, beside(part[at, :], part[then, :]))
        out[(x - 1) * EXT : x * EXT, :] = value[:, :CZ]
        out[x * EXT : (x + 1) * EXT, :] = value[:, CZ:]


def forward_kernel(flags, plane, part, inner, fluxes, one, two, out, first):
    before, after = by_parity(flags, one, two)
    table = plane[...]
    flux_a, flux_b = fluxes[0:EXT, :], fluxes[EXT : 2 * EXT, :]
    planes = {x: before(x * EXT, (x + 1) * EXT) for x in range(OVER)}
    planes[7] = planes[7] + flux_a * flags[0]
    planes[8] = part[0:EXT, :] - flux_a
    planes[47] = part[(C - 1) * EXT : C * EXT, :] + flux_b
    planes.update({48 + x: after(x * EXT, (x + 1) * EXT) for x in range(OVER)})
    planes[48] = planes[48] - flux_b * flags[1]
    first[9 * EXT : 47 * EXT, :] = inner[...]
    order = sorted(planes)
    for x, then in zip(order[0::2], order[1::2]):
        value = along_rows(table, beside(planes[x], planes[then]))
        first[x * EXT : (x + 1) * EXT, :] = value[:, :CZ]
        first[then * EXT : (then + 1) * EXT, :] = value[:, CZ:]

    def visit_x(c, _):
        for i in range(14):
            y = 2 * (c * 14 + i)
            value = beside(first[pl.ds(y, EXT, stride=EXT), :], first[pl.ds(y + 1, EXT, stride=EXT), :])
            value = along_rows(table, value)
            out[rows_at(y * EXT, EXT), :] = value[:, :CZ]
            out[rows_at((y + 1) * EXT, EXT), :] = value[:, CZ:]
        return 0

    lax.fori_loop(0, 2, visit_x, 0)


def face_terms(own_z, far_z):
    both = own_z[...] + far_z[...]
    half = 0.5 * roll(both, -1, 1)
    return half, half * (far_z[...] - own_z[...])


STEP = 28


def solve_kernel(
    flags, _, own_z, far_z, main, plane, forward, inverse, scale_a, scale_b,
    second_a, second_b, sol, strip, first, second, halo, right, left,
):
    gz = lax.axis_index("gz")
    table = plane[...]
    _, flux = face_terms(own_z, far_z)
    pack = jnp.where(lax.rem(lanes(ZROWS), 10) == 0, flux, far_z[...])
    blocks = [pack[q * EXT : (q + 1) * EXT] for q in range(BLOCKS_Z)]
    done = []
    for q in range(0, BLOCKS_Z - 1, 2):
        value = along_rows(table, beside(blocks[q], blocks[q + 1]))
        done += [value[:, :CZ], value[:, CZ:]]
    done.append(along_rows(table, blocks[-1]))
    for x in range(EXT):
        q, j = x // PER_Z, x % PER_Z
        halo[x * EXT : (x + 1) * EXT, :] = roll(done[q], -10 * j, 1)

    forward_table = forward[gz]
    inverse_table = inverse[gz]

    def visit(c, _):
        parts = []
        for i in range(0, STEP, 2):
            y = c * STEP + i
            value = beside(halo[pl.ds(y, EXT, stride=EXT), :], halo[pl.ds(y + 1, EXT, stride=EXT), :])
            value = along_rows(table, value)
            parts.append(beside(main[rows_at(y * EXT, EXT), :], value[:, :CZ]))
            parts.append(beside(main[rows_at((y + 1) * EXT, EXT), :], value[:, CZ:]))
        value = along_lanes(jnp.concatenate(parts, axis=0), forward_table)
        at = rows_at(c * STEP * EXT, STEP * EXT)
        value = value * beside(scale_a[at, :], scale_b[at, :])
        for i in range(STEP):
            part = along_rows(table, value[i * EXT : (i + 1) * EXT])
            to = pl.ds(c * STEP + i, EXT, stride=EXT)
            second_a[to, :] = part[:, :CZ]
            second_b[to, :] = part[:, CZ:]
        return 0

    lax.fori_loop(0, EXT // STEP, visit, 0)

    for k, (message, start) in enumerate(((left, 0), (right, 47))):
        inverse_planes(table, inverse_table, second_a, second_b, sol, strip, range(start, start + 9), 9 * k)
        message[0 : 9 * EXT, :] = sol[9 * k * EXT : 9 * (k + 1) * EXT, :]
        tiles = [strip[pl.ds((9 * k * TILES + j) * 8, 8), :] for j in range(63)]
        pack_tiles(message, 9 * EXT, tiles)
    first[...] = choose(flags[4], right[...], left[...])
    second[...] = choose(flags[4], left[...], right[...])


def inverse_planes(table, inverse_table, second_a, second_b, sol, strip, planes, to):
    parts = []
    for x in planes:
        at = pl.ds(x * EXT, EXT)
        parts.append(along_rows(table, beside(second_a[at, :], second_b[at, :])))
    value = along_lanes(jnp.concatenate(parts, axis=0), inverse_table)
    at = pl.ds(to * EXT, len(planes) * EXT)
    sol[at, :] = value[:, :CZ]
    strip[at, :] = value[:, CZ:]


def rest_kernel(plane, inverse, second_a, second_b, sides, side_strip, sol, strip):
    table, inverse_table = plane[...], inverse[lax.axis_index("gz")]
    for first, last in ((9, 19), (19, 29), (29, 38), (38, 47)):
        inverse_planes(
            table, inverse_table, second_a, second_b, sol, strip, range(first, last), first - 7
        )
    for target, source in ((sol, sides), (strip, side_strip)):
        target[0 : 2 * EXT, :] = source[7 * EXT : 9 * EXT, :]
        target[40 * EXT : 42 * EXT, :] = source[9 * EXT : 11 * EXT, :]


def own_kernel(part, fluxes, own_z, far_z, resid, c_face):
    face = face_lane()
    half, flux = face_terms(own_z, far_z)
    half, flux = roll(half, face, 1), roll(flux, face, 1)
    lane8 = lanes(8)
    for x in range(C):
        q, j = (x + OVER) // PER_Z, (x + OVER) % PER_Z
        for t in range(5):
            at = q * EXT + 8 * (t + 1)
            to = x * C + 8 * t
            source = x * EXT + 8 * (t + 1)
            moved = jnp.where(lane8 == face, roll(flux[at : at + 8], -10 * j, 1), 0.0)
            if x == 0:
                moved = moved - fluxes[source : source + 8, :]
            elif x == C - 1:
                moved = moved + fluxes[source + EXT - x * EXT : source + EXT - x * EXT + 8, :]
            resid[to : to + 8, :] = part[source : source + 8, :] + moved
            c_face[to : to + 8, :] = jnp.where(
                lane8 == face, roll(half[at : at + 8], -10 * j, 1), 0.0
            )


def coefficients_kernel(flags, h, low, high, one, two, c_x, c_down, c_up, c_z, cond):
    before, after = by_parity(flags, one, two)
    cond[0:C, :] = before(512, 552)
    cond[C : C + C * C, :] = h[...]
    cond[C + C * C :, :] = after(512, 552)
    z_half = jnp.where(lanes(C) < CZ - 1, 0.5, 0.0)
    row = lax.broadcasted_iota(jnp.int32, (C, CZ), 0)
    for x in range(C):
        at = x * C
        hi = h[at : at + C, :]
        c_x[at : at + C, :] = 0.5 * (cond[at : at + C, :] + hi)
        below = jnp.where(row == 0, low[360 + x : 361 + x, :], roll(hi, 1, 0))
        above = jnp.where(row == C - 1, high[360 + x : 361 + x, :], roll(hi, -1, 0))
        c_down[at : at + C, :] = 0.5 * (hi + below)
        c_up[at : at + C, :] = 0.5 * (hi + above)
        c_z[at : at + C, :] = z_half * (hi + roll(hi, -1, 1))
    c_x[C * C :, :] = 0.5 * (cond[C * C : C * C + C, :] + cond[C * C + C :, :])


def pack_tiles(message, at, values):
    for q in range(-(-len(values) // PER)):
        acc = values[q * PER]
        for j, value in enumerate(values[q * PER + 1 : (q + 1) * PER], 1):
            acc = acc + roll(value, 9 * j, 1)
        message[at + 8 * q : at + 8 * q + 8, :] = acc


def unpack_tile(message, at, index):
    q = index // PER
    return roll(message[rows_at(at + 8 * q, 8), :], -9 * (index - q * PER), 1)


def fold_x_kernel(
    flags, sol, strip, one, two, _, out, up, down, across, across_up, across_down, out_strip, line
):
    size = 42 * EXT
    narrow = lanes(8) < 9
    before, after = by_parity(flags, one, two)
    tail = 33 * EXT
    out[0 : 9 * EXT, :] = sol[0 : 9 * EXT, :] + before(0, 9 * EXT)
    out[9 * EXT : tail, :] = sol[9 * EXT : tail, :]
    out[tail:size, :] = sol[tail:size, :] + after(0, 9 * EXT)
    out_strip[9 * EXT : tail, :] = strip[9 * EXT : tail, :]
    packs = [side(9 * EXT, XROWS2) for side in (before, after)]

    for j in range(63):
        q, i = divmod(j, PER)
        for pack, at in ((packs[0], 8 * j), (packs[1], tail + 8 * j)):
            value = jnp.where(narrow, roll(pack[8 * q : 8 * q + 8], -9 * i, 1), 0.0)
            out_strip[at : at + 8, :] = strip[at : at + 8, :] + value

    for array in (out, out_strip):
        array[0:EXT, :] = array[0:EXT, :] * flags[0]
        array[41 * EXT : size, :] = array[41 * EXT : size, :] * flags[1]

    for message, tile, single in ((up, 6, 47), (down, 0, 8)):
        for p in range(42):
            message[8 * p : 8 * p + 8, :] = out[p * EXT + 8 * tile : p * EXT + 8 * tile + 8, :]
        message[376:384, :] = jnp.zeros((8, CZ), F32)
        message[336:378, :] = out[pl.ds(single, 42, stride=EXT), :]
        line[40:48, :] = jnp.zeros((8, CZ), F32)
        line[0:42, :] = out_strip[pl.ds(single, 42, stride=EXT), :]
        values = [out_strip[p * EXT + 8 * tile : p * EXT + 8 * tile + 8, :] for p in range(42)]
        values += [line[8 * j : 8 * j + 8, :] for j in range(6)]
        pack_tiles(message, 384, values)
    across_up[...] = up[384:416, :]
    across_down[...] = down[384:416, :]
    values = []
    for p in range(42):
        for t in range(1, 6):
            at = p * EXT + 8 * t
            values.append(out_strip[at : at + 8, :])
    for k, single in enumerate((7, 48)):
        at = 48 * (k + 1)
        line[at + 40 : at + 48, :] = jnp.zeros((8, CZ), F32)
        line[at : at + 42, :] = out_strip[pl.ds(single, 42, stride=EXT), :] * flags[2 + k]
        values += [line[at + 8 * j : at + 8 * j + 8, :] for j in range(6)]
    pack_tiles(across, 0, values)


def fold_y_kernel(flags, sol, low, high, out):
    for p in range(42):
        for message, tile in ((low, 1), (high, 5)):
            at = p * EXT + 8 * tile
            out[at : at + 8, :] = sol[at : at + 8, :] + message[8 * p : 8 * p + 8, :]
        at = p * EXT
        out[at : at + 8, :] = sol[at : at + 8, :]
        out[at + 16 : at + 40, :] = sol[at + 16 : at + 40, :]
        out[at + 48 : at + 56, :] = sol[at + 48 : at + 56, :]
    for k, (single, message) in enumerate(((7, low), (48, high))):
        at = pl.ds(single, 42, stride=EXT)
        out[at, :] = (out[at, :] + message[336:378, :]) * flags[2 + k]


def apply_kernel(
    sol, low, high, own_z, far_z, far_low, far_high, resid, c_x, c_down, c_up, c_z, c_face, h,
    out, applied, sums, field, pack, line,
):
    gz = lax.axis_index("gz")
    end = YROWS2 - 384
    lane = lanes(ZROWS2 + 2 * end)
    at_face = lax.rem(lane, 9) == jnp.where(gz == 0, 8, 0)
    shift = jnp.where(gz == 0, 7, 121)
    near = jnp.concatenate([own_z[...], low[384:YROWS2, :], high[384:YROWS2, :]], axis=0)
    got = jnp.concatenate([far_z[...], far_low[...], far_high[...]], axis=0)
    got = got + jnp.where(at_face, roll(near, shift, 1), 0.0)
    pack[...] = roll(got, jnp.where(gz == 0, 120, 127), 1)
    toward = jnp.where(gz == 0, 127, 1)
    lane8 = lanes(8)
    folded = jnp.where(gz == 0, lane8 - 120, 7 - lane8) >= 0

    def tile(index, start=0):
        q, j = divmod(index, PER)
        return roll(pack[start + 8 * q : start + 8 * q + 8, :], -9 * j, 1)

    def along_z(p, t):
        value = tile(p * 5 + t - 1)
        if t == 1:
            value = value + tile(p, ZROWS2)
        if t == 5:
            value = value + tile(p, ZROWS2 + end)
        return value

    for p in range(42):
        for t in range(1, 6):
            at = p * EXT + 8 * t
            value = sol[at : at + 8, :] + jnp.where(folded, along_z(p, t), 0.0)
            field[at : at + 8, :] = value
    for k, single in enumerate((7, 48)):
        for j in range(6):
            value = tile(210 + 6 * k + j) + tile(42 + j, ZROWS2 + k * end)
            line[8 * j : 8 * j + 8, :] = jnp.where(folded, value, 0.0)
        at = pl.ds(single, 42, stride=EXT)
        field[at, :] = sol[at, :] + line[0:42, :]
    pack[...] = roll(pack[...], toward, 1)

    outer = jnp.where(lanes(C) == outer_lane(), 0.5, 0.0)
    flux_x = c_x[0:C, :] * (field[EXT + 8 : EXT + 48, :] - field[8:48, :])
    sum_a = jnp.zeros((8, CZ), F32)
    sum_b = jnp.zeros((8, CZ), F32)
    def visit(x, carry):
        flux_x, sum_a, sum_b = carry
        at = (x + 1) * EXT
        to = rows_at(x * C, C)
        z = field[rows_at(at + 8, C), :]
        next_x = c_x[rows_at(x * C + C, C), :] * (field[rows_at(at + EXT + 8, C), :] - z)
        net = next_x - flux_x
        net = net + c_up[to, :] * (field[pl.ds(at + 9, C), :] - z)
        net = net - c_down[to, :] * (z - field[pl.ds(at + 7, C), :])
        flux_z = c_z[to, :] * (roll(z, -1, 1) - z)
        net = net + (flux_z - roll(flux_z, 1, 1)) + c_face[to, :] * (out[to, :] - z)
        image = mass_term * z - net + outer * h[to, :] * z
        out[to, :] = z
        applied[to, :] = image
        a, b = resid[to, :] * z, z * image
        for t in range(5):
            sum_a = sum_a + a[8 * t : 8 * t + 8]
            sum_b = sum_b + b[8 * t : 8 * t + 8]
        return next_x, sum_a, sum_b

    for x in range(C):
        for t in range(5):
            out[x * C + 8 * t : x * C + 8 * t + 8, :] = along_z(x + 1, t + 1)
    _, sum_a, sum_b = lax.fori_loop(0, C, visit, (flux_x, sum_a, sum_b), unroll=8)
    total_a = jnp.sum(sum_a, axis=0, keepdims=True)
    total_b = jnp.sum(sum_b, axis=0, keepdims=True)
    total_a = total_a + roll(total_a, CZ // 2, 1)
    total_b = total_b + roll(total_b, CZ // 2, 1)
    total = jnp.where(lanes(1) < CZ // 2, total_a, total_b)
    sums[...] = jnp.broadcast_to(total, sums.shape)


def gather_kernel(sums, out):
    out[...] = jnp.broadcast_to(jnp.sum(sums[...], axis=0, keepdims=True), out.shape)


def update_kernel(sums, guess, resid, field, applied, solution_out, resid_out):
    total = jnp.sum(sums[...], axis=0, keepdims=True)
    first = lanes(1) < CZ // 2
    above = jnp.sum(jnp.where(first, total, 0.0), axis=1, keepdims=True)
    below = jnp.sum(jnp.where(first, 0.0, total), axis=1, keepdims=True)
    step = above / below
    solution_out[...] = guess[...] + step * field[...]
    resid_out[...] = resid[...] - step * applied[...]


def on_device(gx, splits, right_side, guess_field, conduct_field):
    shape = right_side.shape
    b, v, h = (a.reshape(C * C, CZ) for a in (right_side, guess_field, conduct_field))
    n_gx, n_gy = lax.axis_size(gx), lax.axis_size("gy")
    at_x, at_y = lax.axis_index(gx), lax.axis_index("gy")
    flags = jnp.stack([at_x > 0, at_x < n_gx - 1, at_y > 0, at_y < n_gy - 1, at_x % 2 == 1]).astype(F32)

    def exchange(axis, up, down):
        n = lax.axis_size(axis)
        forward = [(i, i + 1) for i in range(n - 1)]
        backward = [(i + 1, i) for i in range(n - 1)]
        return lax.ppermute(up, axis, forward), lax.ppermute(down, axis, backward)

    def exchange_x(first, second):
        pairs = [[(i + k, i + 1 - k) for i in range(start, n_gx - 1, 2) for k in (0, 1)] for start in (1, 0)]
        return lax.ppermute(first, gx, pairs[0]), lax.ppermute(second, gx, pairs[1])

    def swap(value):
        return lax.ppermute(value, "gz", [(0, 1), (1, 0)])

    plane, forward, inverse, denom, eigen = tables()
    own = C * C
    box = EXT * EXT

    def buffer(rows):
        return pltpu.VMEM((rows, CZ), F32)

    up, down = call(
        strips_kernel, (YROWS, YROWS), guess_field, conduct_field, right_side,
        scratch=[pltpu.VMEM((C, C, CZ), F32)] * 3 + [pltpu.SemaphoreType.DMA((3, 2))],
        hbm=(0, 1, 2), limit=56, name="strips", work=2,
    )
    part, edge = call(residual_kernel, (own, 160), v, h, b, name="residual", work=2)
    low, high = exchange("gy", up, down)
    pairs, scale_a, scale_b = call(
        prepare_kernel, (own, box, box), eigen, v, h, denom, smem=(0,), name="prepare", work=2
    )
    (middle,) = call(pack_middle_kernel, (24 * BLOCKS_Z,), part, pairs, name="pack_middle", work=1)
    right, left, faces = call(
        extend_y_kernel, (XROWS, XROWS, 4 * EXT),
        flags, part, pairs, up, down, edge, low, high, middle,
        scratch=[buffer(XROWS)] * 2, smem=(0,), name="extend_y", work=1,
    )
    one, two = exchange_x(right, left)
    inner, part = call(
        inner_kernel, (38 * EXT, C * EXT),
        flags, plane, part, up, down, low, high, smem=(0,), name="inner", work=1,
    )
    (packed,) = call(pack_z_kernel, (ZROWS,), part, pairs, low, high, middle, name="pack_z", work=2)
    own_z, fluxes = call(
        extend_x_kernel, (ZROWS, 2 * EXT), flags, packed, faces, one, two, inner,
        smem=(0,), name="extend_x", work=1,
    )
    far_z = swap(own_z)
    (main,) = call(
        forward_kernel, (box,), flags, plane, part, inner, fluxes, one, two,
        scratch=[buffer(box)], smem=(0,), name="forward", work=2,
    )
    c_x, c_down, c_up, c_z = call(
        coefficients_kernel, (own + C, own, own, own), flags, h, low, high, one, two,
        scratch=[buffer(own + 2 * C)], smem=(0,), name="coefficients", work=1,
    )
    second_a, second_b, sides, side_strip, right, left = call(
        solve_kernel, (box, box, 18 * EXT, 18 * EXT, XROWS2, XROWS2),
        flags, c_z, own_z, far_z, main, plane, forward, inverse, scale_a, scale_b,
        scratch=[buffer(box), buffer(XROWS2), buffer(XROWS2)], smem=(0,), name="solve", work=6,
    )
    resid, c_face = call(
        own_kernel, (own, own), part, fluxes, own_z, far_z, name="own", work=1
    )
    one, two = exchange_x(right, left)
    sol, strip = call(
        rest_kernel, (42 * EXT, 42 * EXT),
        plane, inverse, second_a, second_b, sides, side_strip, name="rest", work=2,
    )
    sol, up, down, own_z, across_up, across_down = call(
        fold_x_kernel, (42 * EXT, YROWS2, YROWS2, ZROWS2, 32, 32),
        flags, sol, strip, one, two, resid,
        scratch=[buffer(42 * EXT), buffer(144)], smem=(0,), name="fold_x", work=1,
    )
    low, high = exchange("gy", up, down)
    far_z = swap(own_z)
    diagonal = [((j, k), (j + 1, 1 - k)) for j in range(n_gy - 1) for k in range(2)]
    pairs = [(2 * a + b, 2 * c + d) for (a, b), (c, d) in diagonal]
    far_low = lax.ppermute(across_up, ("gy", "gz"), pairs)
    far_high = lax.ppermute(across_down, ("gy", "gz"), [(b, a) for a, b in pairs])
    (sol,) = call(
        fold_y_kernel, (42 * EXT,), flags, sol, low, high, smem=(0,), name="fold_y", work=1
    )
    first, last = splits
    field, applied, sums = call(
        apply_kernel, (own, own, lax.axis_size(first)),
        sol, low, high, own_z, far_z, far_low, far_high, resid, c_x, c_down, c_up, c_z, c_face, h,
        scratch=[buffer(42 * EXT), buffer(ZROWS2 + 64), buffer(48)], name="apply", work=3,
    )
    sums = lax.all_to_all(sums, first, 0, 0, tiled=True)
    (sums,) = call(gather_kernel, (lax.axis_size(last),), sums, name="gather")
    sums = lax.all_to_all(sums, last, 0, 0, tiled=True)
    out, resid = call(update_kernel, (own, own), sums, v, resid, field, applied, name="update", work=2)
    return out.reshape(shape), resid.reshape(shape)


def solution(mesh):
    n_gx, n_gy, n_gz = mesh.devices.shape
    if n_gx == 64:
        mesh = Mesh(mesh.devices.reshape(4, 8, 2, n_gy, n_gz), ("gx_x", "gx_y", "gx_c", "gy", "gz"))
        gx = ("gx_x", "gx_y", "gx_c")
        splits = (("gx_c", "gy", "gz"), ("gx_x", "gx_y"))
    else:
        gx = "gx"
        splits = (("gx",), ("gy", "gz"))
    placed = P(gx, "gy", "gz")
    return jax.shard_map(
        functools.partial(on_device, gx, splits),
        mesh=mesh,
        in_specs=(placed,) * 3,
        out_specs=(placed,) * 2,
        check_vma=False,
    )
```

```python
import functools

import jax
import jax.numpy as jnp
import ml_dtypes
import numpy as np
from jax import lax
from jax.experimental import pallas as pl
from jax.experimental.pallas import tpu as pltpu
from jax.sharding import Mesh
from jax.sharding import PartitionSpec as P

OVER = 8
C = 40
CZ = 128
EXT = C + 2 * OVER
EXTZ = CZ + 2 * OVER
TILES = EXT // 8
stiff_scale = 3.0
mass_term = 0.001

F32 = jnp.float32
BF16 = jnp.bfloat16
VMEM = pl.BlockSpec(memory_space=pltpu.VMEM)
SMEM = pl.BlockSpec(memory_space=pltpu.SMEM)
HBM = pl.BlockSpec(memory_space=pltpu.HBM)

YROWS = 440
XROWS = 616
PER_Z = 12
BLOCKS_Z = -(-EXT // PER_Z)
ZROWS = BLOCKS_Z * EXT
PER = 14
XROWS2 = 9 * EXT + 40
YROWS2 = 416
ZGROUPS2 = 42 * 5 + 12
ZROWS2 = 8 * -(-ZGROUPS2 // PER)


def sine_table(count):
    k = np.arange(1, count + 1)
    basis = np.sqrt(2.0 / (count + 1)) * np.sin(np.pi * k[:, None] * k[None, :] / (count + 1))
    eigen = 2.0 - 2.0 * np.cos(np.pi * k / (count + 1))
    return basis, eigen


def two_parts(table):
    high = table.astype(ml_dtypes.bfloat16)
    low = (table - high.astype(np.float64)).astype(ml_dtypes.bfloat16)
    return high, low


@functools.cache
def tables():
    basis, eigen = sine_table(EXT)
    basis_z, eigen_z = sine_table(EXTZ)
    high, low = two_parts(basis)
    plane = np.zeros((EXT, 192), ml_dtypes.bfloat16)
    plane[:, 0:EXT] = high
    plane[:, 64 : 64 + EXT] = low
    plane[:, 128 : 128 + EXT] = high
    forward = np.zeros((2, 256, 256))
    inverse = np.zeros((2, 256, 256))
    for gz in range(2):
        own = basis_z[8 : 8 + CZ]
        strip = basis_z[136:144] if gz == 0 else basis_z[0:8]
        face_own, face_far = (135, 136) if gz == 0 else (8, 7)
        forward[gz, :CZ, :EXTZ] = own
        forward[gz, CZ, :EXTZ] = basis_z[face_own] - basis_z[face_far]
        forward[gz, CZ + 2 : CZ + 10, :EXTZ] = strip
        inverse[gz, :EXTZ, :CZ] = own.T
        inverse[gz, :EXTZ, CZ : CZ + 9] = (basis_z[135:144] if gz == 0 else basis_z[0:9]).T

    def stacked(table):
        high, low = two_parts(table)
        return np.concatenate([high, high, low], axis=1)

    denom = np.full((EXT, 256), 1.0)
    denom[:, :EXTZ] = stiff_scale * (eigen[:, None] + eigen_z[None, :]) + mass_term
    return (
        plane,
        stacked(forward),
        stacked(inverse),
        denom.astype(np.float32),
        (stiff_scale * eigen).astype(np.float32),
    )


def roll(value, shift, axis):
    if isinstance(shift, int):
        shift = shift % value.shape[axis]
        return value if shift == 0 else pltpu.roll(value, shift, axis)
    return pltpu.roll(value, lax.rem(shift + 2 * value.shape[axis], value.shape[axis]), axis)


def lanes(rows):
    return lax.broadcasted_iota(jnp.int32, (rows, CZ), 1)


def rows_at(start, size):
    return pl.ds(pl.multiple_of(start, 8), size)


def tile_at(index):
    return rows_at(index * 8, 8)


def call(body, out_rows, *args, scratch=(), limit=16, name=None, smem=(), hbm=(), work=0):
    place = {**{i: SMEM for i in smem}, **{i: HBM for i in hbm}}
    return pl.pallas_call(
        body,
        out_shape=[jax.ShapeDtypeStruct((rows, CZ), F32) for rows in out_rows],
        in_specs=[place.get(i, VMEM) for i in range(len(args))],
        out_specs=[VMEM] * len(out_rows),
        scratch_shapes=list(scratch),
        compiler_params=pltpu.CompilerParams(vmem_limit_bytes=limit * 2**20),
        cost_estimate=pl.CostEstimate(
            flops=int(work * 1e9), bytes_accessed=int(work * 2e6), transcendentals=0
        )
        if work
        else None,
        name=name,
    )(*args)


def strip_base():
    return jnp.where(lax.axis_index("gz") == 0, 118, 126)


def face_lane():
    return jnp.where(lax.axis_index("gz") == 0, 127, 0)


def outer_lane():
    return jnp.where(lax.axis_index("gz") == 0, 0, 127)


def pair_of(v, h, lane, base, face):
    return jnp.where(lane == base, roll(v, base - face, 1), 0.0) + jnp.where(
        lane == base + 1, roll(h, base + 1 - face, 1), 0.0
    )


def strips_kernel(v_in, h_in, b_in, up, down, v, h, b, sems):
    copies = []
    for k, (source, target, size) in enumerate(((v_in, v, 16), (h_in, h, 16), (b_in, b, 8))):
        for side, first in enumerate((0, C - size)):
            at = pl.ds(first, size)
            copies.append(
                pltpu.make_async_copy(source.at[:, at, :], target.at[:, at, :], sems.at[k, side])
            )
            copies[-1].start()
    base, face = strip_base(), face_lane()
    lane = lanes(8)
    row = lax.broadcasted_iota(jnp.int32, (8, CZ), 0)
    z_half = jnp.where(lane < CZ - 1, 0.5, 0.0)
    outer = jnp.where(lane == outer_lane(), 0.5, 0.0)
    last = C - 1
    for copy in copies:
        copy.wait()

    def tile(x, start, beyond, sign, flux_x):
        following = jnp.minimum(x + 1, last)
        at, to = pl.ds(start, 8), pl.ds(beyond, 8)
        vi, hi = v[x, at, :], h[x, at, :]
        next_x = 0.5 * (hi + h[following, at, :]) * (v[following, at, :] - vi)
        flux_y = 0.5 * (hi + h[x, to, :]) * (v[x, to, :] - vi)
        edge = 0 if sign > 0 else 7
        net_y = flux_y - jnp.where(row == edge, 0.0, roll(flux_y, sign, 0))
        flux_z = z_half * (hi + roll(hi, -1, 1)) * (roll(vi, -1, 1) - vi)
        applied = (
            mass_term * vi
            - (next_x - flux_x)
            - net_y
            - (flux_z - roll(flux_z, 1, 1))
            + outer * hi * vi
        )
        return b[x, at, :] - applied, next_x, vi, hi

    def visit(x, carry):
        flux_up, flux_down, pack_up, pack_down = carry
        resid, flux_down, vi, hi = tile(x, 0, 1, 1, flux_down)
        down[tile_at(x), :] = resid
        down[pl.ds(320 + x, 1), :] = vi[0:1]
        down[pl.ds(360 + x, 1), :] = hi[0:1]
        pack_down = pack_down + roll(pair_of(vi, hi, lane, base, face), 2 * x - base, 1)
        resid, flux_up, vi, hi = tile(x, 32, 31, -1, flux_up)
        up[tile_at(x), :] = resid
        up[pl.ds(320 + x, 1), :] = vi[7:8]
        up[pl.ds(360 + x, 1), :] = hi[7:8]
        pack_up = pack_up + roll(pair_of(vi, hi, lane, base, face), 2 * x - base, 1)
        return flux_up, flux_down, pack_up, pack_down

    zero = jnp.zeros((8, CZ), F32)
    _, _, pack_up, pack_down = lax.fori_loop(0, C, visit, (zero,) * 4, unroll=20)
    up[432:440, :] = pack_up
    down[432:440, :] = pack_down
    for message, first in ((up, 32), (down, 0)):
        at = pl.ds(first, 8)
        message[400:408, :] = v[0, at, :]
        message[408:416, :] = h[0, at, :]
        message[416:424, :] = v[last, at, :]
        message[424:432, :] = h[last, at, :]


def residual_kernel(v, h, b, part, edge):
    lane = lanes(C)
    row = lax.broadcasted_iota(jnp.int32, (C, CZ), 0)
    y_half = jnp.where(row > 0, 0.5, 0.0)
    z_half = jnp.where(lane < CZ - 1, 0.5, 0.0)
    outer = jnp.where(lane == outer_lane(), 0.5, 0.0)

    def visit(x, flux_x):
        own = rows_at(x * C, C)
        following = rows_at(jnp.minimum(x + 1, C - 1) * C, C)
        vi, hi = v[own, :], h[own, :]
        next_x = 0.5 * (hi + h[following, :]) * (v[following, :] - vi)
        flux_y = y_half * (hi + roll(hi, 1, 0)) * (vi - roll(vi, 1, 0))
        flux_z = z_half * (hi + roll(hi, -1, 1)) * (roll(vi, -1, 1) - vi)
        applied = (
            mass_term * vi
            - (next_x - flux_x)
            - (roll(flux_y, -1, 0) - flux_y)
            - (flux_z - roll(flux_z, 1, 1))
            + outer * hi * vi
        )
        part[own, :] = b[own, :] - applied
        return next_x

    lax.fori_loop(0, C, visit, jnp.zeros((C, CZ), F32), unroll=4)
    last = (C - 1) * C
    edge[0:40, :] = v[0:40, :]
    edge[40:80, :] = h[0:40, :]
    edge[80:120, :] = v[last : last + 40, :]
    edge[120:160, :] = h[last : last + 40, :]


def prepare_kernel(eigen, v, h, denom, out, out_a, out_b):
    base, face = strip_base(), face_lane()
    lane = lanes(C)

    def visit_pair(x, _):
        at = rows_at(x * C, C)
        out[at, :] = pair_of(v[at, :], h[at, :], lane, base, face)
        return 0

    lax.fori_loop(0, C, visit_pair, 0, unroll=8)

    def visit(y, _):
        value = 1.0 / (denom[...] + eigen[y])
        at = rows_at(y * EXT, EXT)
        out_a[at, :] = value[:, :CZ]
        out_b[at, :] = value[:, CZ:]
        return 0

    lax.fori_loop(0, EXT, visit, 0, unroll=4)


def choose(flag, a, b):
    return jnp.where(flag > 0.5, a, b)


def by_parity(flags, first, second):
    def before(start, stop):
        return choose(flags[4], second[start:stop, :], first[start:stop, :])

    def after(start, stop):
        return choose(flags[4], first[start:stop, :], second[start:stop, :])

    return before, after


def pick(pack, index, to):
    pair = lax.div(lanes(8), 2) == index
    return roll(jnp.where(pair, pack, 0.0), to - 2 * index, 1)


def strip_mask():
    lane = lanes(8)
    return jnp.where(lax.axis_index("gz") == 0, lane - 120, 7 - lane) >= 0


def y_fluxes(up, down, low, high):
    flux_a = 0.5 * (low[360:400, :] + down[360:400, :]) * (down[320:360, :] - low[320:360, :])
    flux_b = 0.5 * (up[360:400, :] + high[360:400, :]) * (high[320:360, :] - up[320:360, :])
    return flux_a, flux_b


def extend_y(flags, fluxes, part, low, high, out, start, stop):
    for x in range(start, stop):
        at = (x - start) * EXT
        out[at : at + 8, :] = low[8 * x : 8 * x + 8, :]
        out[at + 8 : at + 48, :] = part[x * C : x * C + C, :]
        out[at + 48 : at + 56, :] = high[8 * x : 8 * x + 8, :]
    flux_a, flux_b = (flux[start:stop] for flux in fluxes)
    for row, value in ((8, -flux_a), (7, flux_a * flags[2]), (47, flux_b), (48, -flux_b * flags[3])):
        at = pl.ds(row, stop - start, stride=EXT)
        out[at, :] = out[at, :] + value


def extend_y_kernel(flags, part, vh, up, down, edge, low, high, _, first, second, faces, right, left):
    base, strip_lanes = strip_base(), strip_mask()
    fluxes = y_fluxes(up, down, low, high)
    for message, start, strip, own in ((left, 0, 400, 0), (right, 32, 416, 80)):
        extend_y(flags, fluxes, part, low, high, message, start, start + OVER)
        for k in range(2):
            at = 448 + k * EXT
            message[at : at + 8, :] = low[strip + 8 * k : strip + 8 * k + 8, :]
            message[at + 8 : at + 48, :] = edge[own + 40 * k : own + 40 * k + 40, :]
            message[at + 48 : at + 56, :] = high[strip + 8 * k : strip + 8 * k + 8, :]
        for t in range(TILES):
            near = jnp.zeros((8, CZ), F32)
            taken = jnp.zeros((8, CZ), F32)
            for i in range(OVER):
                x = start + i
                at = i * EXT + 8 * t
                value = jnp.where(strip_lanes, message[at : at + 8, :], 0.0)
                if t == 0:
                    taken = taken + pick(low[432:440, :], x, 10 * i)
                elif t == 6:
                    taken = taken + pick(high[432:440, :], x, 10 * i)
                else:
                    value = value + vh[x * C + 8 * t - 8 : x * C + 8 * t, :]
                near = near + roll(value, 10 * i, 1)
            message[560 + 8 * t : 568 + 8 * t, :] = roll(near, -base, 1) + taken
    faces[0:112, :] = left[448:560, :]
    faces[112:224, :] = right[448:560, :]
    first[...] = choose(flags[4], right[...], left[...])
    second[...] = choose(flags[4], left[...], right[...])


def pack_planes(tiles, value_of, taken_of):
    base = strip_base()
    packs = {}
    for q in range(BLOCKS_Z):
        for t in tiles:
            near = jnp.zeros((8, CZ), F32)
            taken = jnp.zeros((8, CZ), F32)
            for j in range(PER_Z):
                x = q * PER_Z + j - OVER
                if 0 <= x < C:
                    near = near + roll(value_of(x, t), 10 * j, 1)
                    if t in (0, 6):
                        taken = taken + taken_of(x, t, 10 * j)
            packs[q, t] = roll(near, -base, 1) + taken
    return packs


def pack_middle_kernel(part, vh, out):
    strip_lanes = strip_mask()

    def value_of(x, t):
        at = pl.ds(x * C + 8 * t - 8, 8)
        return jnp.where(strip_lanes, part[at, :], 0.0) + vh[at, :]

    for (q, t), value in pack_planes((2, 3, 4), value_of, None).items():
        at = q * 24 + 8 * (t - 2)
        out[at : at + 8, :] = value


def pack_z_kernel(part, vh, low, high, middle, message):
    strip_lanes = strip_mask()

    def value_of(x, t):
        value = jnp.where(strip_lanes, part[x * EXT + 8 * t : x * EXT + 8 * t + 8, :], 0.0)
        if t in (1, 5):
            value = value + vh[x * C + 8 * t - 8 : x * C + 8 * t, :]
        return value

    def taken_of(x, t, lane):
        return pick((low if t == 0 else high)[432:440, :], x, lane)

    for q in range(BLOCKS_Z):
        message[q * EXT + 16 : q * EXT + 40, :] = middle[24 * q : 24 * q + 24, :]
    for (q, t), value in pack_planes((0, 1, 5, 6), value_of, taken_of).items():
        at = q * EXT + 8 * t
        message[at : at + 8, :] = value


def extend_x_kernel(flags, packed, faces, first, second, inner, message, fluxes):
    base, strip_lanes = strip_base(), strip_mask()
    before, after = by_parity(flags, first, second)
    flux_a = 0.5 * (before(504, 560) + faces[56:112, :]) * (faces[0:56, :] - before(448, 504))
    flux_b = 0.5 * (faces[168:224, :] + after(504, 560)) * (after(448, 504) - faces[112:168, :])
    fluxes[0:EXT, :] = flux_a
    fluxes[EXT : 2 * EXT, :] = flux_b
    message[...] = packed[...]
    end = (BLOCKS_Z - 1) * EXT
    message[0:EXT, :] = message[0:EXT, :] + before(560, 616)
    message[end : end + EXT, :] = message[end : end + EXT, :] + after(560, 616)

    def add(x, t, value):
        q, j = divmod(x, PER_Z)
        at = q * EXT + 8 * t
        message[at : at + 8, :] = message[at : at + 8, :] + roll(value, 10 * j, 1)

    for t in range(TILES):
        a = roll(jnp.where(strip_lanes, flux_a[8 * t : 8 * t + 8], 0.0), -base, 1)
        b = roll(jnp.where(strip_lanes, flux_b[8 * t : 8 * t + 8], 0.0), -base, 1)
        add(OVER - 1, t, a * flags[0])
        add(OVER, t, -a)
        add(OVER + C - 1, t, b)
        add(OVER + C, t, -b * flags[1])


def halves(value):
    high = value.astype(BF16)
    return high, (value - high.astype(F32)).astype(BF16)


def dot(a, b):
    return jnp.dot(a, b, preferred_element_type=F32)


def along_lanes(value, table):
    high, low = halves(value)
    return dot(jnp.concatenate([high, low, high], axis=1), table)


def along_rows(table, value):
    padded = jnp.concatenate([value, jnp.zeros((8, value.shape[1]), F32)], axis=0)
    high, low = halves(padded)
    return dot(table, jnp.concatenate([high, high, low], axis=0))


def beside(a, b):
    return jnp.concatenate([a, b], axis=1)


def inner_kernel(flags, plane, box, up, down, low, high, out, part):
    table = plane[...]
    extend_y(flags, y_fluxes(up, down, low, high), box, low, high, part, 0, C)
    for x in range(1, C - 1, 2):
        at, then = pl.ds(x * EXT, EXT), pl.ds((x + 1) * EXT, EXT)
        value = along_rows(table, beside(part[at, :], part[then, :]))
        out[(x - 1) * EXT : x * EXT, :] = value[:, :CZ]
        out[x * EXT : (x + 1) * EXT, :] = value[:, CZ:]


def forward_kernel(flags, plane, part, inner, fluxes, one, two, out, first):
    before, after = by_parity(flags, one, two)
    table = plane[...]
    flux_a, flux_b = fluxes[0:EXT, :], fluxes[EXT : 2 * EXT, :]
    planes = {x: before(x * EXT, (x + 1) * EXT) for x in range(OVER)}
    planes[7] = planes[7] + flux_a * flags[0]
    planes[8] = part[0:EXT, :] - flux_a
    planes[47] = part[(C - 1) * EXT : C * EXT, :] + flux_b
    planes.update({48 + x: after(x * EXT, (x + 1) * EXT) for x in range(OVER)})
    planes[48] = planes[48] - flux_b * flags[1]
    first[9 * EXT : 47 * EXT, :] = inner[...]
    order = sorted(planes)
    for x, then in zip(order[0::2], order[1::2]):
        value = along_rows(table, beside(planes[x], planes[then]))
        first[x * EXT : (x + 1) * EXT, :] = value[:, :CZ]
        first[then * EXT : (then + 1) * EXT, :] = value[:, CZ:]

    def visit_x(c, _):
        for i in range(14):
            y = 2 * (c * 14 + i)
            value = beside(first[pl.ds(y, EXT, stride=EXT), :], first[pl.ds(y + 1, EXT, stride=EXT), :])
            value = along_rows(table, value)
            out[rows_at(y * EXT, EXT), :] = value[:, :CZ]
            out[rows_at((y + 1) * EXT, EXT), :] = value[:, CZ:]
        return 0

    lax.fori_loop(0, 2, visit_x, 0)


def face_terms(own_z, far_z):
    both = own_z[...] + far_z[...]
    half = 0.5 * roll(both, -1, 1)
    return half, half * (far_z[...] - own_z[...])


STEP = 28


def solve_kernel(
    flags, own_z, far_z, main, plane, forward, inverse, scale_a, scale_b,
    second_a, second_b, sol, strip, first, second, halo, right, left,
):
    gz = lax.axis_index("gz")
    table = plane[...]
    _, flux = face_terms(own_z, far_z)
    pack = jnp.where(lax.rem(lanes(ZROWS), 10) == 0, flux, far_z[...])
    blocks = [pack[q * EXT : (q + 1) * EXT] for q in range(BLOCKS_Z)]
    done = []
    for q in range(0, BLOCKS_Z - 1, 2):
        value = along_rows(table, beside(blocks[q], blocks[q + 1]))
        done += [value[:, :CZ], value[:, CZ:]]
    done.append(along_rows(table, blocks[-1]))
    for x in range(EXT):
        q, j = x // PER_Z, x % PER_Z
        halo[x * EXT : (x + 1) * EXT, :] = roll(done[q], -10 * j, 1)

    forward_table = forward[gz]
    inverse_table = inverse[gz]

    def visit(c, _):
        parts = []
        for i in range(0, STEP, 2):
            y = c * STEP + i
            value = beside(halo[pl.ds(y, EXT, stride=EXT), :], halo[pl.ds(y + 1, EXT, stride=EXT), :])
            value = along_rows(table, value)
            parts.append(beside(main[rows_at(y * EXT, EXT), :], value[:, :CZ]))
            parts.append(beside(main[rows_at((y + 1) * EXT, EXT), :], value[:, CZ:]))
        value = along_lanes(jnp.concatenate(parts, axis=0), forward_table)
        at = rows_at(c * STEP * EXT, STEP * EXT)
        value = value * beside(scale_a[at, :], scale_b[at, :])
        for i in range(STEP):
            part = along_rows(table, value[i * EXT : (i + 1) * EXT])
            to = pl.ds(c * STEP + i, EXT, stride=EXT)
            second_a[to, :] = part[:, :CZ]
            second_b[to, :] = part[:, CZ:]
        return 0

    lax.fori_loop(0, EXT // STEP, visit, 0)

    for k, (message, start) in enumerate(((left, 0), (right, 47))):
        inverse_planes(table, inverse_table, second_a, second_b, sol, strip, range(start, start + 9), 9 * k)
        message[0 : 9 * EXT, :] = sol[9 * k * EXT : 9 * (k + 1) * EXT, :]
        tiles = [strip[pl.ds((9 * k * TILES + j) * 8, 8), :] for j in range(63)]
        pack_tiles(message, 9 * EXT, tiles)
    first[...] = choose(flags[4], right[...], left[...])
    second[...] = choose(flags[4], left[...], right[...])


def inverse_planes(table, inverse_table, second_a, second_b, sol, strip, planes, to):
    parts = []
    for x in planes:
        at = pl.ds(x * EXT, EXT)
        parts.append(along_rows(table, beside(second_a[at, :], second_b[at, :])))
    value = along_lanes(jnp.concatenate(parts, axis=0), inverse_table)
    at = pl.ds(to * EXT, len(planes) * EXT)
    sol[at, :] = value[:, :CZ]
    strip[at, :] = value[:, CZ:]


def rest_kernel(plane, inverse, second_a, second_b, sides, side_strip, sol, strip):
    table, inverse_table = plane[...], inverse[lax.axis_index("gz")]
    for first, last in ((9, 19), (19, 29), (29, 38), (38, 47)):
        inverse_planes(
            table, inverse_table, second_a, second_b, sol, strip, range(first, last), first - 7
        )
    for target, source in ((sol, sides), (strip, side_strip)):
        target[0 : 2 * EXT, :] = source[7 * EXT : 9 * EXT, :]
        target[40 * EXT : 42 * EXT, :] = source[9 * EXT : 11 * EXT, :]


def own_kernel(flags, h, low, high, one, two, part, fluxes, own_z, far_z, resid, c_x, c_down, c_up, c_z, c_face, cond):
    face, outer = face_lane(), outer_lane()
    half, flux = face_terms(own_z, far_z)
    half, flux = roll(half, face, 1), roll(flux, face, 1)
    lane8 = lanes(8)
    for x in range(C):
        q, j = (x + OVER) // PER_Z, (x + OVER) % PER_Z
        for t in range(5):
            at = q * EXT + 8 * (t + 1)
            to = x * C + 8 * t
            source = x * EXT + 8 * (t + 1)
            moved = jnp.where(lane8 == face, roll(flux[at : at + 8], -10 * j, 1), 0.0)
            if x == 0:
                moved = moved - fluxes[source : source + 8, :]
            elif x == C - 1:
                moved = moved + fluxes[source + EXT - x * EXT : source + EXT - x * EXT + 8, :]
            resid[to : to + 8, :] = part[source : source + 8, :] + moved
            c_face[to : to + 8, :] = jnp.where(
                lane8 == face, roll(half[at : at + 8], -10 * j, 1), 0.0
            )
    before, after = by_parity(flags, one, two)
    cond[0:C, :] = before(512, 552)
    cond[C : C + C * C, :] = h[...]
    cond[C + C * C :, :] = after(512, 552)
    z_half = jnp.where(lanes(C) < CZ - 1, 0.5, 0.0)
    row = lax.broadcasted_iota(jnp.int32, (C, CZ), 0)
    for x in range(C):
        at = x * C
        hi = h[at : at + C, :]
        c_x[at : at + C, :] = 0.5 * (cond[at : at + C, :] + hi)
        below = jnp.where(row == 0, low[360 + x : 361 + x, :], roll(hi, 1, 0))
        above = jnp.where(row == C - 1, high[360 + x : 361 + x, :], roll(hi, -1, 0))
        c_down[at : at + C, :] = 0.5 * (hi + below)
        c_up[at : at + C, :] = 0.5 * (hi + above)
        c_z[at : at + C, :] = z_half * (hi + roll(hi, -1, 1))
    c_x[C * C :, :] = 0.5 * (cond[C * C : C * C + C, :] + cond[C * C + C :, :])


def pack_tiles(message, at, values):
    for q in range(-(-len(values) // PER)):
        acc = values[q * PER]
        for j, value in enumerate(values[q * PER + 1 : (q + 1) * PER], 1):
            acc = acc + roll(value, 9 * j, 1)
        message[at + 8 * q : at + 8 * q + 8, :] = acc


def unpack_tile(message, at, index):
    q = index // PER
    return roll(message[rows_at(at + 8 * q, 8), :], -9 * (index - q * PER), 1)


def fold_x_kernel(
    flags, sol, strip, one, two, _, out, up, down, across, across_up, across_down, out_strip, line
):
    size = 42 * EXT
    narrow = lanes(8) < 9
    before, after = by_parity(flags, one, two)
    tail = 33 * EXT
    out[0 : 9 * EXT, :] = sol[0 : 9 * EXT, :] + before(0, 9 * EXT)
    out[9 * EXT : tail, :] = sol[9 * EXT : tail, :]
    out[tail:size, :] = sol[tail:size, :] + after(0, 9 * EXT)
    out_strip[9 * EXT : tail, :] = strip[9 * EXT : tail, :]
    packs = [side(9 * EXT, XROWS2) for side in (before, after)]

    for j in range(63):
        q, i = divmod(j, PER)
        for pack, at in ((packs[0], 8 * j), (packs[1], tail + 8 * j)):
            value = jnp.where(narrow, roll(pack[8 * q : 8 * q + 8], -9 * i, 1), 0.0)
            out_strip[at : at + 8, :] = strip[at : at + 8, :] + value

    for array in (out, out_strip):
        array[0:EXT, :] = array[0:EXT, :] * flags[0]
        array[41 * EXT : size, :] = array[41 * EXT : size, :] * flags[1]

    for message, tile, single in ((up, 6, 47), (down, 0, 8)):
        for p in range(42):
            message[8 * p : 8 * p + 8, :] = out[p * EXT + 8 * tile : p * EXT + 8 * tile + 8, :]
        message[376:384, :] = jnp.zeros((8, CZ), F32)
        message[336:378, :] = out[pl.ds(single, 42, stride=EXT), :]
        line[40:48, :] = jnp.zeros((8, CZ), F32)
        line[0:42, :] = out_strip[pl.ds(single, 42, stride=EXT), :]
        values = [out_strip[p * EXT + 8 * tile : p * EXT + 8 * tile + 8, :] for p in range(42)]
        values += [line[8 * j : 8 * j + 8, :] for j in range(6)]
        pack_tiles(message, 384, values)
    across_up[...] = up[384:416, :]
    across_down[...] = down[384:416, :]
    values = []
    for p in range(42):
        for t in range(1, 6):
            at = p * EXT + 8 * t
            values.append(out_strip[at : at + 8, :])
    for k, single in enumerate((7, 48)):
        at = 48 * (k + 1)
        line[at + 40 : at + 48, :] = jnp.zeros((8, CZ), F32)
        line[at : at + 42, :] = out_strip[pl.ds(single, 42, stride=EXT), :] * flags[2 + k]
        values += [line[at + 8 * j : at + 8 * j + 8, :] for j in range(6)]
    pack_tiles(across, 0, values)


def fold_y_kernel(flags, sol, low, high, out):
    for p in range(42):
        for message, tile in ((low, 1), (high, 5)):
            at = p * EXT + 8 * tile
            out[at : at + 8, :] = sol[at : at + 8, :] + message[8 * p : 8 * p + 8, :]
        at = p * EXT
        out[at : at + 8, :] = sol[at : at + 8, :]
        out[at + 16 : at + 40, :] = sol[at + 16 : at + 40, :]
        out[at + 48 : at + 56, :] = sol[at + 48 : at + 56, :]
    for k, (single, message) in enumerate(((7, low), (48, high))):
        at = pl.ds(single, 42, stride=EXT)
        out[at, :] = (out[at, :] + message[336:378, :]) * flags[2 + k]


def apply_kernel(
    sol, low, high, own_z, far_z, far_low, far_high, resid, c_x, c_down, c_up, c_z, c_face, h,
    out, applied, sums, field, pack, line,
):
    gz = lax.axis_index("gz")
    end = YROWS2 - 384
    lane = lanes(ZROWS2 + 2 * end)
    at_face = lax.rem(lane, 9) == jnp.where(gz == 0, 8, 0)
    shift = jnp.where(gz == 0, 7, 121)
    near = jnp.concatenate([own_z[...], low[384:YROWS2, :], high[384:YROWS2, :]], axis=0)
    got = jnp.concatenate([far_z[...], far_low[...], far_high[...]], axis=0)
    got = got + jnp.where(at_face, roll(near, shift, 1), 0.0)
    pack[...] = roll(got, jnp.where(gz == 0, 120, 127), 1)
    toward = jnp.where(gz == 0, 127, 1)
    lane8 = lanes(8)
    folded = jnp.where(gz == 0, lane8 - 120, 7 - lane8) >= 0

    def tile(index, start=0):
        q, j = divmod(index, PER)
        return roll(pack[start + 8 * q : start + 8 * q + 8, :], -9 * j, 1)

    def along_z(p, t):
        value = tile(p * 5 + t - 1)
        if t == 1:
            value = value + tile(p, ZROWS2)
        if t == 5:
            value = value + tile(p, ZROWS2 + end)
        return value

    for p in range(42):
        for t in range(1, 6):
            at = p * EXT + 8 * t
            value = sol[at : at + 8, :] + jnp.where(folded, along_z(p, t), 0.0)
            field[at : at + 8, :] = value
    for k, single in enumerate((7, 48)):
        for j in range(6):
            value = tile(210 + 6 * k + j) + tile(42 + j, ZROWS2 + k * end)
            line[8 * j : 8 * j + 8, :] = jnp.where(folded, value, 0.0)
        at = pl.ds(single, 42, stride=EXT)
        field[at, :] = sol[at, :] + line[0:42, :]
    pack[...] = roll(pack[...], toward, 1)

    outer = jnp.where(lanes(C) == outer_lane(), 0.5, 0.0)
    flux_x = c_x[0:C, :] * (field[EXT + 8 : EXT + 48, :] - field[8:48, :])
    sum_a = jnp.zeros((8, CZ), F32)
    sum_b = jnp.zeros((8, CZ), F32)
    def visit(x, carry):
        flux_x, sum_a, sum_b = carry
        at = (x + 1) * EXT
        to = rows_at(x * C, C)
        z = field[rows_at(at + 8, C), :]
        next_x = c_x[rows_at(x * C + C, C), :] * (field[rows_at(at + EXT + 8, C), :] - z)
        net = next_x - flux_x
        net = net + c_up[to, :] * (field[pl.ds(at + 9, C), :] - z)
        net = net - c_down[to, :] * (z - field[pl.ds(at + 7, C), :])
        flux_z = c_z[to, :] * (roll(z, -1, 1) - z)
        net = net + (flux_z - roll(flux_z, 1, 1)) + c_face[to, :] * (out[to, :] - z)
        image = mass_term * z - net + outer * h[to, :] * z
        out[to, :] = z
        applied[to, :] = image
        a, b = resid[to, :] * z, z * image
        for t in range(5):
            sum_a = sum_a + a[8 * t : 8 * t + 8]
            sum_b = sum_b + b[8 * t : 8 * t + 8]
        return next_x, sum_a, sum_b

    for x in range(C):
        for t in range(5):
            out[x * C + 8 * t : x * C + 8 * t + 8, :] = along_z(x + 1, t + 1)
    _, sum_a, sum_b = lax.fori_loop(0, C, visit, (flux_x, sum_a, sum_b), unroll=20)
    total_a = jnp.sum(sum_a, axis=0, keepdims=True)
    total_b = jnp.sum(sum_b, axis=0, keepdims=True)
    total_a = total_a + roll(total_a, CZ // 2, 1)
    total_b = total_b + roll(total_b, CZ // 2, 1)
    total = jnp.where(lanes(1) < CZ // 2, total_a, total_b)
    sums[...] = jnp.broadcast_to(total, sums.shape)


def gather_kernel(sums, out):
    out[...] = jnp.broadcast_to(jnp.sum(sums[...], axis=0, keepdims=True), out.shape)


def update_kernel(sums, guess, resid, field, applied, solution_out, resid_out):
    total = jnp.sum(sums[...], axis=0, keepdims=True)
    first = lanes(1) < CZ // 2
    above = jnp.sum(jnp.where(first, total, 0.0), axis=1, keepdims=True)
    below = jnp.sum(jnp.where(first, 0.0, total), axis=1, keepdims=True)
    step = above / below
    solution_out[...] = guess[...] + step * field[...]
    resid_out[...] = resid[...] - step * applied[...]


def on_device(gx, splits, right_side, guess_field, conduct_field):
    shape = right_side.shape
    b, v, h = (a.reshape(C * C, CZ) for a in (right_side, guess_field, conduct_field))
    n_gx, n_gy = lax.axis_size(gx), lax.axis_size("gy")
    at_x, at_y = lax.axis_index(gx), lax.axis_index("gy")
    flags = jnp.stack([at_x > 0, at_x < n_gx - 1, at_y > 0, at_y < n_gy - 1, at_x % 2 == 1]).astype(F32)

    def exchange(axis, up, down):
        n = lax.axis_size(axis)
        forward = [(i, i + 1) for i in range(n - 1)]
        backward = [(i + 1, i) for i in range(n - 1)]
        return lax.ppermute(up, axis, forward), lax.ppermute(down, axis, backward)

    def exchange_x(first, second):
        pairs = [[(i + k, i + 1 - k) for i in range(start, n_gx - 1, 2) for k in (0, 1)] for start in (1, 0)]
        return lax.ppermute(first, gx, pairs[0]), lax.ppermute(second, gx, pairs[1])

    def swap(value):
        return lax.ppermute(value, "gz", [(0, 1), (1, 0)])

    plane, forward, inverse, denom, eigen = tables()
    own = C * C
    box = EXT * EXT

    def buffer(rows):
        return pltpu.VMEM((rows, CZ), F32)

    up, down = call(
        strips_kernel, (YROWS, YROWS), guess_field, conduct_field, right_side,
        scratch=[pltpu.VMEM((C, C, CZ), F32)] * 3 + [pltpu.SemaphoreType.DMA((3, 2))],
        hbm=(0, 1, 2), limit=56, name="strips", work=2,
    )
    part, edge = call(residual_kernel, (own, 160), v, h, b, name="residual", work=2)
    low, high = exchange("gy", up, down)
    pairs, scale_a, scale_b = call(
        prepare_kernel, (own, box, box), eigen, v, h, denom, smem=(0,), name="prepare", work=2
    )
    (middle,) = call(pack_middle_kernel, (24 * BLOCKS_Z,), part, pairs, name="pack_middle", work=1)
    right, left, faces = call(
        extend_y_kernel, (XROWS, XROWS, 4 * EXT),
        flags, part, pairs, up, down, edge, low, high, middle,
        scratch=[buffer(XROWS)] * 2, smem=(0,), name="extend_y", work=1,
    )
    one, two = exchange_x(right, left)
    inner, part = call(
        inner_kernel, (38 * EXT, C * EXT),
        flags, plane, part, up, down, low, high, smem=(0,), name="inner", work=1,
    )
    (packed,) = call(pack_z_kernel, (ZROWS,), part, pairs, low, high, middle, name="pack_z", work=2)
    own_z, fluxes = call(
        extend_x_kernel, (ZROWS, 2 * EXT), flags, packed, faces, one, two, inner,
        smem=(0,), name="extend_x", work=1,
    )
    far_z = swap(own_z)
    (main,) = call(
        forward_kernel, (box,), flags, plane, part, inner, fluxes, one, two,
        scratch=[buffer(box)], smem=(0,), name="forward", work=2,
    )
    second_a, second_b, sides, side_strip, right, left = call(
        solve_kernel, (box, box, 18 * EXT, 18 * EXT, XROWS2, XROWS2),
        flags, own_z, far_z, main, plane, forward, inverse, scale_a, scale_b,
        scratch=[buffer(box), buffer(XROWS2), buffer(XROWS2)], smem=(0,), name="solve", work=6,
    )
    resid, c_x, c_down, c_up, c_z, c_face = call(
        own_kernel, (own, own + C, own, own, own, own),
        flags, h, low, high, one, two, part, fluxes, own_z, far_z,
        scratch=[buffer(own + 2 * C)], smem=(0,), name="own", work=2,
    )
    one, two = exchange_x(right, left)
    sol, strip = call(
        rest_kernel, (42 * EXT, 42 * EXT),
        plane, inverse, second_a, second_b, sides, side_strip, name="rest", work=2,
    )
    sol, up, down, own_z, across_up, across_down = call(
        fold_x_kernel, (42 * EXT, YROWS2, YROWS2, ZROWS2, 32, 32),
        flags, sol, strip, one, two, resid,
        scratch=[buffer(42 * EXT), buffer(144)], smem=(0,), name="fold_x", work=1,
    )
    low, high = exchange("gy", up, down)
    far_z = swap(own_z)
    diagonal = [((j, k), (j + 1, 1 - k)) for j in range(n_gy - 1) for k in range(2)]
    pairs = [(2 * a + b, 2 * c + d) for (a, b), (c, d) in diagonal]
    far_low = lax.ppermute(across_up, ("gy", "gz"), pairs)
    far_high = lax.ppermute(across_down, ("gy", "gz"), [(b, a) for a, b in pairs])
    (sol,) = call(
        fold_y_kernel, (42 * EXT,), flags, sol, low, high, smem=(0,), name="fold_y", work=1
    )
    first, last = splits
    field, applied, sums = call(
        apply_kernel, (own, own, lax.axis_size(first)),
        sol, low, high, own_z, far_z, far_low, far_high, resid, c_x, c_down, c_up, c_z, c_face, h,
        scratch=[buffer(42 * EXT), buffer(ZROWS2 + 64), buffer(48)], name="apply", work=3,
    )
    sums = lax.all_to_all(sums, first, 0, 0, tiled=True)
    (sums,) = call(gather_kernel, (lax.axis_size(last),), sums, name="gather")
    sums = lax.all_to_all(sums, last, 0, 0, tiled=True)
    out, resid = call(update_kernel, (own, own), sums, v, resid, field, applied, name="update", work=2)
    return out.reshape(shape), resid.reshape(shape)


def solution(mesh):
    n_gx, n_gy, n_gz = mesh.devices.shape
    if n_gx == 64:
        mesh = Mesh(mesh.devices.reshape(4, 8, 2, n_gy, n_gz), ("gx_x", "gx_y", "gx_c", "gy", "gz"))
        gx = ("gx_x", "gx_y", "gx_c")
        splits = (("gx_c", "gy", "gz"), ("gx_x", "gx_y"))
    else:
        gx = "gx"
        splits = (("gx",), ("gy", "gz"))
    placed = P(gx, "gy", "gz")
    return jax.shard_map(
        functools.partial(on_device, gx, splits),
        mesh=mesh,
        in_specs=(placed,) * 3,
        out_specs=(placed,) * 2,
        check_vma=False,
    )
```
